32 devices in a mesh: dp: 2 (over x), batch: 4 (over z), head: 4 (over y, core).
Axes of the slice: x: 2, y: 2, z: 4, core: 2. Of those that a mesh axis runs over, the one named last changes fastest.
Arguments:
- block_in: bfloat16 [32768, 768], P(('dp', 'batch', 'head')), may hold values from -6 to 6
- cotangent: bfloat16 [32768, 768], P(('dp', 'batch', 'head')), may hold values from -6 to 6
- seq_len: int32 [8, 2], P(('dp', 'batch')), may hold values from 1024 to 2048, as said below
- w_qkv: float32 [768, 3, 768], P(('dp', 'batch'), None, 'head'), may hold values from -0.21875 to 0.21875
- w_out: float32 [768, 768], P('head', ('dp', 'batch')), may hold values from -6 to 6
- w_feat: float32 [2, 12, 4096], P(None, 'head', ('dp', 'batch')), may hold values from -1.5 to 1.5
- w_fc: float32 [768, 3072], P(None, ('dp', 'batch', 'head')), may hold values from -0.36084392 to 0.36084392
- w_proj: float32 [3072, 768], P(('dp', 'batch', 'head')), may hold values from -0.109375 to 0.109375
- norm_params: float32 [4, 768], replicated, may hold values from -0.6 to 1.8, as said below
- first_qkv: float32 [768, 3, 768], P(('dp', 'batch'), None, 'head'), may hold values from -0.00024414062 to 0.00024414062
- second_qkv: float32 [768, 3, 768], P(('dp', 'batch'), None, 'head'), may hold values from 7.326656e-09 to 2.9320555e-08
- first_out: float32 [768, 768], P('head', ('dp', 'batch')), may hold values from -0.00024414062 to 0.00024414062
- second_out: float32 [768, 768], P('head', ('dp', 'batch')), may hold values from 1.7689836e-10 to 7.0759343e-10
- first_feat: float32 [2, 12, 4096], P(None, 'head', ('dp', 'batch')), may hold values from -0.00024414062 to 0.00024414062
- second_feat: float32 [2, 12, 4096], P(None, 'head', ('dp', 'batch')), may hold values from 7.326656e-09 to 2.9320555e-08
- first_fc: float32 [768, 3072], P(None, ('dp', 'batch', 'head')), may hold values from -0.00024414062 to 0.00024414062
- second_fc: float32 [768, 3072], P(None, ('dp', 'batch', 'head')), may hold values from 8.176326e-10 to 3.273316e-09
- first_proj: float32 [3072, 768], P(('dp', 'batch', 'head')), may hold values from -0.00024414062 to 0.00024414062
- second_proj: float32 [3072, 768], P(('dp', 'batch', 'head')), may hold values from 7.326656e-09 to 2.9320555e-08
- first_norms: float32 [4, 768], replicated, may hold values from -0.00024414062 to 0.00024414062
- second_norms: float32 [4, 768], replicated, may hold values from 7.326656e-09 to 2.9320555e-08
Outputs:
- grad_norm: float32 [], replicated
- block_out: bfloat16 [32768, 768], P(('dp', 'batch', 'head'))
- block_in_grad: float32 [32768, 768], P(('dp', 'batch', 'head'))
- new_qkv: float32 [768, 3, 768], P(('dp', 'batch'), None, 'head')
- new_out: float32 [768, 768], P('head', ('dp', 'batch'))
- new_feat: float32 [2, 12, 4096], P(None, 'head', ('dp', 'batch'))
- new_fc: float32 [768, 3072], P(None, ('dp', 'batch', 'head'))
- new_proj: float32 [3072, 768], P(('dp', 'batch', 'head'))
- new_norms: float32 [4, 768], replicated
- new_first_qkv: float32 [768, 3, 768], P(('dp', 'batch'), None, 'head')
- new_first_out: float32 [768, 768], P('head', ('dp', 'batch'))
- new_first_feat: float32 [2, 12, 4096], P(None, 'head', ('dp', 'batch'))
- new_first_fc: float32 [768, 3072], P(None, ('dp', 'batch', 'head'))
- new_first_proj: float32 [3072, 768], P(('dp', 'batch', 'head'))
- new_first_norms: float32 [4, 768], replicated
- new_second_qkv: float32 [768, 3, 768], P(('dp', 'batch'), None, 'head')
- new_second_out: float32 [768, 768], P('head', ('dp', 'batch'))
- new_second_feat: float32 [2, 12, 4096], P(None, 'head', ('dp', 'batch'))
- new_second_fc: float32 [768, 3072], P(None, ('dp', 'batch', 'head'))
- new_second_proj: float32 [3072, 768], P(('dp', 'batch', 'head'))
- new_second_norms: float32 [2, 768], replicated
- new_second_late_norm: float32 [2, 768], replicated
- copy_qkv: bfloat16 [768, 3, 768], P(('dp', 'batch'), None, 'head')
- copy_out: bfloat16 [768, 768], P('head', ('dp', 'batch'))
- copy_feat: bfloat16 [2, 12, 4096], P(None, 'head', ('dp', 'batch'))
- copy_fc: bfloat16 [768, 3072], P(None, ('dp', 'batch', 'head'))
- copy_proj: bfloat16 [3072, 768], P(('dp', 'batch', 'head'))
- copy_norms: bfloat16 [4, 768], replicated
The draws below stay inside these ranges and needn't reach their ends.
Inputs may be any that keep to these rules, and one draw needn't show every extreme that they name: `seq_len`: every length is a multiple of 64; a group's two lengths together are at most 4096. `norm_params`: rows 0 and 2 are positive gains, rows 1 and 3 shifts.
All inputs are finite; a program needn't handle non-finite values.
Results may differ from the reference program's by a relative error of at most 0.02.
Values may be sent and summed in bfloat16 or wider, within the bound.
A program may use at most 256 MiB of HBM per device.

```python
import math
import jax
import jax.numpy as jnp
from jax import lax

D = 768
HEADS = 12
HD = 64
FF = 3072
BLOCK = 64
SLOTS = 2
STEP = 8
SEQ_MIN = 1024
GROUP = 4096
GROUPS = 8
TOKENS = 32768
NPARAM = 7179264


def draw_seq_len(key, part):
    key = jax.random.fold_in(key, 11)
    low_blocks = SEQ_MIN // BLOCK
    counts = jax.random.randint(key, (GROUPS, SLOTS), low_blocks, 2 * low_blocks + 1)
    chosen = jax.random.randint(jax.random.fold_in(key, 1), (), 0, GROUPS)
    filled = (jnp.arange(GROUPS)[:, None] == chosen) & (jnp.arange(SLOTS)[None, :] == 0)
    counts = jnp.where(filled, 2 * low_blocks, counts)
    return (counts * BLOCK).astype(jnp.int32)


def draw_norm_params(key, part):
    key = jax.random.fold_in(key, 23)
    column = jnp.arange(D, dtype=jnp.float32) / D
    factors = jax.random.uniform(key, (2, D), jnp.float32, 0.8, 1.2)
    gain_rows = (0.5 + column) * factors
    shifts = jnp.clip(0.2 * jax.random.normal(jax.random.fold_in(key, 1), (2, D), jnp.float32), -0.6, 0.6)
    return jnp.stack([gain_rows[0], shifts[0], gain_rows[1], shifts[1]])


def draw_w_fc(key, part):
    key = jax.random.fold_in(key, 37)
    spread = D ** (-0.5)
    noise = jnp.clip(jax.random.normal(key, (D, FF), jnp.float32), -6.0, 6.0) * spread
    common = jnp.clip(jax.random.normal(jax.random.fold_in(key, 1), (FF,), jnp.float32), -4.0, 4.0) * spread
    return noise + common[None, :]


def block_levels(stream_key, dims, cuts, smallest, high):
    def one(axis_at, blocks):
        draws = jax.random.uniform(jax.random.fold_in(jax.random.fold_in(stream_key, 6), axis_at), (blocks,), jnp.float32, smallest / len(cuts), high / len(cuts))
        return jnp.repeat(jnp.exp(draws), dims[axis_at] // blocks).reshape((-1,) + (1,) * (len(dims) - axis_at - 1))

    level = one(*cuts[0])
    for cut in cuts[1:]:
        level = level * one(*cut)
    return level


def centred(own_key, extent, scale, bound, cuts=(), held_as=jnp.bfloat16):
    level = block_levels(own_key, extent, cuts, -0.22, 0.18) if cuts else 1.0
    drawn = jax.random.normal(own_key, extent, jnp.float32) * scale * level
    return jnp.minimum(jnp.maximum(drawn, -bound), bound).astype(held_as)


def setup_inputs(seed: int = 0) -> dict:
    key_of = jax.random.split(jax.random.key(seed), 22)
    return {
        "block_in": centred(key_of[0], (TOKENS, D), 1.0, 6.0, ((0, 32),)),
        "cotangent": centred(key_of[1], (TOKENS, D), 1.0, 6.0, ((0, 32),)),
        "seq_len": draw_seq_len(jax.random.fold_in(key_of[21], 71), 0),
        "w_qkv": centred(key_of[3], (D, 3, D), D ** -0.5, 0.21875, ((0, 8), (2, 4)), jnp.float32),
        "w_out": centred(key_of[4], (D, D), (max(1, D // SEQ_MIN)) ** -0.5, 6.0, ((0, 4), (1, 8)), jnp.float32),
        "w_feat": centred(key_of[5], (2, HEADS, HD * HD), (max(1, HD // 4)) ** -0.5, 1.5, ((1, 4), (2, 8)), jnp.float32),
        "w_fc": draw_w_fc(jax.random.fold_in(key_of[21], 71), 0),
        "w_proj": centred(key_of[7], (FF, D), FF ** -0.5, 0.109375, ((0, 32),), jnp.float32),
        "norm_params": draw_norm_params(jax.random.fold_in(key_of[21], 71), 0),
        "first_qkv": centred(key_of[9], (D, 3, D), (0.111 * NPARAM ** -0.5), 0.00024414062, ((0, 8), (2, 4)), jnp.float32),
        "second_qkv": jnp.clip(jnp.exp(math.log(2.932055487292473e-08) - 1.38676957 * jax.random.uniform(key_of[10], (D, 3, D), jnp.float32) ** block_levels(key_of[10], (D, 3, D), ((0, 8), (2, 4)), -0.2, 0.2)), 7.326656170647539e-09, 2.932055487292473e-08),
        "first_out": centred(key_of[11], (D, D), (0.111 * NPARAM ** -0.5), 0.00024414062, ((0, 4), (1, 8)), jnp.float32),
        "second_out": jnp.clip(jnp.exp(math.log(7.075934282951835e-10) - 1.3862944 * jax.random.uniform(key_of[12], (D, D), jnp.float32) ** block_levels(key_of[12], (D, D), ((0, 4), (1, 8)), -0.2, 0.2)), 1.7689835707379586e-10, 7.075934282951835e-10),
        "first_feat": centred(key_of[13], (2, HEADS, HD * HD), (0.111 * NPARAM ** -0.5), 0.00024414062, ((1, 4), (2, 8)), jnp.float32),
        "second_feat": jnp.clip(jnp.exp(math.log(2.932055487292473e-08) - 1.38676957 * jax.random.uniform(key_of[14], (2, HEADS, HD * HD), jnp.float32) ** block_levels(key_of[14], (2, HEADS, HD * HD), ((1, 4), (2, 8)), -0.2, 0.2)), 7.326656170647539e-09, 2.932055487292473e-08),
        "first_fc": centred(key_of[15], (D, FF), (0.111 * NPARAM ** -0.5), 0.00024414062, ((1, 32),), jnp.float32),
        "second_fc": jnp.clip(jnp.exp(math.log(3.2733160626463587e-09) - 1.3871458 * jax.random.uniform(key_of[16], (D, FF), jnp.float32) ** block_levels(key_of[16], (D, FF), ((1, 32),), -0.2, 0.2)), 8.176325727582423e-10, 3.2733160626463587e-09),
        "first_proj": centred(key_of[17], (FF, D), (0.111 * NPARAM ** -0.5), 0.00024414062, ((0, 32),), jnp.float32),
        "second_proj": jnp.clip(jnp.exp(math.log(2.932055487292473e-08) - 1.38676957 * jax.random.uniform(key_of[18], (FF, D), jnp.float32) ** block_levels(key_of[18], (FF, D), ((0, 32),), -0.2, 0.2)), 7.326656170647539e-09, 2.932055487292473e-08),
        "first_norms": centred(key_of[19], (4, D), (0.111 * NPARAM ** -0.5), 0.00024414062, (), jnp.float32),
        "second_norms": jnp.clip(jnp.exp(jax.random.uniform(key_of[20], (4, D), jnp.float32, math.log(7.326656170647539e-09), math.log(2.932055487292473e-08))), 7.326656170647539e-09, 2.932055487292473e-08),
    }


@jax.custom_vjp
def low(v):
    return lax.optimization_barrier(v.astype(jnp.bfloat16)).astype(jnp.float32)

@jax.custom_vjp
def low_back(v):
    return v

def low_keep(v):
    return (low(v), None)

def low_pass(kept, grad):
    return (grad,)

def back_keep(v):
    return (v, None)

def back_low(kept, grad):
    return (low(grad),)
low.defvjp(low_keep, low_pass)
low_back.defvjp(back_keep, back_low)
norm_eps = 1e-05
beta_one = 0.9
beta_two = 0.95
adam_eps = 1e-08
clip_limit = 1.0
highest = lax.Precision.HIGHEST

def layer_norm(values, gain_row, shifts):
    center = values - lax.optimization_barrier(jnp.mean(values, axis=-1, keepdims=True))
    spread = lax.optimization_barrier(jnp.mean(center * center, axis=-1, keepdims=True))
    return center * lax.rsqrt(spread + norm_eps) * gain_row + shifts

def gelu_tanh(values):
    return jax.nn.gelu(values, approximate=True)

def features(inputs, feat_map):
    scaled = jnp.einsum('rhd,hde->rhe', inputs, feat_map, precision=highest)
    return jnp.concatenate([jax.nn.softmax(scaled, axis=-1), jax.nn.softmax(-scaled, axis=-1)], axis=-1)

def block_layout(lengths, total_rows):
    blocks = total_rows // BLOCK
    begins = jnp.arange(blocks, dtype=jnp.int32) * BLOCK
    endings = jnp.cumsum(lengths).astype(jnp.int32)
    doc_index = lax.optimization_barrier(jnp.sum((begins[:, None] >= endings[None, :]).astype(jnp.int32), axis=1))
    earlier = (doc_index[:, None] == doc_index[None, :]) & (begins[None, :] < begins[:, None]) & (doc_index[:, None] < SLOTS)
    live_rows = (jnp.arange(total_rows, dtype=jnp.int32) < endings[-1]).astype(jnp.float32)
    return (earlier.astype(jnp.float32), live_rows)

def linear_core(queries, key_rows, values, earlier, live_rows):
    total_rows, heads, feat = queries.shape
    blocks = total_rows // BLOCK
    query_blocks = queries.reshape(blocks, BLOCK, heads, feat)
    key_blocks = key_rows.reshape(blocks, BLOCK, heads, feat)
    value_blocks = values.reshape(blocks, BLOCK, heads, -1)
    causal = jnp.tril(jnp.ones((BLOCK, BLOCK), jnp.float32))
    scores = jnp.einsum('nihf,njhf->nhij', query_blocks, key_blocks, precision=highest) * causal
    numerator = jnp.einsum('nhij,njhd->nihd', scores, value_blocks, precision=highest)
    denominator = jnp.einsum('nhij->nih', scores)
    states = jnp.einsum('njhf,njhd->nhfd', key_blocks, value_blocks, precision=highest)
    totals = lax.optimization_barrier(jnp.sum(key_blocks, axis=1))
    prior_state = jnp.einsum('nm,mhfd->nhfd', earlier, states, precision=highest)
    prior_sum = jnp.einsum('nm,mhf->nhf', earlier, totals, precision=highest)
    numerator = numerator + jnp.einsum('nihf,nhfd->nihd', query_blocks, prior_state, precision=highest)
    denominator = denominator + jnp.einsum('nihf,nhf->nih', query_blocks, prior_sum, precision=highest)
    denominator = denominator + (1.0 - live_rows.reshape(blocks, BLOCK, 1))
    return (numerator / denominator[..., None]).reshape(total_rows, heads, -1)

def group_forward(group_in, lengths, qkv_w, out_w, feat_w, fc_w, proj_w, norm_w):
    earlier, live_rows = block_layout(lengths, group_in.shape[0])
    normed = low(layer_norm(group_in, norm_w[0], norm_w[1]))
    qkv_rows = low(low_back(jnp.dot(normed, qkv_w.reshape(D, 3 * D), precision=highest)))
    qkv_split = qkv_rows.reshape(-1, 3, HEADS, HD)
    feat_map = feat_w.reshape(2, HEADS, HD, HD)
    live_col = live_rows[:, None, None]
    query_feat = low(low_back(features(qkv_split[:, 0], feat_map[0]) * live_col))
    key_feat = low(low_back(features(qkv_split[:, 1], feat_map[1]) * live_col))
    attn_mixed = low(low_back(linear_core(query_feat, key_feat, qkv_split[:, 2], earlier, live_rows)))
    attended = low_back(jnp.dot(attn_mixed.reshape(-1, D), out_w, precision=highest))
    middle = group_in + attended
    hidden = low(layer_norm(middle, norm_w[2], norm_w[3]))
    pre_act = low_back(jnp.dot(hidden, fc_w, precision=highest))
    active = low(gelu_tanh(pre_act))
    return middle + jnp.dot(active, proj_w, precision=highest)

def adamw_update(master, first_mom, second_mom, grad_in, factor, step_rate, decay_rate):
    clipped = grad_in * factor
    first_new = beta_one * first_mom + (1.0 - beta_one) * clipped
    second_new = beta_two * second_mom + (1.0 - beta_two) * clipped * clipped
    direction = first_new / (1.0 - beta_one ** STEP) / (jnp.sqrt(second_new / (1.0 - beta_two ** STEP)) + adam_eps)
    master_new = master - step_rate * (direction + decay_rate * master)
    return (master_new, first_new, second_new)

def reference(block_in, cotangent, seq_len, w_qkv, w_out, w_feat, w_fc, w_proj, norm_params, first_qkv, second_qkv, first_out, second_out, first_feat, second_feat, first_fc, second_fc, first_proj, second_proj, first_norms, second_norms):
    masters = (w_qkv, w_out, w_feat, w_fc, w_proj, norm_params)

    def forward(inputs_f, params):
        copies = [low(member) for member in params]
        step_fn = jax.checkpoint(group_forward)

        def one_group(paired):
            return step_fn(paired[0], paired[1], copies[0], copies[1], copies[2], copies[3], copies[4], copies[5])
        grouped = lax.map(one_group, (inputs_f.reshape(GROUPS, GROUP, D), seq_len))
        return grouped.reshape(TOKENS, D)
    outputs, pullback = jax.vjp(forward, block_in.astype(jnp.float32), masters)
    block_in_grad, gradients = pullback(cotangent.astype(jnp.float32))
    squares = jnp.float32(0.0)
    for member in gradients:
        squares = squares + jnp.sum(member * member)
    grad_norm = jnp.sqrt(squares)
    factor = clip_limit / jnp.maximum(grad_norm, clip_limit)
    firsts = (first_qkv, first_out, first_feat, first_fc, first_proj, first_norms)
    seconds = (second_qkv, second_out, second_feat, second_fc, second_proj, second_norms)
    rates = (0.02, 0.4, 0.15, 0.02, 0.01, 0.3)
    decays = (0.1, 0.1, 0.1, 0.1, 0.1, 0.0)
    updated = [adamw_update(masters[index], firsts[index], seconds[index], gradients[index], factor, rates[index], decays[index]) for index in range(6)]
    return (grad_norm, outputs.astype(jnp.bfloat16), block_in_grad, updated[0][0], updated[1][0], updated[2][0], updated[3][0], updated[4][0], updated[5][0], updated[0][1], updated[1][1], updated[2][1], updated[3][1], updated[4][1], updated[5][1], updated[0][2], updated[1][2], updated[2][2], updated[3][2], updated[4][2], updated[5][2][:2], updated[5][2][2:], updated[0][0].astype(jnp.bfloat16), updated[1][0].astype(jnp.bfloat16), updated[2][0].astype(jnp.bfloat16), updated[3][0].astype(jnp.bfloat16), updated[4][0].astype(jnp.bfloat16), updated[5][0].astype(jnp.bfloat16))
```

```python
import functools

import jax
import jax.numpy as jnp
from jax import lax
from jax.experimental import pallas as pl
from jax.experimental.pallas import tpu as pltpu
from jax.sharding import PartitionSpec as P

HD = 64
STEP = 8
CHUNK = 256
FEAT_ROWS = 32
MESH = pl.DeviceIdType.MESH
VMEM = pltpu.VMEM
F32 = jnp.float32
BF16 = jnp.bfloat16

norm_eps = 1e-05
beta_one = 0.9
beta_two = 0.95
adam_eps = 1e-08
clip_limit = 1.0


def dot(left, right):
    return lax.dot_general(left, right, (((1,), (0,)), ((), ())), preferred_element_type=F32)


def dot_nt(left, right):
    return lax.dot_general(left, right, (((1,), (1,)), ((), ())), preferred_element_type=F32)


def dot_tn(left, right):
    return lax.dot_general(left, right, (((0,), (0,)), ((), ())), preferred_element_type=F32)


def flip_bit(value, bit, on=1):
    low = 2**bit
    return value + on * (low - 2 * low * lax.rem(value // low, 2))


class Network:
    def __init__(self, sizes):
        self.X, self.Z, self.H = sizes
        self.dp, self.b, self.h = (lax.axis_index(name) for name in ("dp", "batch", "head"))
        dp_bits, head_bits = self.X.bit_length() - 1, self.H.bit_length() - 1
        if (self.X, self.H) == (2, 4):
            def first(dp, h):
                odd = lax.rem(h, 2)
                return flip_bit(dp, 0, 1 - odd), flip_bit(h, 1, odd)

            def second(dp, h):
                odd = lax.rem(h, 2)
                return flip_bit(dp, 0, odd), flip_bit(h, 1, 1 - odd)

            self.flips = [first, second, lambda dp, h: (dp, flip_bit(h, 0))]
        else:
            self.flips = [lambda dp, h, k=k: (flip_bit(dp, k), h) for k in range(dp_bits)]
            self.flips += [lambda dp, h, k=k: (dp, flip_bit(h, k)) for k in reversed(range(head_bits))]
        self.sets = [()]
        for k in range(len(self.flips)):
            self.sets += [s + (k,) for s in self.sets]
        self.index = {s: i for i, s in enumerate(self.sets)}

    def coord(self, chosen):
        dp, h = self.dp, self.h
        for k in sorted(chosen, reverse=True):
            dp, h = self.flips[k](dp, h)
        return dp, h

    def behind(self, off):
        return lax.rem(self.b + self.Z - off, self.Z)

    def ahead(self, off):
        return lax.rem(self.b + off, self.Z)

    def slot(self, chosen, off):
        dp, h = self.coord(chosen)
        return dp, self.behind(off), h

    def partner(self, k):
        dp, h = self.flips[k](self.dp, self.h)
        return {"dp": dp, "batch": self.b, "head": h}

    def along(self, b):
        return {"dp": self.dp, "batch": b, "head": self.h}

    def stages(self, chosen):
        return range(max(chosen) + 1 if chosen else 0, len(self.flips))

    def barrier(self, extra=()):
        sem = pltpu.get_barrier_semaphore()
        devices = [self.along(self.ahead(off)) for off in range(1, self.Z)]
        devices += [self.partner(k) for k in range(len(self.flips))]
        for device in devices:
            pl.semaphore_signal(sem, inc=1, device_id=device, device_id_type=MESH)
        pl.semaphore_wait(sem, len(devices))


def gather_sems(sizes):
    X, Z, H = sizes
    n = X * H - 1
    return [pltpu.SemaphoreType.DMA((n + 1, Z)), pltpu.SemaphoreType.DMA((n + 1, Z))]


class Gather:
    def __init__(self, net, shard, buf, send, recv):
        self.net, self.shard, self.buf, self.send, self.recv = net, shard, buf, send, recv

    def copy(self, chosen, off, k=None):
        net = self.net
        place = self.buf.at[net.slot(chosen, off)]
        into = net.index[chosen + (k,)]
        return pltpu.make_async_remote_copy(
            src_ref=place, dst_ref=place, send_sem=self.send.at[into, off], recv_sem=self.recv.at[into, off],
            device_id=net.partner(k), device_id_type=MESH,
        )

    def copy_along(self, off):
        net = self.net
        place = self.buf.at[net.slot((), 0)]
        return pltpu.make_async_remote_copy(
            src_ref=place, dst_ref=place, send_sem=self.send.at[0, off], recv_sem=self.recv.at[0, off],
            device_id=net.along(net.ahead(off)), device_id_type=MESH,
        )

    def arrived(self, chosen, off):
        net = self.net
        place = self.buf.at[net.slot(chosen, off)]
        into = net.index[chosen]
        pltpu.make_async_remote_copy(
            src_ref=place, dst_ref=place, send_sem=self.send.at[into, off], recv_sem=self.recv.at[into, off],
            device_id=net.partner(0), device_id_type=MESH,
        ).wait_recv()

    def begin(self):
        net = self.net
        self.buf[net.slot((), 0)] = self.shard[...]
        for off in range(1, net.Z):
            self.copy_along(off).start()
        for k in net.stages(()):
            self.copy((), 0, k).start()

    def step(self, chosen, off):
        self.arrived(chosen, off)
        for k in self.net.stages(chosen):
            self.copy(chosen, off, k).start()

    def steps(self):
        net = self.net
        order = []
        for off in range(1, net.Z):
            order.append(((), off))
        for chosen in net.sets[1:]:
            order += [(chosen, off) for off in range(net.Z)]
        return [functools.partial(self.step, *item) for item in order]

    def finish(self):
        net = self.net
        for off in range(1, net.Z):
            self.copy_along(off).wait_send()
        for chosen in net.sets:
            for k in net.stages(chosen):
                for off in range(net.Z):
                    self.copy(chosen, off, k).wait_send()


def scatter_scratch(sizes, shape):
    X, Z, H = sizes
    n = X * H
    return [
        VMEM((n // 2, Z) + shape, BF16),
        VMEM((n, Z) + shape, BF16),
        pltpu.SemaphoreType.DMA((n, Z)),
        pltpu.SemaphoreType.DMA((n, Z)),
    ]


class Scatter:
    def __init__(self, net, part, acc, inbox, send, recv):
        self.net, self.part, self.acc, self.inbox, self.send, self.recv = net, part, acc, inbox, send, recv

    def copy(self, chosen, off, k):
        net = self.net
        into = net.index[chosen + (k,)]
        last = k == len(net.flips) - 1
        source = self.part.at[net.slot(chosen + (k,), off)] if last else self.acc.at[into, off]
        return pltpu.make_async_remote_copy(
            src_ref=source, dst_ref=self.inbox.at[into, off], send_sem=self.send.at[into, off],
            recv_sem=self.recv.at[into, off], device_id=net.partner(k), device_id_type=MESH,
        )

    def copy_along(self, off):
        net = self.net
        return pltpu.make_async_remote_copy(
            src_ref=self.acc.at[0, off], dst_ref=self.inbox.at[0, off], send_sem=self.send.at[0, off],
            recv_sem=self.recv.at[0, off], device_id=net.along(net.behind(off)), device_id_type=MESH,
        )

    def begin(self):
        net = self.net
        last = len(net.flips) - 1
        for chosen in reversed(net.sets[: len(net.sets) // 2]):
            for off in range(net.Z):
                self.copy(chosen, off, last).start()

    def add(self, chosen, off, k):
        net = self.net
        into = net.index[chosen + (k,)]
        self.copy(chosen, off, k).wait_recv()
        last = k == len(net.flips) - 1
        mine = self.part[net.slot(chosen, off)] if last else self.acc[net.index[chosen], off]
        self.acc[net.index[chosen], off] = (mine.astype(F32) + self.inbox[into, off].astype(F32)).astype(BF16)

    def step(self, chosen, off):
        net = self.net
        for k in reversed(net.stages(chosen)):
            self.add(chosen, off, k)
        if chosen:
            self.copy(chosen[:-1], off, chosen[-1]).start()
        elif off:
            self.copy_along(off).start()

    def steps(self):
        net = self.net
        order = []
        for chosen in reversed(net.sets[: len(net.sets) // 2]):
            order += [(chosen, off) for off in reversed(range(net.Z))]
        return [functools.partial(self.step, *item) for item in order]

    def result(self):
        net = self.net
        total = self.acc[0, 0].astype(F32)
        for off in range(1, net.Z):
            self.copy_along(off).wait_recv()
            total = total + self.inbox[0, off].astype(F32)
        return total

    def finish(self):
        net = self.net
        for off in range(1, net.Z):
            self.copy_along(off).wait_send()
        for chosen in net.sets:
            for k in net.stages(chosen):
                for off in range(net.Z):
                    self.copy(chosen, off, k).wait_send()


def total_scratch(sizes, shape):
    X, Z, H = sizes
    bits = (X * H).bit_length() - 1
    return [
        VMEM((Z + 2 * bits,) + shape, F32),
        pltpu.SemaphoreType.DMA((Z + bits,)),
        pltpu.SemaphoreType.DMA((Z + bits,)),
    ]


def total_over_all(net, value, slots, send, recv):
    Z = net.Z
    slots[net.b] = value
    copies = []
    for off in range(1, Z):
        copies.append(
            pltpu.make_async_remote_copy(
                src_ref=slots.at[net.b], dst_ref=slots.at[net.b], send_sem=send.at[off], recv_sem=recv.at[off],
                device_id=net.along(net.ahead(off)), device_id_type=MESH,
            )
        )
    for copy in copies:
        copy.start()
    for off in range(1, Z):
        place = slots.at[net.behind(off)]
        pltpu.make_async_remote_copy(
            src_ref=place, dst_ref=place, send_sem=send.at[off], recv_sem=recv.at[off],
            device_id=net.along(net.ahead(off)), device_id_type=MESH,
        ).wait_recv()
    for copy in copies:
        copy.wait_send()
    value = slots[0]
    for off in range(1, Z):
        value = value + slots[off]
    for k in range(len(net.flips)):
        slots[Z + 2 * k] = value
        copy = pltpu.make_async_remote_copy(
            src_ref=slots.at[Z + 2 * k], dst_ref=slots.at[Z + 2 * k + 1], send_sem=send.at[Z + k],
            recv_sem=recv.at[Z + k], device_id=net.partner(k), device_id_type=MESH,
        )
        copy.start()
        copy.wait()
        value = value + slots[Z + 2 * k + 1]
    return value


def gather_kernel(sizes, count, *refs):
    shards, bufs, sems = refs[:count], refs[count : 2 * count], refs[2 * count :]
    net = Network(sizes)
    net.barrier()
    gathers = [Gather(net, shards[i], bufs[i], sems[2 * i], sems[2 * i + 1]) for i in range(count)]
    for gather in gathers:
        gather.begin()
    for gather in gathers:
        for step in gather.steps():
            step()
    for gather in gathers:
        gather.finish()


def scatter_kernel(sizes, count, *refs):
    parts, norm_ref = refs[:count], refs[count]
    outs, norm_out, sq_out = refs[count + 1 : 2 * count + 1], refs[2 * count + 1], refs[2 * count + 2]
    scratch = refs[2 * count + 3 :]
    net = Network(sizes)
    net.barrier()
    scatters = [Scatter(net, parts[i], *scratch[4 * i : 4 * i + 4]) for i in range(count)]
    rest = scratch[4 * count :]
    for scatter in scatters:
        scatter.begin()
    for scatter in scatters:
        for step in scatter.steps():
            step()
    norm_out[...] = total_over_all(net, norm_ref[...], *rest[:3])
    square = jnp.zeros((1, 128), F32)
    for scatter, out in zip(scatters, outs):
        total = scatter.result()
        out[...] = total
        column = jnp.sum(total * total, axis=0, keepdims=True)
        for at in range(0, column.shape[1], 128):
            square = square + column[:, at : at + 128]
    first_row = lax.broadcasted_iota(jnp.int32, (8, 128), 0) == 0
    sq_out[...] = total_over_all(net, jnp.where(first_row, square, 0.0), *rest[3:])
    for scatter in scatters:
        scatter.finish()


def norm_stats(values):
    mean = jnp.mean(values, axis=-1, keepdims=True)
    center = values - mean
    spread = jnp.mean(center * center, axis=-1, keepdims=True)
    return center, lax.rsqrt(spread + norm_eps)


def norm_backward(values, gain_row, grads):
    center, scale = norm_stats(values)
    normal = center * scale
    inner = grads * gain_row
    part = jnp.mean(inner * normal, axis=-1, keepdims=True)
    back = scale * (inner - jnp.mean(inner, axis=-1, keepdims=True) - normal * part)
    return back, jnp.sum(grads * normal, axis=0, keepdims=True), jnp.sum(grads, axis=0, keepdims=True)


def low_half(shape):
    return lax.rem(lax.broadcasted_iota(jnp.int32, shape, len(shape) - 1), 128) < HD


def swap_halves(values):
    cols = values.shape[1]
    parts = [pltpu.roll(values[:, at : at + 128], HD, 1) for at in range(0, cols, 128)]
    return parts[0] if len(parts) == 1 else jnp.concatenate(parts, axis=1)


def feature_pair(scaled, live):
    low = low_half(scaled.shape)
    top = jnp.max(jnp.where(low, scaled, -jnp.inf), axis=-1, keepdims=True)
    bottom = jnp.max(jnp.where(low, -jnp.inf, scaled), axis=-1, keepdims=True)
    powers = jnp.exp(scaled - jnp.where(low, top, bottom))
    first = jnp.sum(jnp.where(low, powers, 0.0), axis=-1, keepdims=True)
    second = jnp.sum(jnp.where(low, 0.0, powers), axis=-1, keepdims=True)
    return powers * (live / jnp.where(low, first, second))


def feature_back(feature, grads):
    low = low_half(feature.shape)
    product = feature * grads
    first = jnp.sum(jnp.where(low, product, 0.0), axis=-1, keepdims=True)
    second = jnp.sum(jnp.where(low, 0.0, product), axis=-1, keepdims=True)
    return product - feature * jnp.where(low, first, second)


class Rows:
    def __init__(self, len_ref, rows, h):
        self.first_len = len_ref[0, 0]
        self.both_len = len_ref[0, 0] + len_ref[0, 1]
        self.start = h * rows
        self.rows = rows

    def second(self, row):
        return row >= self.first_len

    def column(self, chunk):
        return self.start + chunk * CHUNK + lax.broadcasted_iota(jnp.int32, (CHUNK, 1), 0)

    def live(self, chunk):
        return (self.column(chunk) < self.both_len).astype(F32)

    def second_column(self, chunk):
        return self.second(self.column(chunk))

    def masks(self, chunk):
        base = self.start + chunk * CHUNK
        down = base + lax.broadcasted_iota(jnp.int32, (CHUNK, CHUNK), 0)
        across = base + lax.broadcasted_iota(jnp.int32, (CHUNK, CHUNK), 1)
        same = (down >= self.first_len) == (across >= self.first_len)
        return same & (across <= down), same & (across >= down)

    def scalar(self, row):
        return jnp.where(self.second(row), 1.0, 0.0).astype(F32)

    def before(self):
        return self.scalar(self.start - 1)

    def first(self):
        return self.scalar(self.start)

    def last(self):
        return self.scalar(self.start + self.rows - 1)

    def after(self):
        return self.scalar(self.start + self.rows)


def with_ones(block, head, low):
    ones = jnp.ones_like(block)
    return jnp.where(low, block, ones) if head % 2 == 0 else jnp.where(low, ones, block)


def by_sequence(values, second):
    zero = jnp.zeros_like(values)
    return jnp.concatenate([jnp.where(second, zero, values), jnp.where(second, values, zero)], axis=1)


def chain(step, n, h, total_ref, pick, same, place, cin, cout, send, recv):
    begin = h == (0 if step == 1 else n - 1)
    end = h == (n - 1 if step == 1 else 0)
    neighbour = {"head": lax.rem(h + n + step, n)}
    copy = pltpu.make_async_remote_copy(
        src_ref=cout, dst_ref=cin, send_sem=send, recv_sem=recv, device_id=neighbour, device_id_type=MESH
    )

    @pl.when(begin)
    def _():
        cin[...] = jnp.zeros_like(cin)

    @pl.when(jnp.logical_not(begin))
    def _():
        copy.wait_recv()

    @pl.when(jnp.logical_not(end))
    def _():
        for i in range(cout.shape[0]):
            for j in range(cout.shape[1]):
                both = total_ref[i, j]
                mine = both[:, :128] * (1.0 - pick) + both[:, 128:] * pick
                cout[i, j] = (mine + cin[i, j].astype(F32) * same).astype(BF16)
        copy.start()
        copy.wait_send()


def chain_barrier(n, h):
    sem = pltpu.get_barrier_semaphore()
    for step in (1, n - 1):
        pl.semaphore_signal(sem, inc=1, device_id={"head": lax.rem(h + step, n)}, device_id_type=MESH)
    pl.semaphore_wait(sem, 2)


def equal(a, b):
    return a * b + (1.0 - a) * (1.0 - b)


def attention_forward(
    groups, heads, len_ref, x_ref, w_ref, feat_ref, norm_ref,
    normed_ref, qkv_ref, fq_ref, fk_ref, state_ref, mixed_ref, rden_ref, wo_ref, maps_ref, middle_ref, hidden_ref,
    total_ref, cin, cout, send, recv,
):
    h = lax.axis_index("head")
    rows = x_ref.shape[0]
    chunks = rows // CHUNK
    width = x_ref.shape[1]
    seq = Rows(len_ref, rows, h)
    chain_barrier(groups, h)
    low = low_half((CHUNK, 128))

    maps_ref[...] = jnp.zeros_like(maps_ref)
    low64 = low_half((HD, 128))
    for g in range(groups):
        for j in range(heads):
            pair = feat_ref[g * heads + j]
            swapped = pltpu.roll(pair, HD, 1)
            at = slice(HD * j, HD * j + HD), slice(128 * j, 128 * j + 128)
            maps_ref[0, g, at[0], at[1]] = jnp.where(low64, pair, -swapped).astype(BF16)
            maps_ref[1, g, at[0], at[1]] = jnp.where(low64, swapped, -pair).astype(BF16)

    def first_norm(c, _):
        at = pl.ds(pl.multiple_of(c * CHUNK, CHUNK), CHUNK)
        center, scale = norm_stats(x_ref[at].astype(F32))
        normed_ref[at] = (center * scale * norm_ref[0:1] + norm_ref[1:2]).astype(BF16)
        return 0

    lax.fori_loop(0, chunks, first_norm, 0)

    def project(g, _):
        weight = w_ref[:, :, g].reshape(width, width)
        lowd = low_half((width, 128))
        a = swap_halves(weight[:, 128:256].astype(F32))
        b = weight[:, 384:512].astype(F32)
        c_ = swap_halves(weight[:, 640:768].astype(F32))
        wo_ref[g, :, 0:128] = jnp.where(lowd, a, b).astype(BF16)
        wo_ref[g, :, 128:256] = jnp.where(lowd, c_, 0.0).astype(BF16)
        for j in range(heads):
            total_ref[g, j] = jnp.zeros_like(total_ref[g, j])

        def part(c, _):
            at = pl.ds(pl.multiple_of(c * CHUNK, CHUNK), CHUNK)
            live, second = seq.live(c), seq.second_column(c)
            qkv = dot(normed_ref[at], w_ref[:, :, g].reshape(width, width)).astype(BF16)
            qkv_ref[g, at] = qkv
            scaled_q = dot(qkv[:, 0:256], maps_ref[0, g])
            scaled_k = dot(qkv[:, 256:512], maps_ref[1, g])
            for j in range(heads):
                lanes = slice(128 * j, 128 * j + 128)
                fq_ref[g, at, lanes] = feature_pair(scaled_q[:, lanes], live).astype(BF16)
                fk = feature_pair(scaled_k[:, lanes], live).astype(BF16)
                fk_ref[g, at, lanes] = fk
                block = qkv[:, 512 + 128 * (j // 2) : 640 + 128 * (j // 2)]
                values = by_sequence(with_ones(block, j, low), second)
                state_ref[g, j, c] = total_ref[g, j].astype(BF16)
                total_ref[g, j] += dot_tn(fk, values)
            return 0

        lax.fori_loop(0, chunks, part, 0)
        return 0

    lax.fori_loop(0, groups, project, 0)

    before = seq.before()
    chain(1, groups, h, total_ref, seq.last(), equal(before, seq.last()), None, cin, cout, send, recv)

    def mix(g, _):
        def part(c, _):
            at = pl.ds(pl.multiple_of(c * CHUNK, CHUNK), CHUNK)
            live, second = seq.live(c), seq.second_column(c)
            lower, _ = seq.masks(c)
            found = []
            for j in range(heads):
                lanes = slice(128 * j, 128 * j + 128)
                fq, fk = fq_ref[g, at, lanes], fk_ref[g, at, lanes]
                carry = cin[g, j].astype(F32)
                prior = jnp.concatenate([carry * (1.0 - before), carry * before], axis=1)
                state = (state_ref[g, j, c].astype(F32) + prior).astype(BF16)
                state_ref[g, j, c] = state
                scores = jnp.where(lower, dot_nt(fq, fk), 0.0).astype(BF16)
                block = qkv_ref[g, at, 512 + 128 * (j // 2) : 640 + 128 * (j // 2)]
                inter = dot(fq, state)
                found.append(
                    dot(scores, with_ones(block, j, low)) + jnp.where(second, inter[:, 128:], inter[:, :128])
                )
            pair = jnp.where(low, found[0], found[1])
            rden = 1.0 / (swap_halves(jnp.where(low, found[1], found[0])) + (1.0 - live))
            mixed_ref[g, at, 0:128] = (pair * rden).astype(BF16)
            rden_ref[g, at, 0:128] = rden
            rden = jnp.where(low, 1.0 / (swap_halves(found[2]) + (1.0 - live)), 1.0)
            mixed_ref[g, at, 128:256] = jnp.where(low, found[2] * rden, 0.0).astype(BF16)
            rden_ref[g, at, 128:256] = rden
            return 0

        lax.fori_loop(0, chunks, part, 0)
        return 0

    lax.fori_loop(0, groups, mix, 0)

    def close(c, _):
        at = pl.ds(pl.multiple_of(c * CHUNK, CHUNK), CHUNK)
        attended = dot_nt(mixed_ref[0, at], wo_ref[0])
        for g in range(1, groups):
            attended = attended + dot_nt(mixed_ref[g, at], wo_ref[g])
        middle = x_ref[at].astype(F32) + attended
        middle_ref[at] = middle
        center, scale = norm_stats(middle)
        hidden_ref[at] = (center * scale * norm_ref[2:3] + norm_ref[3:4]).astype(BF16)
        return 0

    lax.fori_loop(0, chunks, close, 0)


def feed_forward(
    hidden_ref, dy_ref, fc_ref, proj_ref, middle_ref, norm_ref,
    out_ref, dmid_ref, datt_ref, gfc_ref, gproj_ref, gnorm_ref,
    branch_ref, dhid_ref, act_ref, dpre_ref,
):
    X, Z, H, part, width = fc_ref.shape
    rows = hidden_ref.shape[0]
    tile = 256
    branch_ref[...] = jnp.zeros_like(branch_ref)
    dhid_ref[...] = jnp.zeros_like(dhid_ref)

    def block(i, _):
        dp, b = i // Z, lax.rem(i, Z)

        def rowed(c, _):
            at = pl.ds(pl.multiple_of(c * tile, tile), tile)
            fc = fc_ref[dp, b].reshape(H * part, width)
            proj = proj_ref[dp, b].reshape(H * part, width)
            pre = dot_nt(hidden_ref[at], fc)
            square = pre * pre
            inner = jnp.tanh(0.7978845608 * pre * (1.0 + 0.044715 * square))
            half = 0.5 * (1.0 + inner)
            act = (pre * half).astype(BF16)
            slope = half + 0.5 * pre * (1.0 - inner * inner) * (0.7978845608 * (1.0 + 3 * 0.044715 * square))
            dpre = (dot_nt(dy_ref[at], proj) * slope).astype(BF16)
            act_ref[at] = act
            dpre_ref[at] = dpre
            branch_ref[at] += dot(act, proj)
            dhid_ref[at] += dot(dpre, fc)
            return 0

        lax.fori_loop(0, rows // tile, rowed, 0)
        gproj_ref[dp, b] = dot_tn(act_ref[...], dy_ref[...]).astype(BF16).reshape(H, part, width)
        gfc_ref[dp, b] = dot_tn(dpre_ref[...], hidden_ref[...]).astype(BF16).reshape(H, part, width)
        return 0

    lax.fori_loop(0, X * Z, block, 0)

    gnorm_ref[...] = jnp.zeros_like(gnorm_ref)

    def close(c, _):
        at = pl.ds(pl.multiple_of(c * tile, tile), tile)
        middle = middle_ref[at]
        out_ref[at] = (middle + branch_ref[at]).astype(BF16)
        back, gain, shift = norm_backward(middle, norm_ref[2:3], dhid_ref[at])
        dmid = dy_ref[at].astype(F32) + back
        dmid_ref[at] = dmid
        datt_ref[at] = dmid.astype(BF16)
        gnorm_ref[2:3] += gain
        gnorm_ref[3:4] += shift
        return 0

    lax.fori_loop(0, rows // tile, close, 0)


def attention_backward(
    groups, heads, len_ref, x_ref, normed_ref, qkv_ref, fq_ref, fk_ref, state_ref, mixed_ref, rden_ref, wo_ref,
    maps_ref, w_ref, datt_ref, dmid_ref, norm_ref, gnorm_in,
    dx_ref, gw_ref, gmap_ref, gnorm_ref,
    dne_ref, back_ref, total_ref, dqkv_ref, dnormed_ref, gsum_ref, cin, cout, send, recv,
):
    h = lax.axis_index("head")
    rows, width = x_ref.shape
    chunks = rows // CHUNK
    X, Z, H, part, _ = w_ref.shape
    seq = Rows(len_ref, rows, h)
    chain_barrier(groups, h)
    low = low_half((CHUNK, 128))
    down = lax.broadcasted_iota(jnp.int32, (256, 256), 0) // HD
    across = lax.broadcasted_iota(jnp.int32, (256, 256), 1) // HD
    other_half = ((down // 2 == across // 2) & (down != across)).astype(BF16)

    def ahead(g, _):
        for j in range(heads):
            total_ref[g, j] = jnp.zeros_like(total_ref[g, j])

        def piece(i, _):
            c = chunks - 1 - i
            at = pl.ds(pl.multiple_of(c * CHUNK, CHUNK), CHUNK)
            second = seq.second_column(c)
            dm = dot(datt_ref[at], wo_ref[g]).astype(BF16).astype(F32)
            rden = rden_ref[g, at]
            sums = dot((dm * mixed_ref[g, at].astype(F32)).astype(BF16), other_half)
            dnum = dm * rden
            dden = sums * swap_halves(rden) * (-1.0 / HD)
            for j in range(heads):
                lanes = slice(128 * (j // 2), 128 * (j // 2) + 128)
                first, other = dnum[:, lanes], dden[:, lanes]
                dne = (jnp.where(low, first, other) if j % 2 == 0 else jnp.where(low, other, first)).astype(BF16)
                dne_ref[g, j, at] = dne
                back_ref[g, j, c] = total_ref[g, j].astype(BF16)
                total_ref[g, j] += dot_tn(fq_ref[g, at, 128 * j : 128 * j + 128], by_sequence(dne, second))
            return 0

        lax.fori_loop(0, chunks, piece, 0)
        return 0

    lax.fori_loop(0, groups, ahead, 0)
    after = seq.after()
    chain(-1, groups, h, total_ref, seq.first(), equal(after, seq.first()), None, cin, cout, send, recv)

    dnormed_ref[...] = jnp.zeros_like(dnormed_ref)

    def group(g, _):
        gsum_ref[...] = jnp.zeros_like(gsum_ref)

        def piece(c, _):
            at = pl.ds(pl.multiple_of(c * CHUNK, CHUNK), CHUNK)
            second = seq.second_column(c)
            lower, upper = seq.masks(c)
            dus_q, dus_k, dvs = [], [], []
            for j in range(heads):
                lanes = slice(128 * j, 128 * j + 128)
                fq, fk, dne = fq_ref[g, at, lanes], fk_ref[g, at, lanes], dne_ref[g, j, at]
                carry = cin[g, j].astype(F32)
                later = jnp.concatenate([carry * (1.0 - after), carry * after], axis=1)
                back = (back_ref[g, j, c].astype(F32) + later).astype(BF16)
                state = state_ref[g, j, c]
                block = qkv_ref[g, at, 512 + 128 * (j // 2) : 640 + 128 * (j // 2)]
                values = with_ones(block, j, low)
                scores_t = jnp.where(upper, dot_nt(fk, fq), 0.0).astype(BF16)
                weigh = jnp.where(lower, dot_nt(dne, values), 0.0).astype(BF16)
                weigh_t = jnp.where(upper, dot_nt(values, dne), 0.0).astype(BF16)
                dfq = dot(weigh, fk) + dot_nt(by_sequence(dne, second), state)
                dfk = dot(weigh_t, fq) + dot_nt(by_sequence(values, second), back)
                inter = dot(fk, back)
                dvs.append(dot(scores_t, dne) + jnp.where(second, inter[:, 128:], inter[:, :128]))
                dus_q.append(feature_back(fq.astype(F32), dfq.astype(BF16).astype(F32)).astype(BF16))
                dus_k.append(feature_back(fk.astype(F32), dfk.astype(BF16).astype(F32)).astype(BF16))
            du_q, du_k = jnp.concatenate(dus_q, axis=1), jnp.concatenate(dus_k, axis=1)
            dq = dot_nt(du_q, maps_ref[0, g]).astype(BF16)
            dk = dot_nt(du_k, maps_ref[1, g]).astype(BF16)
            dv = jnp.concatenate([jnp.where(low, dvs[0], dvs[1]), jnp.where(low, dvs[2], 0.0)], axis=1).astype(BF16)
            gsum_ref[0] += dot_tn(qkv_ref[g, at, 0:256], du_q)
            gsum_ref[1] += dot_tn(qkv_ref[g, at, 256:512], du_k)
            dqkv = jnp.concatenate([dq, dk, dv], axis=1)
            dqkv_ref[at] = dqkv
            dnormed_ref[at] += dot_nt(dqkv, w_ref[:, :, g].reshape(width, width))
            return 0

        lax.fori_loop(0, chunks, piece, 0)
        for side in range(2):
            for j in range(heads):
                gmap_ref[side, g, j] = gsum_ref[side, HD * j : HD * j + HD, 128 * j : 128 * j + 128]
        lowd = low_half((width, 128))
        shape = (X, Z, part, 128)
        for third in range(3):
            grad = dot_tn(normed_ref[...], dqkv_ref[:, 256 * third : 256 * third + 256])
            beside = dot_tn(datt_ref[...], mixed_ref[g, :, 128 * (third // 2) : 128 * (third // 2) + 128])
            if third != 1:
                beside = swap_halves(beside)
            at = 256 * third
            gw_ref[:, :, g, :, at : at + 128] = grad[:, 0:128].astype(BF16).reshape(shape)
            gw_ref[:, :, g, :, at + 128 : at + 256] = (
                jnp.where(lowd, grad[:, 128:256], beside).astype(BF16).reshape(shape)
            )
        return 0

    lax.fori_loop(0, groups, group, 0)

    gnorm_ref[...] = gnorm_in[...]

    def close(c, _):
        at = pl.ds(pl.multiple_of(c * CHUNK, CHUNK), CHUNK)
        back, gain, shift = norm_backward(x_ref[at].astype(F32), norm_ref[0:1], dnormed_ref[at])
        dx_ref[at] = dmid_ref[at] + back
        gnorm_ref[0:1] += gain
        gnorm_ref[1:2] += shift
        return 0

    lax.fori_loop(0, chunks, close, 0)


def adamw_update(master, first_mom, second_mom, grad_in, factor, step_rate, decay_rate):
    clipped = grad_in * factor
    first_new = beta_one * first_mom + (1.0 - beta_one) * clipped
    second_new = beta_two * second_mom + (1.0 - beta_two) * clipped * clipped
    direction = (
        first_new
        / (1.0 - beta_one**STEP)
        / (jnp.sqrt(second_new / (1.0 - beta_two**STEP)) + adam_eps)
    )
    master_new = master - step_rate * (direction + decay_rate * master)
    return (master_new, first_new, second_new)


def in_vmem(count):
    return [pl.BlockSpec(memory_space=VMEM)] * count


def struct(shape, dtype):
    return jax.ShapeDtypeStruct(shape, dtype)


def call(kernel, outs, smem, operands, scratch, collective_id, name, flops, limit=63):
    specs = [pl.BlockSpec(memory_space=pltpu.SMEM)] * smem + in_vmem(len(operands) - smem)
    traffic = sum(o.size * o.dtype.itemsize for o in outs) + sum(o.size * o.dtype.itemsize for o in operands)
    extra = {} if collective_id is None else {"collective_id": collective_id, "has_side_effects": True}
    return pl.pallas_call(
        kernel,
        out_shape=tuple(outs),
        in_specs=specs,
        out_specs=tuple(in_vmem(len(outs))),
        scratch_shapes=scratch,
        compiler_params=pltpu.CompilerParams(vmem_limit_bytes=limit * 2**20, **extra),
        cost_estimate=pl.CostEstimate(flops=flops, bytes_accessed=traffic, transcendentals=0),
        name=name,
    )(*operands)


def on_device(
    sizes,
    block_in,
    cotangent,
    seq_len,
    w_qkv,
    w_out,
    w_feat,
    w_fc,
    w_proj,
    norm_params,
    first_qkv,
    second_qkv,
    first_out,
    second_out,
    first_feat,
    second_feat,
    first_fc,
    second_fc,
    first_proj,
    second_proj,
    first_norms,
    second_norms,
):
    X, Z, H = sizes
    rows, width = block_in.shape
    part, _, head_width = w_qkv.shape
    heads = w_feat.shape[1]
    depth = w_feat.shape[2] // HD
    chunks = rows // CHUNK

    norm_low = norm_params.astype(BF16).astype(F32)
    out_t = w_out.T
    pieces = []
    for j in range(3):
        pieces += [w_qkv[:, j, :], out_t[:, HD * j : HD * j + HD]]
    attn_shard = jnp.concatenate(pieces, axis=1).astype(BF16)
    fc_shard = w_fc.T.astype(BF16)
    proj_shard = w_proj.astype(BF16)
    feat_rows = w_feat.reshape(2, heads, depth, HD).transpose(1, 2, 0, 3).reshape(heads * depth, 2 * HD)
    feat_shard = jnp.pad(feat_rows.astype(BF16), ((0, FEAT_ROWS - heads * depth), (0, 0)))

    big = (X, Z, H, part, width)
    small = (X, Z, H, FEAT_ROWS, 2 * HD)
    attn_w, feat_all, fc_w, proj_w = call(
        functools.partial(gather_kernel, sizes, 4),
        [struct(big, BF16), struct(small, BF16), struct(big, BF16), struct(big, BF16)],
        0,
        [attn_shard, feat_shard, fc_shard, proj_shard],
        [sem for _ in range(4) for sem in gather_sems(sizes)],
        0,
        "gather",
        0,
    )
    feat_maps = (
        feat_all.reshape(X * Z, H, FEAT_ROWS, 2 * HD)[:, :, : heads * depth]
        .reshape(X * Z, H, heads, depth, 2 * HD)
        .transpose(1, 2, 0, 3, 4)
        .reshape(H * heads, HD, 2 * HD)
        .astype(F32)
    )

    chain_scratch = [
        VMEM((H, heads, 128, 128), BF16),
        VMEM((H, heads, 128, 128), BF16),
        pltpu.SemaphoreType.DMA,
        pltpu.SemaphoreType.DMA,
    ]
    normed, qkv, fq, fk, states, mixed, rden, wo, maps, middle, hidden = call(
        functools.partial(attention_forward, H, heads),
        [
            struct((rows, width), BF16),
            struct((H, rows, width), BF16),
            struct((H, rows, 128 * heads), BF16),
            struct((H, rows, 128 * heads), BF16),
            struct((H, heads, chunks, 128, 256), BF16),
            struct((H, rows, 256), BF16),
            struct((H, rows, 256), F32),
            struct((H, width, 256), BF16),
            struct((2, H, 256, 128 * heads), BF16),
            struct((rows, width), F32),
            struct((rows, width), BF16),
        ],
        1,
        [seq_len, block_in, attn_w, feat_maps, norm_low],
        [VMEM((H, heads, 128, 256), F32)] + chain_scratch,
        1,
        "attention_forward",
        10**10,
    )

    block_out, d_middle, d_att, g_fc_all, g_proj_all, g_norm = call(
        feed_forward,
        [
            struct((rows, width), BF16),
            struct((rows, width), F32),
            struct((rows, width), BF16),
            struct(big, BF16),
            struct(big, BF16),
            struct((8, width), F32),
        ],
        0,
        [hidden, cotangent, fc_w, proj_w, middle, norm_low],
        [
            VMEM((rows, width), F32),
            VMEM((rows, width), F32),
            VMEM((rows, H * part), BF16),
            VMEM((rows, H * part), BF16),
        ],
        None,
        "feed_forward",
        3 * 10**10,
    )

    block_in_grad, g_attn_all, g_maps, g_norm = call(
        functools.partial(attention_backward, H, heads),
        [
            struct((rows, width), F32),
            struct(big, BF16),
            struct((2, H, heads, HD, 128), F32),
            struct((8, width), F32),
        ],
        1,
        [
            seq_len, block_in, normed, qkv, fq, fk, states, mixed, rden, wo, maps, attn_w, d_att, d_middle, norm_low,
            g_norm,
        ],
        [
            VMEM((H, heads, rows, 128), BF16),
            VMEM((H, heads, chunks, 128, 256), BF16),
            VMEM((H, heads, 128, 256), F32),
            VMEM((rows, width), BF16),
            VMEM((rows, width), F32),
            VMEM((2, 256, 128 * heads), F32),
        ]
        + chain_scratch,
        2,
        "attention_backward",
        2 * 10**10,
    )

    blocks = g_maps[..., :HD] - g_maps[..., HD:]
    g_feat_all = (
        jnp.concatenate([blocks[0], blocks[1]], axis=-1)
        .reshape(H, heads, X * Z, depth, 2 * HD)
        .transpose(2, 0, 1, 3, 4)
        .reshape(X, Z, H, heads * depth, 2 * HD)
    )
    g_feat_all = jnp.pad(
        g_feat_all, ((0, 0), (0, 0), (0, 0), (0, FEAT_ROWS - heads * depth), (0, 0))
    ).astype(BF16)

    shapes = [(part, width)] * 3 + [(FEAT_ROWS, 2 * HD)]
    g_fc, g_proj, g_attn, g_feat, norm_sum, square_sum = call(
        functools.partial(scatter_kernel, sizes, 4),
        [struct(shape, F32) for shape in shapes] + [struct((8, width), F32), struct((8, 128), F32)],
        0,
        [g_fc_all, g_proj_all, g_attn_all, g_feat_all, g_norm],
        [item for shape in shapes for item in scatter_scratch(sizes, shape)]
        + total_scratch(sizes, (8, width))
        + total_scratch(sizes, (8, 128)),
        3,
        "scatter",
        0,
    )

    norm_grads = norm_sum[:4]
    grad_norm = jnp.sqrt(jnp.sum(square_sum) + jnp.sum(norm_grads * norm_grads))
    factor = clip_limit / jnp.maximum(grad_norm, clip_limit)
    reduced_qkv = jnp.stack([g_attn[:, 256 * j : 256 * j + head_width] for j in range(3)], axis=1)
    reduced_out = jnp.concatenate(
        [g_attn[:, 256 * j + head_width : 256 * j + 256] for j in range(3)], axis=1
    ).T
    reduced_feat = (
        g_feat[: heads * depth].reshape(heads, depth, 2, HD).transpose(2, 0, 1, 3).reshape(2, heads, depth * HD)
    )
    up_qkv = adamw_update(w_qkv, first_qkv, second_qkv, reduced_qkv, factor, 0.02, 0.1)
    up_out = adamw_update(w_out, first_out, second_out, reduced_out, factor, 0.4, 0.1)
    up_feat = adamw_update(w_feat, first_feat, second_feat, reduced_feat, factor, 0.15, 0.1)
    up_fc = adamw_update(w_fc, first_fc, second_fc, g_fc.T, factor, 0.02, 0.1)
    up_proj = adamw_update(w_proj, first_proj, second_proj, g_proj, factor, 0.01, 0.1)
    up_norms = adamw_update(norm_params, first_norms, second_norms, norm_grads, factor, 0.3, 0.0)
    return (
        grad_norm,
        block_out,
        block_in_grad,
        up_qkv[0],
        up_out[0],
        up_feat[0],
        up_fc[0],
        up_proj[0],
        up_norms[0],
        up_qkv[1],
        up_out[1],
        up_feat[1],
        up_fc[1],
        up_proj[1],
        up_norms[1],
        up_qkv[2],
        up_out[2],
        up_feat[2],
        up_fc[2],
        up_proj[2],
        up_norms[2][:2],
        up_norms[2][2:],
        up_qkv[0].astype(BF16),
        up_out[0].astype(BF16),
        up_feat[0].astype(BF16),
        up_fc[0].astype(BF16),
        up_proj[0].astype(BF16),
        up_norms[0].astype(BF16),
    )


def solution(mesh):
    everything = ("dp", "batch", "head")
    rows = P(everything, None)
    qkv, out, feat = P(("dp", "batch"), None, "head"), P("head", ("dp", "batch")), P(None, "head", ("dp", "batch"))
    fc, proj, whole = P(None, everything), P(everything, None), P()
    weights = (qkv, out, feat, fc, proj, whole)
    in_specs = (rows, rows, P(("dp", "batch"), None)) + weights
    for spec in weights:
        in_specs += (spec, spec)
    out_specs = (whole, rows, rows) + weights + weights + weights[:5] + (whole, whole) + weights
    sizes = (mesh.shape["dp"], mesh.shape["batch"], mesh.shape["head"])
    return jax.shard_map(
        functools.partial(on_device, sizes), mesh=mesh, in_specs=in_specs, out_specs=out_specs, check_vma=False
    )
```

```python
import functools

import jax
import jax.numpy as jnp
from jax import lax
from jax.experimental import pallas as pl
from jax.experimental.pallas import tpu as pltpu
from jax.sharding import PartitionSpec as P

HD = 64
STEP = 8
CHUNK = 256
FEAT_ROWS = 32
MESH = pl.DeviceIdType.MESH
VMEM = pltpu.VMEM
F32 = jnp.float32
BF16 = jnp.bfloat16

norm_eps = 1e-05
beta_one = 0.9
beta_two = 0.95
adam_eps = 1e-08
clip_limit = 1.0


def dot(left, right):
    return lax.dot_general(left, right, (((1,), (0,)), ((), ())), preferred_element_type=F32)


def dot_nt(left, right):
    return lax.dot_general(left, right, (((1,), (1,)), ((), ())), preferred_element_type=F32)


def dot_tn(left, right):
    return lax.dot_general(left, right, (((0,), (0,)), ((), ())), preferred_element_type=F32)


def flip_bit(value, bit, on=1):
    low = 2**bit
    return value + on * (low - 2 * low * lax.rem(value // low, 2))


class Network:
    def __init__(self, sizes):
        self.X, self.Z, self.H = sizes
        self.dp, self.b, self.h = (lax.axis_index(name) for name in ("dp", "batch", "head"))
        dp_bits, head_bits = self.X.bit_length() - 1, self.H.bit_length() - 1
        if (self.X, self.H) == (2, 4):
            def first(dp, h):
                odd = lax.rem(h, 2)
                return flip_bit(dp, 0, 1 - odd), flip_bit(h, 1, odd)

            def second(dp, h):
                odd = lax.rem(h, 2)
                return flip_bit(dp, 0, odd), flip_bit(h, 1, 1 - odd)

            self.flips = [first, second, lambda dp, h: (dp, flip_bit(h, 0))]
        else:
            self.flips = [lambda dp, h, k=k: (flip_bit(dp, k), h) for k in range(dp_bits)]
            self.flips += [lambda dp, h, k=k: (dp, flip_bit(h, k)) for k in reversed(range(head_bits))]
        self.sets = [()]
        for k in range(len(self.flips)):
            self.sets += [s + (k,) for s in self.sets]
        self.index = {s: i for i, s in enumerate(self.sets)}

    def coord(self, chosen):
        dp, h = self.dp, self.h
        for k in sorted(chosen, reverse=True):
            dp, h = self.flips[k](dp, h)
        return dp, h

    def behind(self, off):
        return lax.rem(self.b + self.Z - off, self.Z)

    def ahead(self, off):
        return lax.rem(self.b + off, self.Z)

    def slot(self, chosen, off):
        dp, h = self.coord(chosen)
        return dp, self.behind(off), h

    def partner(self, k):
        dp, h = self.flips[k](self.dp, self.h)
        return {"dp": dp, "batch": self.b, "head": h}

    def along(self, b):
        return {"dp": self.dp, "batch": b, "head": self.h}

    def stages(self, chosen):
        return range(max(chosen) + 1 if chosen else 0, len(self.flips))

    def barrier(self, chained=False):
        sem = pltpu.get_barrier_semaphore()
        devices = [self.along(self.ahead(off)) for off in range(1, self.Z)]
        devices += [self.partner(k) for k in range(len(self.flips))]
        if chained:
            devices += [{"head": lax.rem(self.h + step, self.H)} for step in (1, self.H - 1)]
        for device in devices:
            pl.semaphore_signal(sem, inc=1, device_id=device, device_id_type=MESH)
        pl.semaphore_wait(sem, len(devices))


def gather_sems(sizes):
    X, Z, H = sizes
    n = X * H - 1
    return [pltpu.SemaphoreType.DMA((n + 1, Z)), pltpu.SemaphoreType.DMA((n + 1, Z))]


class Gather:
    def __init__(self, net, shard, buf, send, recv):
        self.net, self.shard, self.buf, self.send, self.recv = net, shard, buf, send, recv

    def source(self, chosen, off):
        return self.shard if chosen == () and off == 0 else self.buf.at[self.net.slot(chosen, off)]

    def copy(self, chosen, off, k):
        net = self.net
        into = net.index[chosen + (k,)]
        return pltpu.make_async_remote_copy(
            src_ref=self.source(chosen, off), dst_ref=self.buf.at[net.slot(chosen, off)],
            send_sem=self.send.at[into, off], recv_sem=self.recv.at[into, off],
            device_id=net.partner(k), device_id_type=MESH,
        )

    def copy_along(self, off):
        net = self.net
        return pltpu.make_async_remote_copy(
            src_ref=self.shard, dst_ref=self.buf.at[net.slot((), 0)],
            send_sem=self.send.at[0, off], recv_sem=self.recv.at[0, off],
            device_id=net.along(net.ahead(off)), device_id_type=MESH,
        )

    def copy_own(self):
        return pltpu.make_async_copy(self.shard, self.buf.at[self.net.slot((), 0)], self.send.at[0, 0])

    def arrived(self, chosen, off):
        net = self.net
        place = self.buf.at[net.slot(chosen, off)]
        into = net.index[chosen]
        pltpu.make_async_remote_copy(
            src_ref=place, dst_ref=place, send_sem=self.send.at[into, off], recv_sem=self.recv.at[into, off],
            device_id=net.partner(0), device_id_type=MESH,
        ).wait_recv()

    def begin(self):
        net = self.net
        for k in net.stages(()):
            self.copy((), 0, k).start()
        for off in range(1, net.Z):
            self.copy_along(off).start()
        self.copy_own().start()

    def step(self, chosen, off):
        self.arrived(chosen, off)
        for k in self.net.stages(chosen):
            self.copy(chosen, off, k).start()

    def steps(self):
        net = self.net
        order = [((), off) for off in range(1, net.Z)]
        for chosen in net.sets[1:]:
            order += [(chosen, off) for off in range(net.Z)]
        half = len(net.sets) // 2 * net.Z - 1
        return [functools.partial(self.step, *item) for item in order[:half]], [
            functools.partial(self.step, *item) for item in order[half:]
        ]

    def finish(self):
        net = self.net
        for off in range(1, net.Z):
            self.copy_along(off).wait_send()
        for chosen in net.sets:
            for k in net.stages(chosen):
                for off in range(net.Z):
                    self.copy(chosen, off, k).wait_send()


def scatter_scratch(sizes, shape):
    X, Z, H = sizes
    n = X * H
    return [VMEM((n, Z) + shape, BF16), pltpu.SemaphoreType.DMA((n, Z)), pltpu.SemaphoreType.DMA((n, Z))]


class Scatter:
    def __init__(self, net, part, inbox, send, recv):
        self.net, self.part, self.inbox, self.send, self.recv = net, part, inbox, send, recv
        self.last = len(net.flips) - 1

    def sum_at(self, chosen, off):
        return self.inbox.at[self.net.index[chosen + (self.last,)], off]

    def copy(self, chosen, off, k):
        net = self.net
        into = net.index[chosen + (k,)]
        first = k == self.last
        source = self.part.at[net.slot(chosen + (k,), off)] if first else self.sum_at(chosen + (k,), off)
        return pltpu.make_async_remote_copy(
            src_ref=source, dst_ref=self.inbox.at[into, off], send_sem=self.send.at[into, off],
            recv_sem=self.recv.at[into, off], device_id=net.partner(k), device_id_type=MESH,
        )

    def copy_along(self, off):
        net = self.net
        return pltpu.make_async_remote_copy(
            src_ref=self.sum_at((), off), dst_ref=self.inbox.at[0, off], send_sem=self.send.at[0, off],
            recv_sem=self.recv.at[0, off], device_id=net.along(net.behind(off)), device_id_type=MESH,
        )

    def early_sets(self):
        return self.net.sets[: len(self.net.sets) // 2]

    def begin(self, ready=None, offs=None):
        for chosen in reversed(self.early_sets()):

            def start(chosen=chosen):
                for off in range(self.net.Z) if offs is None else offs:
                    self.copy(chosen, off, self.last).start()

            if ready is None:
                start()
            else:
                pl.when(ready(*self.net.coord(chosen + (self.last,))))(start)

    def step(self, chosen, off):
        net = self.net
        total = self.part[net.slot(chosen, off)].astype(F32)
        for k in reversed(net.stages(chosen)):
            self.copy(chosen, off, k).wait_recv()
            total = total + self.inbox[net.index[chosen + (k,)], off].astype(F32)
        self.sum_at(chosen, off)[...] = total.astype(BF16)
        if chosen:
            self.copy(chosen[:-1], off, chosen[-1]).start()
        elif off:
            self.copy_along(off).start()

    def result(self):
        net = self.net
        total = self.sum_at((), 0)[...].astype(F32)
        for off in range(1, net.Z):
            self.copy_along(off).wait_recv()
            total = total + self.inbox[0, off].astype(F32)
        return total

    def finish(self):
        net = self.net
        for off in range(1, net.Z):
            self.copy_along(off).wait_send()
        for chosen in net.sets:
            for k in net.stages(chosen):
                for off in range(net.Z):
                    self.copy(chosen, off, k).wait_send()


def total_scratch(sizes, shape):
    X, Z, H = sizes
    bits = (X * H).bit_length() - 1
    return [
        VMEM((Z + 2 * bits,) + shape, F32),
        pltpu.SemaphoreType.DMA((Z + bits,)),
        pltpu.SemaphoreType.DMA((Z + bits,)),
    ]


def total_over_all(net, value, slots, send, recv):
    Z = net.Z
    slots[net.b] = value
    copies = []
    for off in range(1, Z):
        copies.append(
            pltpu.make_async_remote_copy(
                src_ref=slots.at[net.b], dst_ref=slots.at[net.b], send_sem=send.at[off], recv_sem=recv.at[off],
                device_id=net.along(net.ahead(off)), device_id_type=MESH,
            )
        )
    for copy in copies:
        copy.start()
    for off in range(1, Z):
        place = slots.at[net.behind(off)]
        pltpu.make_async_remote_copy(
            src_ref=place, dst_ref=place, send_sem=send.at[off], recv_sem=recv.at[off],
            device_id=net.along(net.ahead(off)), device_id_type=MESH,
        ).wait_recv()
    for copy in copies:
        copy.wait_send()
    value = slots[0]
    for off in range(1, Z):
        value = value + slots[off]
    for k in range(len(net.flips)):
        slots[Z + 2 * k] = value
        copy = pltpu.make_async_remote_copy(
            src_ref=slots.at[Z + 2 * k], dst_ref=slots.at[Z + 2 * k + 1], send_sem=send.at[Z + k],
            recv_sem=recv.at[Z + k], device_id=net.partner(k), device_id_type=MESH,
        )
        copy.start()
        copy.wait()
        value = value + slots[Z + 2 * k + 1]
    return value


class Mover:
    def __init__(self, sems):
        self.sems, self.used = sems, 0

    def plan(self, source, target, count=None):
        at = self.used
        self.used += 1 if count is None else count

        def make(i):
            if count is None:
                return pltpu.make_async_copy(source, target, self.sems.at[at])
            return pltpu.make_async_copy(source.at[i], target.at[i], self.sems.at[at + i])

        return make


def norm_stats(values):
    mean = jnp.mean(values, axis=-1, keepdims=True)
    center = values - mean
    spread = jnp.mean(center * center, axis=-1, keepdims=True)
    return center, lax.rsqrt(spread + norm_eps)


def norm_backward(values, gain_row, grads):
    center, scale = norm_stats(values)
    normal = center * scale
    inner = grads * gain_row
    part = jnp.mean(inner * normal, axis=-1, keepdims=True)
    back = scale * (inner - jnp.mean(inner, axis=-1, keepdims=True) - normal * part)
    return back, jnp.sum(grads * normal, axis=0, keepdims=True), jnp.sum(grads, axis=0, keepdims=True)


def low_half(shape):
    return lax.rem(lax.broadcasted_iota(jnp.int32, shape, len(shape) - 1), 128) < HD


def swap_halves(values):
    cols = values.shape[1]
    parts = [pltpu.roll(values[:, at : at + 128], HD, 1) for at in range(0, cols, 128)]
    return parts[0] if len(parts) == 1 else jnp.concatenate(parts, axis=1)


def feature_pair(scaled, live):
    low = low_half(scaled.shape)
    top = jnp.max(jnp.where(low, scaled, -jnp.inf), axis=-1, keepdims=True)
    bottom = jnp.max(jnp.where(low, -jnp.inf, scaled), axis=-1, keepdims=True)
    powers = jnp.exp(scaled - jnp.where(low, top, bottom))
    first = jnp.sum(jnp.where(low, powers, 0.0), axis=-1, keepdims=True)
    second = jnp.sum(jnp.where(low, 0.0, powers), axis=-1, keepdims=True)
    return powers * (live / jnp.where(low, first, second))


def feature_back(feature, grads):
    low = low_half(feature.shape)
    product = feature * grads
    first = jnp.sum(jnp.where(low, product, 0.0), axis=-1, keepdims=True)
    second = jnp.sum(jnp.where(low, 0.0, product), axis=-1, keepdims=True)
    return product - feature * jnp.where(low, first, second)


class Rows:
    def __init__(self, len_ref, rows, h):
        self.first_len = len_ref[0, 0]
        self.both_len = len_ref[0, 0] + len_ref[0, 1]
        self.start = h * rows
        self.rows = rows

    def second(self, row):
        return row >= self.first_len

    def column(self, chunk):
        return self.start + chunk * CHUNK + lax.broadcasted_iota(jnp.int32, (CHUNK, 1), 0)

    def live(self, chunk):
        return (self.column(chunk) < self.both_len).astype(F32)

    def second_column(self, chunk):
        return self.second(self.column(chunk))

    def masks(self, chunk):
        base = self.start + chunk * CHUNK
        down = base + lax.broadcasted_iota(jnp.int32, (CHUNK, CHUNK), 0)
        across = base + lax.broadcasted_iota(jnp.int32, (CHUNK, CHUNK), 1)
        same = (down >= self.first_len) == (across >= self.first_len)
        return same & (across <= down), same & (across >= down)

    def scalar(self, row):
        return jnp.where(self.second(row), 1.0, 0.0).astype(F32)

    def before(self):
        return self.scalar(self.start - 1)

    def first(self):
        return self.scalar(self.start)

    def last(self):
        return self.scalar(self.start + self.rows - 1)

    def after(self):
        return self.scalar(self.start + self.rows)


def with_ones(block, head, low):
    ones = jnp.ones_like(block)
    return jnp.where(low, block, ones) if head % 2 == 0 else jnp.where(low, ones, block)


def by_sequence(values, second):
    zero = jnp.zeros_like(values)
    return jnp.concatenate([jnp.where(second, zero, values), jnp.where(second, values, zero)], axis=1)


class Chain:
    def __init__(self, step, n, h, same, picked, cin, cout, send, recv):
        self.first = h == (0 if step == 1 else n - 1)
        self.final = h == (n - 1 if step == 1 else 0)
        self.neighbour = {"head": lax.rem(h + n + step, n)}
        self.same, self.picked, self.cin, self.cout, self.send, self.recv = same, picked, cin, cout, send, recv

    def copy(self, g):
        return pltpu.make_async_remote_copy(
            src_ref=self.cout.at[g], dst_ref=self.cin.at[g], send_sem=self.send.at[g], recv_sem=self.recv.at[g],
            device_id=self.neighbour, device_id_type=MESH,
        )

    def step(self, g):
        @pl.when(self.first)
        def _():
            self.cin[g] = jnp.zeros_like(self.cin[g])

        @pl.when(jnp.logical_not(self.first))
        def _():
            self.copy(g).wait_recv()

        @pl.when(jnp.logical_not(self.final))
        def _():
            self.cout[g] = (self.picked[g] + self.cin[g].astype(F32) * self.same).astype(BF16)
            self.copy(g).start()

    def finish(self, n):
        @pl.when(jnp.logical_not(self.final))
        def _():
            for g in range(n):
                self.copy(g).wait_send()


def group_at(h, i, n):
    bits = n.bit_length() - 1
    for k in range(bits):
        h = flip_bit(h, bits - 1 - k, lax.rem(i // 2**k, 2))
    return h


def run_at(slots, i, count):
    for k in range(count):
        if slots.get(k):

            @pl.when(i == k)
            def _(items=slots[k]):
                for item in items:
                    item()


def rest_of(slots, count):
    for k in sorted(slots):
        if k >= count:
            for item in slots[k]:
                item()


def equal(a, b):
    return a * b + (1.0 - a) * (1.0 - b)


def attention_forward(
    sizes, heads, depth, len_ref, x_ref, wqkv_ref, wout_ref, wfeat_ref, wfc_ref, wproj_ref, norm_in,
    normed_out, qkv_out, fq_out, fk_out, state_out, mixed_out, rden_out, wo_out, maps_out, middle_out, hidden_out,
    attn_out, fc_out, proj_out,
    normed_ref, qkv_ref, fq_ref, fk_ref, state_ref, mixed_ref, rden_ref, wo_ref, maps_ref, middle_ref, hidden_ref,
    attn_shard, feat_shard, fc_shard, proj_shard, feat_rows, norm_ref,
    w_ref, feat_ref, pairs_ref, total_ref, picked_ref, cin, cout, chain_send, chain_recv, move_sem,
    *sems,
):
    X, Z, groups = sizes
    lanes_here = heads * HD
    for j in range(3):
        attn_shard[:, 256 * j : 256 * j + 128] = wqkv_ref[j, :, 0:128].astype(BF16)
        attn_shard[:, 256 * j + 128 : 256 * j + 256] = jnp.concatenate(
            [wqkv_ref[j, :, 128:lanes_here], wout_ref[HD * j : HD * j + HD].T], axis=1
        ).astype(BF16)
    feat_rows[...] = jnp.zeros_like(feat_rows)
    low_row = low_half((1, 128))
    for j in range(heads):
        for d in range(depth):
            q, k = (wfeat_ref[j, side : side + 1, 128 * (d // 2) : 128 * (d // 2) + 128] for side in range(2))
            row = jnp.where(low_row, q, pltpu.roll(k, HD, 1)) if d % 2 == 0 else jnp.where(low_row, pltpu.roll(q, HD, 1), k)
            feat_rows[depth * j + d : depth * j + d + 1] = row
    feat_shard[...] = feat_rows[...].astype(BF16)
    fc_shard[...] = wfc_ref[...].astype(BF16)
    proj_shard[...] = wproj_ref[...].astype(BF16)
    norm_ref[...] = norm_in[...].astype(BF16).astype(F32)
    net = Network(sizes)
    h = net.h
    rows, width = x_ref.shape
    chunks = rows // CHUNK
    seq = Rows(len_ref, rows, h)
    low = low_half((CHUNK, 128))
    mover = Mover(move_sem)
    push_normed, push_wo, push_maps, push_attn = (
        mover.plan(*pair)
        for pair in ((normed_ref, normed_out), (wo_ref, wo_out), (maps_ref, maps_out), (w_ref, attn_out))
    )
    push_qkv, push_fq, push_fk, push_state, push_mixed, push_rden = (
        mover.plan(*pair, groups)
        for pair in (
            (qkv_ref, qkv_out), (fq_ref, fq_out), (fk_ref, fk_out), (state_ref, state_out), (mixed_ref, mixed_out),
            (rden_ref, rden_out),
        )
    )
    push_middle, push_hidden = mover.plan(middle_ref, middle_out), mover.plan(hidden_ref, hidden_out)

    net.barrier(chained=True)
    shards = (attn_shard, feat_shard, fc_shard, proj_shard)
    attn, feat, fc, proj = (
        Gather(net, shard, buf, sems[2 * i], sems[2 * i + 1])
        for i, (shard, buf) in enumerate(zip(shards, (w_ref, feat_ref, fc_out, proj_out)))
    )
    feat.begin()
    attn.begin()

    def first_norm(c, _):
        at = pl.ds(pl.multiple_of(c * CHUNK, CHUNK), CHUNK)
        center, scale = norm_stats(x_ref[at].astype(F32))
        normed_ref[at] = (center * scale * norm_ref[0:1] + norm_ref[1:2]).astype(BF16)
        return 0

    feat.copy_own().wait()
    attn.copy_own().wait()
    feat_on, feat_in = feat.steps()
    attn_on, attn_in = attn.steps()
    for step in feat_on[: Z - 1] + attn_on[: Z - 1]:
        step()
    lax.fori_loop(0, chunks, first_norm, 0)
    push_normed(0).start()
    late = Z if (X, groups) == (2, 4) else 0
    now = len(attn_on) - late
    for step in attn_on[Z - 1 : now] + feat_on[Z - 1 :] + feat_in:
        step()

    maps_ref[...] = jnp.zeros_like(maps_ref)
    low64 = low_half((HD, 128))
    for i in range(X * Z):
        for g in range(groups):
            block = feat_ref[i // Z, i % Z, g].astype(F32)
            for j in range(heads):
                pairs_ref[g * heads + j, depth * i : depth * i + depth] = block[depth * j : depth * j + depth]
    for g in range(groups):
        for j in range(heads):
            pair = pairs_ref[g * heads + j]
            swapped = pltpu.roll(pair, HD, 1)
            at = slice(HD * j, HD * j + HD), slice(128 * j, 128 * j + 128)
            maps_ref[0, g, at[0], at[1]] = jnp.where(low64, pair, -swapped).astype(BF16)
            maps_ref[1, g, at[0], at[1]] = jnp.where(low64, swapped, -pair).astype(BF16)
    push_maps(0).start()

    turns = groups * chunks
    slots = {}
    if late:
        for k, step in enumerate(attn_on[now:]):
            slots.setdefault(k, []).append(step)
        slots.setdefault(2 * chunks, []).extend(attn_in)
    else:
        slots[0] = list(attn_in)
    slots.setdefault(1, []).extend([fc.begin, proj.begin])
    fc_on, fc_in = fc.steps()
    proj_on, proj_in = proj.steps()
    for k, pair in enumerate(zip(fc_on, proj_on)):
        slots.setdefault(4 + k * (2 * turns - 6) // len(fc_on), []).extend(pair)
    mix_slots = {k - turns: items for k, items in slots.items() if k >= turns}
    last = seq.last()

    def project(i, _):
        g = group_at(h, i, groups)
        for j in range(heads):
            total_ref[j] = jnp.zeros_like(total_ref[j])

        def part(c, _):
            run_at(slots, i * chunks + c, turns)
            at = pl.ds(pl.multiple_of(c * CHUNK, CHUNK), CHUNK)
            live, second = seq.live(c), seq.second_column(c)
            qkv = dot(normed_ref[at], w_ref[:, :, g].reshape(width, width)).astype(BF16)
            qkv_ref[g, at] = qkv
            scaled_q = dot(qkv[:, 0:256], maps_ref[0, g])
            scaled_k = dot(qkv[:, 256:512], maps_ref[1, g])
            for j in range(heads):
                lanes = slice(128 * j, 128 * j + 128)
                fq_ref[g, at, lanes] = feature_pair(scaled_q[:, lanes], live).astype(BF16)
                fk = feature_pair(scaled_k[:, lanes], live).astype(BF16)
                fk_ref[g, at, lanes] = fk
                block = qkv[:, 512 + 128 * (j // 2) : 640 + 128 * (j // 2)]
                values = by_sequence(with_ones(block, j, low), second)
                state_ref[g, j, c] = total_ref[j].astype(BF16)
                total_ref[j] += dot_tn(fk, values)
            return 0

        lax.fori_loop(0, chunks, part, 0)
        for push in (push_qkv, push_fq, push_fk):
            push(g).start()
        for j in range(heads):
            picked_ref[g, j] = total_ref[j, :, :128] * (1.0 - last) + total_ref[j, :, 128:] * last
        weight = w_ref[:, :, g].reshape(width, width)
        lowd = low_half((width, 128))
        a = swap_halves(weight[:, 128:256].astype(F32))
        b = weight[:, 384:512].astype(F32)
        c_ = swap_halves(weight[:, 640:768].astype(F32))
        wo_ref[g, :, 0:128] = jnp.where(lowd, a, b).astype(BF16)
        wo_ref[g, :, 128:256] = jnp.where(lowd, c_, 0.0).astype(BF16)
        return 0

    lax.fori_loop(0, groups, project, 0)
    push_wo(0).start()
    push_attn(0).start()

    before = seq.before()
    chain = Chain(1, groups, h, equal(before, last), picked_ref, cin, cout, chain_send, chain_recv)

    def mix(g, _):
        chain.step(g)

        def part(c, _):
            run_at(mix_slots, g * chunks + c, turns)
            at = pl.ds(pl.multiple_of(c * CHUNK, CHUNK), CHUNK)
            live, second = seq.live(c), seq.second_column(c)
            lower, _ = seq.masks(c)
            found = []
            for j in range(heads):
                lanes = slice(128 * j, 128 * j + 128)
                fq, fk = fq_ref[g, at, lanes], fk_ref[g, at, lanes]
                carry = cin[g, j].astype(F32)
                prior = jnp.concatenate([carry * (1.0 - before), carry * before], axis=1)
                state = (state_ref[g, j, c].astype(F32) + prior).astype(BF16)
                state_ref[g, j, c] = state
                scores = jnp.where(lower, dot_nt(fq, fk), 0.0).astype(BF16)
                block = qkv_ref[g, at, 512 + 128 * (j // 2) : 640 + 128 * (j // 2)]
                inter = dot(fq, state)
                found.append(
                    dot(scores, with_ones(block, j, low)) + jnp.where(second, inter[:, 128:], inter[:, :128])
                )
            pair = jnp.where(low, found[0], found[1])
            rden = 1.0 / (swap_halves(jnp.where(low, found[1], found[0])) + (1.0 - live))
            mixed_ref[g, at, 0:128] = (pair * rden).astype(BF16)
            rden_ref[g, at, 0:128] = rden.astype(BF16)
            rden = jnp.where(low, 1.0 / (swap_halves(found[2]) + (1.0 - live)), 1.0)
            mixed_ref[g, at, 128:256] = jnp.where(low, found[2] * rden, 0.0).astype(BF16)
            rden_ref[g, at, 128:256] = rden.astype(BF16)
            return 0

        lax.fori_loop(0, chunks, part, 0)
        for push in (push_state, push_mixed, push_rden):
            push(g).start()
        return 0

    lax.fori_loop(0, groups, mix, 0)
    rest_of(mix_slots, turns)

    def close(c, _):
        at = pl.ds(pl.multiple_of(c * CHUNK, CHUNK), CHUNK)
        attended = dot_nt(mixed_ref[0, at], wo_ref[0])
        for g in range(1, groups):
            attended = attended + dot_nt(mixed_ref[g, at], wo_ref[g])
        middle = x_ref[at].astype(F32) + attended
        middle_ref[at] = middle
        center, scale = norm_stats(middle)
        hidden_ref[at] = (center * scale * norm_ref[2:3] + norm_ref[3:4]).astype(BF16)
        return 0

    lax.fori_loop(0, chunks, close, 0)
    push_middle(0).start()
    push_hidden(0).start()
    for step in fc_in + proj_in:
        step()
    fc.copy_own().wait()
    proj.copy_own().wait()
    chain.finish(groups)
    for gather in (attn, feat, fc, proj):
        gather.finish()
    for push in (push_normed, push_wo, push_maps, push_attn, push_middle, push_hidden):
        push(0).wait()
    for push in (push_qkv, push_fq, push_fk, push_state, push_mixed, push_rden):
        for g in range(groups):
            push(g).wait()


def feed_forward(
    sizes, hidden_ref, dy_ref, norm_ref, fc_in, proj_in, middle_in,
    block_out, dmid_out, datt_out, gfc_out, gproj_out, gnorm_ref,
    fc_ref, proj_ref, middle_ref, out_ref, datt_ref, gfc_ref, gproj_ref, branch_ref, dhid_ref, act_ref, dpre_ref,
    move_sem, fc_sem, proj_sem, *scratch,
):
    X, Z, H = sizes
    net = Network(sizes)
    part, width = fc_ref.shape[3:]
    rows = hidden_ref.shape[0]
    tile = 256
    tiles = rows // tile
    turns = X * Z

    def place(i):
        off = Z - 1 - lax.rem(i, Z)
        return lax.rem(net.dp + 1 + i // Z, X), net.behind(off), off

    def fetch(i):
        dp, b, _ = place(i)
        at = dp * Z + b
        return (
            pltpu.make_async_copy(fc_in.at[dp, b], fc_ref.at[dp, b], fc_sem.at[at]),
            pltpu.make_async_copy(proj_in.at[dp, b], proj_ref.at[dp, b], proj_sem.at[at]),
        )

    for i in range(turns):
        for copy in fetch(i):
            copy.start()
    mover = Mover(move_sem)
    pull_middle = mover.plan(middle_in, middle_ref)
    pull_middle(0).start()
    net.barrier()
    scatters = [Scatter(net, gfc_ref, *scratch[:3]), Scatter(net, gproj_ref, *scratch[3:])]
    branch_ref[...] = jnp.zeros_like(branch_ref)
    dhid_ref[...] = jnp.zeros_like(dhid_ref)

    slots = {}
    if (X, H) == (2, 4):
        own, first, second, both = scatters[0].early_sets()
        for k in range(Z):
            off = Z - 1 - k
            for scatter in scatters:
                slots.setdefault(k + 1, []).append(functools.partial(scatter.step, both, off))
                for late, chosen in ((1, second), (1, first), (2, own)):
                    slots.setdefault(Z + k + late, []).append(functools.partial(scatter.step, chosen, off))
    else:
        for scatter in scatters:
            for chosen in reversed(scatter.early_sets()):
                for off in reversed(range(Z)):
                    slots.setdefault(turns, []).append(functools.partial(scatter.step, chosen, off))

    def block(i, _):
        dp, b, off = place(i)
        for copy in fetch(i):
            copy.wait()

        def rowed(c, _):
            at = pl.ds(pl.multiple_of(c * tile, tile), tile)
            fc = fc_ref[dp, b].reshape(H * part, width)
            proj = proj_ref[dp, b].reshape(H * part, width)
            pre = dot_nt(hidden_ref[at], fc)
            square = pre * pre
            inner = jnp.tanh(0.7978845608 * pre * (1.0 + 0.044715 * square))
            half = 0.5 * (1.0 + inner)
            act = (pre * half).astype(BF16)
            slope = half + 0.5 * pre * (1.0 - inner * inner) * (0.7978845608 * (1.0 + 3 * 0.044715 * square))
            dpre = (dot_nt(dy_ref[at], proj) * slope).astype(BF16)
            act_ref[at] = act
            dpre_ref[at] = dpre
            branch_ref[at] += dot(act, proj)
            dhid_ref[at] += dot(dpre, fc)
            return 0

        lax.fori_loop(0, tiles, rowed, 0)
        run_at(slots, i, turns)
        gproj_ref[dp, b] = dot_tn(act_ref[...], dy_ref[...]).astype(BF16).reshape(H, part, width)
        gfc_ref[dp, b] = dot_tn(dpre_ref[...], hidden_ref[...]).astype(BF16).reshape(H, part, width)
        for scatter in scatters:
            scatter.begin(lambda dp_at, h_at: dp_at == dp, [off])
        return 0

    lax.fori_loop(0, turns, block, 0)

    gnorm_ref[...] = jnp.zeros_like(gnorm_ref)
    pull_middle(0).wait()
    late = [slots[k] for k in sorted(slots) if k >= turns]
    late_slots = dict(enumerate(late[: tiles - 1]))
    late_slots[tiles - 1] = [item for items in late[tiles - 1 :] for item in items]

    def close(c, _):
        run_at(late_slots, c, tiles)
        at = pl.ds(pl.multiple_of(c * tile, tile), tile)
        middle = middle_ref[at]
        out_ref[at] = (middle + branch_ref[at]).astype(BF16)
        back, gain, shift = norm_backward(middle, norm_ref[2:3].astype(BF16).astype(F32), dhid_ref[at])
        dmid = dy_ref[at].astype(F32) + back
        middle_ref[at] = dmid
        datt_ref[at] = dmid.astype(BF16)
        gnorm_ref[2:3] += gain
        gnorm_ref[3:4] += shift
        return 0

    lax.fori_loop(0, tiles, close, 0)
    pushes = [mover.plan(*pair) for pair in ((out_ref, block_out), (middle_ref, dmid_out), (datt_ref, datt_out))]
    for push in pushes:
        push(0).start()
    gfc_out[...] = scatters[0].result()
    gproj_out[...] = scatters[1].result()
    for push in pushes:
        push(0).wait()
    for scatter in scatters:
        scatter.finish()


def attention_backward(
    sizes, heads, depth, len_ref, norm_ref, gnorm_in, gfc_ref, gproj_ref, x_in, normed_in, qkv_in, fq_in, fk_in,
    state_in, mixed_in, rden_in, wo_in, maps_in, w_in, datt_in, dmid_in,
    dx_out, gattn_out, gfeat_out, sums_out,
    x_ref, normed_ref, qkv_ref, fq_ref, fk_ref, state_ref, mixed_ref, rden_ref, wo_ref, maps_ref, datt_ref, dmid_ref,
    w_ref, gw_ref, gnorm_ref, featsum_ref, featpart_ref,
    dne_ref, back_ref, total_ref, picked_ref, dqkv_ref, dnormed_ref, gsum_ref, cin, cout, chain_send, chain_recv,
    w_sem, move_sem, *scratch,
):
    X, Z, H = sizes
    groups = H
    net = Network(sizes)
    h = net.h
    rows, width = x_ref.shape
    chunks = rows // CHUNK
    part = w_ref.shape[3]
    seq = Rows(len_ref, rows, h)
    low = low_half((CHUNK, 128))

    mover = Mover(move_sem)
    pull_datt, pull_maps, pull_normed, pull_x, pull_dmid, push_dx = (
        mover.plan(*pair)
        for pair in (
            (datt_in, datt_ref), (maps_in, maps_ref), (normed_in, normed_ref), (x_in, x_ref), (dmid_in, dmid_ref),
            (dmid_ref, dx_out),
        )
    )
    ahead_pulls = [
        mover.plan(*pair, groups)
        for pair in ((wo_in, wo_ref), (rden_in, rden_ref), (mixed_in, mixed_ref), (fq_in, fq_ref))
    ]
    group_pulls = [
        mover.plan(*pair, groups) for pair in ((fk_in, fk_ref), (state_in, state_ref), (qkv_in, qkv_ref))
    ]

    def pull_weight(i):
        slot = lax.rem(i, 2)
        return pltpu.make_async_copy(w_in.at[:, :, backwards(i)], w_ref.at[slot], w_sem.at[slot])

    def backwards(i):
        return group_at(h, groups - 1 - i, groups)

    pull_datt(0).start()
    for g in range(groups):
        for pull in ahead_pulls:
            pull(g).start()
    pull_maps(0).start()
    for i in range(groups):
        for pull in group_pulls:
            pull(backwards(i)).start()
    pull_weight(0).start()
    pull_normed(0).start()
    pull_x(0).start()
    pull_dmid(0).start()
    net.barrier(chained=True)
    attn = Scatter(net, gw_ref, *scratch[:3])
    feat = Scatter(net, featpart_ref, *scratch[3:6])

    down = lax.broadcasted_iota(jnp.int32, (256, 256), 0) // HD
    across = lax.broadcasted_iota(jnp.int32, (256, 256), 1) // HD
    other_half = ((down // 2 == across // 2) & (down != across)).astype(BF16)
    first = seq.first()
    pull_datt(0).wait()

    def ahead(g, _):
        for j in range(heads):
            total_ref[j] = jnp.zeros_like(total_ref[j])
        for pull in ahead_pulls:
            pull(g).wait()

        def piece(i, _):
            c = chunks - 1 - i
            at = pl.ds(pl.multiple_of(c * CHUNK, CHUNK), CHUNK)
            second = seq.second_column(c)
            dm = dot(datt_ref[at], wo_ref[g]).astype(BF16).astype(F32)
            rden = rden_ref[g, at].astype(F32)
            sums = dot((dm * mixed_ref[g, at].astype(F32)).astype(BF16), other_half)
            dnum = dm * rden
            dden = sums * swap_halves(rden) * (-1.0 / HD)
            for j in range(heads):
                lanes = slice(128 * (j // 2), 128 * (j // 2) + 128)
                mine, other = dnum[:, lanes], dden[:, lanes]
                dne = (jnp.where(low, mine, other) if j % 2 == 0 else jnp.where(low, other, mine)).astype(BF16)
                dne_ref[g, j, at] = dne
                back_ref[g, j, c] = total_ref[j].astype(BF16)
                total_ref[j] += dot_tn(fq_ref[g, at, 128 * j : 128 * j + 128], by_sequence(dne, second))
            return 0

        lax.fori_loop(0, chunks, piece, 0)
        for j in range(heads):
            picked_ref[g, j] = total_ref[j, :, :128] * (1.0 - first) + total_ref[j, :, 128:] * first
        return 0

    lax.fori_loop(0, groups, ahead, 0)
    after = seq.after()
    chain = Chain(-1, groups, h, equal(after, first), picked_ref, cin, cout, chain_send, chain_recv)
    lowd = low_half((width, 128))
    shape = (X, Z, part, 128)

    def out_grads(g, _):
        chain.step(g)
        for third in range(3):
            beside = dot_tn(datt_ref[...], mixed_ref[g, :, 128 * (third // 2) : 128 * (third // 2) + 128])
            if third != 1:
                beside = swap_halves(beside)
            gw_ref[:, :, g, :, 256 * third + 128 : 256 * third + 256] = beside.astype(BF16).reshape(shape)
        return 0

    lax.fori_loop(0, groups, out_grads, 0)

    dnormed_ref[...] = jnp.zeros_like(dnormed_ref)
    pull_maps(0).wait()
    pull_normed(0).wait()

    def group(i, _):
        g = backwards(i)
        slot = lax.rem(i, 2)
        for pull in group_pulls:
            pull(g).wait()
        pull_weight(i).wait()

        @pl.when(i < groups - 1)
        def _():
            pull_weight(i + 1).start()

        gsum_ref[...] = jnp.zeros_like(gsum_ref)

        def piece(c, _):
            at = pl.ds(pl.multiple_of(c * CHUNK, CHUNK), CHUNK)
            second = seq.second_column(c)
            lower, upper = seq.masks(c)
            dus_q, dus_k, dvs = [], [], []
            for j in range(heads):
                lanes = slice(128 * j, 128 * j + 128)
                fq, fk, dne = fq_ref[g, at, lanes], fk_ref[g, at, lanes], dne_ref[g, j, at]
                carry = cin[g, j].astype(F32)
                later = jnp.concatenate([carry * (1.0 - after), carry * after], axis=1)
                back = (back_ref[g, j, c].astype(F32) + later).astype(BF16)
                state = state_ref[g, j, c]
                block = qkv_ref[g, at, 512 + 128 * (j // 2) : 640 + 128 * (j // 2)]
                values = with_ones(block, j, low)
                scores_t = jnp.where(upper, dot_nt(fk, fq), 0.0).astype(BF16)
                weigh = jnp.where(lower, dot_nt(dne, values), 0.0).astype(BF16)
                weigh_t = jnp.where(upper, dot_nt(values, dne), 0.0).astype(BF16)
                dfq = dot(weigh, fk) + dot_nt(by_sequence(dne, second), state)
                dfk = dot(weigh_t, fq) + dot_nt(by_sequence(values, second), back)
                inter = dot(fk, back)
                dvs.append(dot(scores_t, dne) + jnp.where(second, inter[:, 128:], inter[:, :128]))
                dus_q.append(feature_back(fq.astype(F32), dfq.astype(BF16).astype(F32)).astype(BF16))
                dus_k.append(feature_back(fk.astype(F32), dfk.astype(BF16).astype(F32)).astype(BF16))
            du_q, du_k = jnp.concatenate(dus_q, axis=1), jnp.concatenate(dus_k, axis=1)
            dq = dot_nt(du_q, maps_ref[0, g]).astype(BF16)
            dk = dot_nt(du_k, maps_ref[1, g]).astype(BF16)
            dv = jnp.concatenate([jnp.where(low, dvs[0], dvs[1]), jnp.where(low, dvs[2], 0.0)], axis=1).astype(BF16)
            gsum_ref[0] += dot_tn(qkv_ref[g, at, 0:256], du_q)
            gsum_ref[1] += dot_tn(qkv_ref[g, at, 256:512], du_k)
            dqkv = jnp.concatenate([dq, dk, dv], axis=1)
            dqkv_ref[at] = dqkv
            dnormed_ref[at] += dot_nt(dqkv, w_ref[slot].reshape(width, width))
            return 0

        lax.fori_loop(0, chunks, piece, 0)
        low64 = low_half((HD, 128))
        for j in range(heads):
            sums = [gsum_ref[side, HD * j : HD * j + HD, 128 * j : 128 * j + 128] for side in range(2)]
            sums = [value - pltpu.roll(value, HD, 1) for value in sums]
            pair = jnp.where(low64, sums[0], -sums[1])
            for k in range(X * Z):
                featsum_ref[k // Z, k % Z, g, depth * j : depth * j + depth] = pair[depth * k : depth * k + depth]
        for third in range(3):
            grad = dot_tn(normed_ref[...], dqkv_ref[:, 256 * third : 256 * third + 256])
            at = 256 * third
            gw_ref[:, :, g, :, at : at + 128] = grad[:, 0:128].astype(BF16).reshape(shape)
            beside = gw_ref[:, :, g, :, at + 128 : at + 256].reshape(width, 128)
            gw_ref[:, :, g, :, at + 128 : at + 256] = (
                jnp.where(lowd, grad[:, 128:256], beside.astype(F32)).astype(BF16).reshape(shape)
            )
        attn.begin(lambda dp_at, h_at: h_at == g)

        if (X, H) == (2, 4):

            @pl.when(i == groups - 1)
            def _():
                for off in reversed(range(Z)):
                    attn.step(attn.early_sets()[3], off)

        return 0

    featsum_ref[...] = jnp.zeros_like(featsum_ref)
    lax.fori_loop(0, groups, group, 0)
    for k in range(X * Z):
        for g in range(groups):
            featpart_ref[k // Z, k % Z, g] = featsum_ref[k // Z, k % Z, g].astype(BF16)
    feat.begin()

    gnorm_ref[...] = gnorm_in[...]
    pull_x(0).wait()
    pull_dmid(0).wait()
    slots = {}
    for scatter in (attn, feat):
        early = list(reversed(scatter.early_sets()))
        if scatter is attn and (X, H) == (2, 4):
            early = early[1:]
        for k, chosen in enumerate(early):
            for off in reversed(range(Z)):
                slots.setdefault(min(k, chunks - 1), []).append(functools.partial(scatter.step, chosen, off))

    def close(c, _):
        run_at(slots, c, chunks)
        at = pl.ds(pl.multiple_of(c * CHUNK, CHUNK), CHUNK)
        gain_row = norm_ref[0:1].astype(BF16).astype(F32)
        back, gain, shift = norm_backward(x_ref[at].astype(F32), gain_row, dnormed_ref[at])
        dmid_ref[at] = dmid_ref[at] + back
        gnorm_ref[0:1] += gain
        gnorm_ref[1:2] += shift
        return 0

    lax.fori_loop(0, chunks, close, 0)
    push_dx(0).start()
    square = jnp.zeros((1, 128), F32)
    gattn_out[...] = attn.result()
    gfeat_out[...] = feat.result()
    for ref in (gattn_out, gfeat_out, gfc_ref, gproj_ref):
        column = jnp.sum(ref[...] * ref[...], axis=0, keepdims=True)
        for at in range(0, column.shape[1], 128):
            square = square + column[:, at : at + 128]
    gnorm_ref[4:5, 0:128] = square
    sums_out[...] = total_over_all(net, gnorm_ref[...], *scratch[6:])
    push_dx(0).wait()
    chain.finish(groups)
    for scatter in (attn, feat):
        scatter.finish()


def adamw_update(master, first_mom, second_mom, grad_in, factor, step_rate, decay_rate):
    clipped = grad_in * factor
    first_new = beta_one * first_mom + (1.0 - beta_one) * clipped
    second_new = beta_two * second_mom + (1.0 - beta_two) * clipped * clipped
    direction = (
        first_new
        / (1.0 - beta_one**STEP)
        / (jnp.sqrt(second_new / (1.0 - beta_two**STEP)) + adam_eps)
    )
    master_new = master - step_rate * (direction + decay_rate * master)
    return (master_new, first_new, second_new)


def update_kernel(heads, depth, sums_ref, gattn_ref, gfeat_ref, gfc_ref, gproj_ref, *refs):
    masters, firsts, seconds = refs[0:6], refs[6:12], refs[12:18]
    block_in, dx_in, norm_out = refs[18:21]
    outs, (block_out, dx_out), (feat_grads, block_ref, dx_ref, sems) = refs[21:46], refs[46:48], refs[48:]
    mover = Mover(sems)
    pulls = [mover.plan(block_in, block_ref)(0), mover.plan(dx_in, dx_ref)(0)]
    pushes = [mover.plan(block_ref, block_out)(0), mover.plan(dx_ref, dx_out)(0)]
    for pull in pulls:
        pull.start()
    norm_grads = sums_ref[0:4]
    squares = jnp.sum(sums_ref[4:5, 0:128], keepdims=True) + jnp.sum(norm_grads * norm_grads, keepdims=True)
    grad_norm = jnp.sqrt(squares)
    norm_out[...] = jnp.broadcast_to(grad_norm, norm_out.shape)
    factor = clip_limit / jnp.maximum(grad_norm, clip_limit)
    rates, decays = (0.02, 0.4, 0.15, 0.02, 0.01, 0.3), (0.1, 0.1, 0.1, 0.1, 0.1, 0.0)

    def update(which, at, grads):
        results = adamw_update(
            masters[which][at], firsts[which][at], seconds[which][at], grads, factor, rates[which], decays[which]
        )
        results += (results[0].astype(BF16),)
        if which < 5:
            for kind, value in enumerate(results):
                outs[6 * kind + which][at] = value
        else:
            outs[5][...], outs[11][...] = results[0], results[1]
            outs[17][...], outs[23][...] = results[2][0:2], results[2][2:4]
            outs[24][...] = results[3]

    low = low_half((1, 128))
    for j in range(heads):
        for d in range(0, depth, 2):
            row, other = (gfeat_ref[depth * j + d + k : depth * j + d + k + 1] for k in range(2))
            at = slice(64 * d, 64 * d + 128)
            feat_grads[j, 0:1, at] = jnp.where(low, row, pltpu.roll(other, HD, 1))
            feat_grads[j, 1:2, at] = jnp.where(low, pltpu.roll(row, HD, 1), other)
    for j in range(3):
        update(0, (j,), gattn_ref[:, 256 * j : 256 * j + heads * HD])
        update(1, (slice(HD * j, HD * j + HD),), gattn_ref[:, 256 * j + heads * HD : 256 * j + 256].T)
    update(2, (slice(None),), feat_grads[...])
    update(3, (slice(None),), gfc_ref[...])
    for pull, push in zip(pulls, pushes):
        pull.wait()
        push.start()
    update(4, (slice(None),), gproj_ref[...])
    update(5, (slice(None),), norm_grads)
    for push in pushes:
        push.wait()


def in_vmem(count):
    return [pl.BlockSpec(memory_space=VMEM)] * count


def struct(shape, dtype):
    return jax.ShapeDtypeStruct(shape, dtype)


def call(kernel, outs, smem, operands, scratch, collective_id, name, flops, hbm_in=0, hbm_out=(), limit=63):
    specs = [pl.BlockSpec(memory_space=pltpu.SMEM)] * smem + in_vmem(len(operands) - smem - hbm_in)
    specs += [pl.BlockSpec(memory_space=pl.ANY)] * hbm_in
    out_specs = [pl.BlockSpec(memory_space=pl.ANY if i in hbm_out else VMEM) for i in range(len(outs))]
    traffic = sum(o.size * o.dtype.itemsize for o in outs) + sum(o.size * o.dtype.itemsize for o in operands)
    extra = {} if collective_id is None else {"collective_id": collective_id, "has_side_effects": True}
    return pl.pallas_call(
        kernel,
        out_shape=tuple(outs),
        in_specs=specs,
        out_specs=tuple(out_specs),
        scratch_shapes=scratch,
        compiler_params=pltpu.CompilerParams(vmem_limit_bytes=limit * 2**20, **extra),
        cost_estimate=pl.CostEstimate(flops=flops, bytes_accessed=traffic, transcendentals=0),
        name=name,
    )(*operands)


def on_device(
    sizes,
    block_in,
    cotangent,
    seq_len,
    w_qkv,
    w_out,
    w_feat,
    w_fc,
    w_proj,
    norm_params,
    first_qkv,
    second_qkv,
    first_out,
    second_out,
    first_feat,
    second_feat,
    first_fc,
    second_fc,
    first_proj,
    second_proj,
    first_norms,
    second_norms,
):
    X, Z, H = sizes
    rows, width = block_in.shape
    part, _, head_width = w_qkv.shape
    heads = w_feat.shape[1]
    depth = w_feat.shape[2] // HD
    chunks = rows // CHUNK

    big = (X, Z, H, part, width)
    small = (X, Z, H, FEAT_ROWS, 2 * HD)
    dma = pltpu.SemaphoreType.DMA
    chain_scratch = [
        VMEM((H, heads, 128, 128), F32),
        VMEM((H, heads, 128, 128), BF16),
        VMEM((H, heads, 128, 128), BF16),
        dma((H,)),
        dma((H,)),
    ]
    held = [
        struct((rows, width), BF16),
        struct((H, rows, width), BF16),
        struct((H, rows, 128 * heads), BF16),
        struct((H, rows, 128 * heads), BF16),
        struct((H, heads, chunks, 128, 256), BF16),
        struct((H, rows, 256), BF16),
        struct((H, rows, 256), BF16),
        struct((H, width, 256), BF16),
        struct((2, H, 256, 128 * heads), BF16),
        struct((rows, width), F32),
        struct((rows, width), BF16),
    ]
    normed, qkv, fq, fk, states, mixed, rden, wo, maps, middle, hidden, attn_w, fc_w, proj_w = call(
        functools.partial(attention_forward, sizes, heads, depth),
        held + [struct(big, BF16)] * 3,
        1,
        [seq_len, block_in, w_qkv.transpose(1, 0, 2), w_out, w_feat.transpose(1, 0, 2), w_fc.T, w_proj, norm_params],
        [VMEM(item.shape, item.dtype) for item in held]
        + [
            VMEM((part, width), BF16),
            VMEM((FEAT_ROWS, 128), BF16),
            VMEM((part, width), BF16),
            VMEM((part, width), BF16),
            VMEM((FEAT_ROWS, 128), F32),
            VMEM((4, width), F32),
        ]
        + [VMEM(big, BF16), VMEM(small, BF16), VMEM((H * heads, HD, 128), F32), VMEM((heads, 128, 256), F32)]
        + chain_scratch
        + [dma((6 + 6 * H,))]
        + [sem for _ in range(4) for sem in gather_sems(sizes)],
        0,
        "attention_forward",
        10**10,
        hbm_out=range(14),
    )

    block_out, d_middle, d_att, g_fc, g_proj, g_norm = call(
        functools.partial(feed_forward, sizes),
        [
            struct((rows, width), BF16),
            struct((rows, width), F32),
            struct((rows, width), BF16),
            struct((part, width), F32),
            struct((part, width), F32),
            struct((8, width), F32),
        ],
        0,
        [hidden, cotangent, norm_params, fc_w, proj_w, middle],
        [
            VMEM(big, BF16),
            VMEM(big, BF16),
            VMEM((rows, width), F32),
            VMEM((rows, width), BF16),
            VMEM((rows, width), BF16),
            VMEM(big, BF16),
            VMEM(big, BF16),
            VMEM((rows, width), F32),
            VMEM((rows, width), F32),
            VMEM((rows, H * part), BF16),
            VMEM((rows, H * part), BF16),
            dma((4,)),
            dma((X * Z,)),
            dma((X * Z,)),
        ]
        + scatter_scratch(sizes, (part, width)) * 2,
        1,
        "feed_forward",
        3 * 10**10,
        hbm_in=3,
        hbm_out=range(3),
    )

    pulled = [struct((rows, width), BF16)] + held[:9] + [struct((rows, width), BF16), struct((rows, width), F32)]
    block_in_grad, g_attn, g_feat, sums = call(
        functools.partial(attention_backward, sizes, heads, depth),
        [
            struct((rows, width), F32),
            struct((part, width), F32),
            struct((FEAT_ROWS, 128), F32),
            struct((8, width), F32),
        ],
        1,
        [
            seq_len, norm_params, g_norm, g_fc, g_proj, block_in, normed, qkv, fq, fk, states, mixed, rden, wo, maps,
            attn_w, d_att, d_middle,
        ],
        [VMEM(item.shape, item.dtype) for item in pulled]
        + [
            VMEM((2, X, Z, part, width), BF16),
            VMEM(big, BF16),
            VMEM((8, width), F32),
            VMEM(small, F32),
            VMEM(small, BF16),
            VMEM((H, heads, rows, 128), BF16),
            VMEM((H, heads, chunks, 128, 256), BF16),
            VMEM((heads, 128, 256), F32),
            chain_scratch[0],
            VMEM((rows, width), BF16),
            VMEM((rows, width), F32),
            VMEM((2, 256, 128 * heads), F32),
        ]
        + chain_scratch[1:]
        + [dma((2,)), dma((6 + 7 * H,))]
        + scatter_scratch(sizes, (part, width))
        + scatter_scratch(sizes, (FEAT_ROWS, 128))
        + total_scratch(sizes, (8, width)),
        2,
        "attention_backward",
        2 * 10**10,
        hbm_in=13,
        hbm_out=(0,),
    )

    def turned(qkv, out, feat, fc, proj, *norms):
        return [qkv.transpose(1, 0, 2), out, feat.transpose(1, 0, 2), fc.T, proj, *norms]

    masters = turned(w_qkv, w_out, w_feat, w_fc, w_proj, norm_params)
    firsts = turned(first_qkv, first_out, first_feat, first_fc, first_proj, first_norms)
    seconds = turned(second_qkv, second_out, second_feat, second_fc, second_proj, second_norms)
    shapes = [item.shape for item in masters]
    halves = (2, width)
    norm_filled, *updated, block_out, block_in_grad = call(
        functools.partial(update_kernel, heads, depth),
        [struct((8, 128), F32)]
        + [struct(shape, F32) for shape in shapes * 2 + shapes[:5] + [halves]]
        + [struct(shape, BF16) for shape in shapes[:5]]
        + [struct(halves, F32), struct(shapes[5], BF16)]
        + [struct((rows, width), BF16), struct((rows, width), F32)],
        0,
        [sums, g_attn, g_feat, g_fc, g_proj] + masters + firsts + seconds + [block_out, block_in_grad],
        [VMEM(shapes[2], F32), VMEM((rows, width), BF16), VMEM((rows, width), F32), dma((4,))],
        None,
        "update",
        10**7,
        hbm_in=2,
        hbm_out=(26, 27),
    )
    new, new_first, new_second = (turned(*updated[6 * kind : 6 * kind + 6]) for kind in range(3))
    copies = turned(*updated[18:23], updated[24])
    return (
        norm_filled[0, 0],
        block_out,
        block_in_grad,
        *new,
        *new_first,
        *new_second[:5],
        new_second[5],
        updated[23],
        *copies,
    )


def solution(mesh):
    everything = ("dp", "batch", "head")
    rows = P(everything, None)
    qkv, out, feat = P(("dp", "batch"), None, "head"), P("head", ("dp", "batch")), P(None, "head", ("dp", "batch"))
    fc, proj, whole = P(None, everything), P(everything, None), P()
    weights = (qkv, out, feat, fc, proj, whole)
    in_specs = (rows, rows, P(("dp", "batch"), None)) + weights
    for spec in weights:
        in_specs += (spec, spec)
    out_specs = (whole, rows, rows) + weights + weights + weights[:5] + (whole, whole) + weights
    sizes = (mesh.shape["dp"], mesh.shape["batch"], mesh.shape["head"])
    return jax.shard_map(
        functools.partial(on_device, sizes), mesh=mesh, in_specs=in_specs, out_specs=out_specs, check_vma=False
    )
```

```python
import functools

import jax
import jax.numpy as jnp
from jax import lax
from jax.experimental import pallas as pl
from jax.experimental.pallas import tpu as pltpu
from jax.sharding import PartitionSpec as P

HD = 64
STEP = 8
CHUNK = 256
FEAT_ROWS = 32
FC_TURNS = (0, 4, 8, 12, 16)
PROJ_BEGIN = 0
PROJ_TURNS = (2, 6, 10, 14, 18)
MESH = pl.DeviceIdType.MESH
VMEM = pltpu.VMEM
F32 = jnp.float32
BF16 = jnp.bfloat16

norm_eps = 1e-05
beta_one = 0.9
beta_two = 0.95
adam_eps = 1e-08
clip_limit = 1.0


def dot(left, right):
    return lax.dot_general(left, right, (((1,), (0,)), ((), ())), preferred_element_type=F32)


def dot_nt(left, right):
    return lax.dot_general(left, right, (((1,), (1,)), ((), ())), preferred_element_type=F32)


def dot_tn(left, right):
    return lax.dot_general(left, right, (((0,), (0,)), ((), ())), preferred_element_type=F32)


def flip_bit(value, bit, on=1):
    low = 2**bit
    return value + on * (low - 2 * low * lax.rem(value // low, 2))


class Network:
    def __init__(self, sizes):
        self.X, self.Z, self.H = sizes
        self.dp, self.b, self.h = (lax.axis_index(name) for name in ("dp", "batch", "head"))
        dp_bits, head_bits = self.X.bit_length() - 1, self.H.bit_length() - 1
        if (self.X, self.H) == (2, 4):
            def first(dp, h):
                odd = lax.rem(h, 2)
                return flip_bit(dp, 0, 1 - odd), flip_bit(h, 1, odd)

            def second(dp, h):
                odd = lax.rem(h, 2)
                return flip_bit(dp, 0, odd), flip_bit(h, 1, 1 - odd)

            self.flips = [first, second, lambda dp, h: (dp, flip_bit(h, 0))]
        else:
            self.flips = [lambda dp, h, k=k: (flip_bit(dp, k), h) for k in range(dp_bits)]
            self.flips += [lambda dp, h, k=k: (dp, flip_bit(h, k)) for k in reversed(range(head_bits))]
        self.sets = [()]
        for k in range(len(self.flips)):
            self.sets += [s + (k,) for s in self.sets]
        self.index = {s: i for i, s in enumerate(self.sets)}

    def coord(self, chosen):
        dp, h = self.dp, self.h
        for k in sorted(chosen, reverse=True):
            dp, h = self.flips[k](dp, h)
        return dp, h

    def behind(self, off):
        return lax.rem(self.b + self.Z - off, self.Z)

    def ahead(self, off):
        return lax.rem(self.b + off, self.Z)

    def slot(self, chosen, off):
        dp, h = self.coord(chosen)
        return dp, self.behind(off), h

    def partner(self, k):
        dp, h = self.flips[k](self.dp, self.h)
        return {"dp": dp, "batch": self.b, "head": h}

    def along(self, b):
        return {"dp": self.dp, "batch": b, "head": self.h}

    def stages(self, chosen):
        return range(max(chosen) + 1 if chosen else 0, len(self.flips))

    def plane(self):
        count = self.X * self.H
        mine = self.dp * self.H + self.h
        for step in range(1, count):
            other = lax.rem(mine + step, count)
            yield step, {"dp": other // self.H, "batch": self.b, "head": lax.rem(other, self.H)}

    def barrier(self, chained=False, whole_plane=False):
        pl.semaphore_wait(pltpu.get_barrier_semaphore(), self.greet(chained, whole_plane))

    def greet(self, chained=False, whole_plane=False):
        sem = pltpu.get_barrier_semaphore()
        devices = [self.along(self.ahead(off)) for off in range(1, self.Z)]
        if whole_plane:
            devices += [device for _, device in self.plane()]
        else:
            devices += [self.partner(k) for k in range(len(self.flips))]
            if chained:
                devices += [{"head": lax.rem(self.h + step, self.H)} for step in (1, self.H - 1)]
        for device in devices:
            pl.semaphore_signal(sem, inc=1, device_id=device, device_id_type=MESH)
        return len(devices)


def gather_sems(sizes):
    X, Z, H = sizes
    return [pltpu.SemaphoreType.DMA((X * H + 1, Z)), pltpu.SemaphoreType.DMA((X * H, Z))]


class Gather:
    def __init__(self, net, shard, buf, send, recv, rows=None):
        self.net, self.send, self.recv = net, send, recv
        self.rows = pl.ds(0, shard.shape[0]) if rows is None else rows
        self.shard, self.buf = shard.at[self.rows], buf
        self.inner = (net.b == 1) | (net.b == 2)
        self.ends = send.shape[0] - 1

    def near(self, t):
        b = self.net.b
        return (b, flip_bit(b, 0), 2 - b // 2, 3 - 3 * (b // 2))[t]

    def slot(self, chosen, t):
        dp, h = self.net.coord(chosen)
        return dp, self.near(t), h, self.rows

    def source(self, chosen, t):
        return self.shard if chosen == () and t == 0 else self.buf.at[self.slot(chosen, t)]

    def copy(self, chosen, t, k):
        net = self.net
        into = net.index[chosen + (k,)]
        return pltpu.make_async_remote_copy(
            src_ref=self.source(chosen, t), dst_ref=self.buf.at[self.slot(chosen, t)],
            send_sem=self.send.at[into, t], recv_sem=self.recv.at[into, t],
            device_id=net.partner(k), device_id_type=MESH,
        )

    def hop(self, t, outward, arrives, send_sem):
        net = self.net
        return pltpu.make_async_remote_copy(
            src_ref=self.source((), t), dst_ref=self.buf.at[self.slot((), t)],
            send_sem=send_sem, recv_sem=self.recv.at[0, arrives],
            device_id=net.along(flip_bit(net.b, 0) if outward else 3 - net.b), device_id_type=MESH,
        )

    def pair_hop(self):
        return self.hop(0, True, 1, self.send.at[self.ends, 0])

    def inner_hops(self, t):
        ends = self.send.at[self.ends, 1]
        return self.hop(t, t > 1, (2, 3, 2, 3)[t], self.send.at[0, t] if t else ends)

    def copy_own(self):
        return pltpu.make_async_copy(self.shard, self.buf.at[self.slot((), 0)], self.send.at[self.ends, 2])

    def arrived(self, chosen, t):
        net = self.net
        place = self.buf.at[self.slot(chosen, t)]
        into = net.index[chosen]
        pltpu.make_async_remote_copy(
            src_ref=place, dst_ref=place, send_sem=self.send.at[into, t], recv_sem=self.recv.at[into, t],
            device_id=net.partner(0), device_id_type=MESH,
        ).wait_recv()

    def begin(self):
        self.pair_hop().start()
        pl.when(self.inner)(lambda: self.inner_hops(0).start())
        for k in self.net.stages(()):
            self.copy((), 0, k).start()
        self.copy_own().start()

    def step(self, chosen, t):
        self.arrived(chosen, t)
        if chosen == ():
            pl.when(self.inner)(lambda: self.inner_hops(t).start())
        for k in self.net.stages(chosen):
            self.copy(chosen, t, k).start()

    def steps(self):
        net = self.net
        early = net.sets[: len(net.sets) // 2]
        rounds = [[] for _ in range(net.Z + max(len(chosen) for chosen in early))]
        for t in range(net.Z):
            for chosen in early:
                if chosen or t:
                    rounds[t + len(chosen)].append(functools.partial(self.step, chosen, t))
        late = [functools.partial(self.step, chosen, t) for chosen in net.sets[len(early) :] for t in range(net.Z)]
        return rounds[1:], late

    def finish(self):
        net = self.net
        self.pair_hop().wait_send()

        @pl.when(self.inner)
        def _():
            for t in range(net.Z):
                self.inner_hops(t).wait_send()

        for chosen in net.sets:
            for k in net.stages(chosen):
                for t in range(net.Z):
                    self.copy(chosen, t, k).wait_send()


def scatter_scratch(sizes, shape):
    X, Z, H = sizes
    n = X * H
    return [VMEM((n, Z) + shape, BF16), pltpu.SemaphoreType.DMA((n, Z)), pltpu.SemaphoreType.DMA((n, Z))]


class Scatter:
    def __init__(self, net, along, part, inbox, send, recv):
        self.net, self.along, self.part, self.inbox, self.send, self.recv = net, along, part, inbox, send, recv
        self.last = len(net.flips) - 1

    def sum_at(self, chosen, off):
        return self.inbox.at[self.net.index[chosen + (self.last,)], off]

    def copy(self, chosen, off, k):
        net = self.net
        into = net.index[chosen + (k,)]
        first = k == self.last
        source = self.part.at[net.slot(chosen + (k,), off)] if first else self.sum_at(chosen + (k,), off)
        return pltpu.make_async_remote_copy(
            src_ref=source, dst_ref=self.inbox.at[into, off], send_sem=self.send.at[into, off],
            recv_sem=self.recv.at[into, off], device_id=net.partner(k), device_id_type=MESH,
        )

    def early_sets(self):
        return self.net.sets[: len(self.net.sets) // 2]

    def begin(self, ready=None, offs=None):
        for chosen in reversed(self.early_sets()):

            def start(chosen=chosen):
                for off in range(self.net.Z) if offs is None else offs:
                    self.copy(chosen, off, self.last).start()

            if ready is None:
                start()
            else:
                pl.when(ready(*self.net.coord(chosen + (self.last,))))(start)

    def step(self, chosen, off):
        net = self.net
        total = self.part[net.slot(chosen, off)].astype(F32)
        for k in reversed(net.stages(chosen)):
            self.copy(chosen, off, k).wait_recv()
            total = total + self.inbox[net.index[chosen + (k,)], off].astype(F32)
        if chosen:
            self.sum_at(chosen, off)[...] = total.astype(BF16)
            self.copy(chosen[:-1], off, chosen[-1]).start()
        else:
            self.along.give(off, total.astype(BF16))

    def finish(self):
        net = self.net
        for chosen in net.sets:
            for k in net.stages(chosen):
                for off in range(net.Z):
                    self.copy(chosen, off, k).wait_send()


def along_scratch(sizes, shape):
    X, Z, H = sizes
    return [VMEM((Z,) + shape, BF16), pltpu.SemaphoreType.DMA((Z,)), pltpu.SemaphoreType.DMA((Z,))]


class Along:
    def __init__(self, net, sums, inbox, send, recv):
        self.net, self.sums, self.inbox, self.send, self.recv = net, sums, inbox, send, recv

    def copy(self, off):
        net = self.net
        return pltpu.make_async_remote_copy(
            src_ref=self.sums.at[off], dst_ref=self.inbox.at[off], send_sem=self.send.at[off],
            recv_sem=self.recv.at[off], device_id=net.along(net.behind(off)), device_id_type=MESH,
        )

    def give(self, off, value):
        self.sums[off] = value
        if off:
            self.copy(off).start()

    def result(self):
        total = self.sums[0].astype(F32)
        for off in range(1, self.net.Z):
            self.copy(off).wait_recv()
            total = total + self.inbox[off].astype(F32)
        return total

    def finish(self):
        for off in range(1, self.net.Z):
            self.copy(off).wait_send()


class Keep:
    def __init__(self, sums):
        self.sums = sums

    def give(self, off, value):
        self.sums[off] = value


def total_scratch(sizes, shape):
    X, Z, H = sizes
    count = X * H
    return [
        VMEM((count + Z,) + shape, F32),
        pltpu.SemaphoreType.DMA((count + Z,)),
        pltpu.SemaphoreType.DMA((count + Z,)),
    ]


def total_over_all(net, value, slots, send, recv):
    count, Z = net.X * net.H, net.Z

    def exchange(value, base, mine, size, devices):
        slots[base + mine] = value
        for step, device in devices:
            place = slots.at[base + mine]
            pltpu.make_async_remote_copy(
                src_ref=place, dst_ref=place, send_sem=send.at[base + step], recv_sem=recv.at[base + step],
                device_id=device, device_id_type=MESH,
            ).start()
        for step, device in devices:
            place = slots.at[base + lax.rem(mine + size - step, size)]
            copy = pltpu.make_async_remote_copy(
                src_ref=place, dst_ref=place, send_sem=send.at[base + step], recv_sem=recv.at[base + step],
                device_id=device, device_id_type=MESH,
            )
            copy.wait_recv()
            copy.wait_send()
        total = slots[base]
        for i in range(1, size):
            total = total + slots[base + i]
        return total

    value = exchange(value, 0, net.dp * net.H + net.h, count, list(net.plane()))
    return exchange(value, count, net.b, Z, [(off, net.along(net.ahead(off))) for off in range(1, Z)])


class Mover:
    def __init__(self, sems):
        self.sems, self.used = sems, 0

    def plan(self, source, target, count=None):
        at = self.used
        self.used += 1 if count is None else count

        def make(i):
            if count is None:
                return pltpu.make_async_copy(source, target, self.sems.at[at])
            return pltpu.make_async_copy(source.at[i], target.at[i], self.sems.at[at + i])

        return make


def norm_stats(values):
    mean = jnp.mean(values, axis=-1, keepdims=True)
    center = values - mean
    spread = jnp.mean(center * center, axis=-1, keepdims=True)
    return center, lax.rsqrt(spread + norm_eps)


def norm_backward(values, gain_row, grads):
    center, scale = norm_stats(values)
    normal = center * scale
    inner = grads * gain_row
    part = jnp.mean(inner * normal, axis=-1, keepdims=True)
    back = scale * (inner - jnp.mean(inner, axis=-1, keepdims=True) - normal * part)
    return back, jnp.sum(grads * normal, axis=0, keepdims=True), jnp.sum(grads, axis=0, keepdims=True)


def low_half(shape):
    return lax.rem(lax.broadcasted_iota(jnp.int32, shape, len(shape) - 1), 128) < HD


def swap_halves(values):
    cols = values.shape[1]
    parts = [pltpu.roll(values[:, at : at + 128], HD, 1) for at in range(0, cols, 128)]
    return parts[0] if len(parts) == 1 else jnp.concatenate(parts, axis=1)


def half_ones():
    down = lax.broadcasted_iota(jnp.int32, (128, 128), 0) // HD
    across = lax.broadcasted_iota(jnp.int32, (128, 128), 1) // HD
    return (down == across).astype(BF16)


def feature_pair(scaled, live):
    low = low_half(scaled.shape)
    top = jnp.max(jnp.where(low, scaled, -jnp.inf), axis=-1, keepdims=True)
    bottom = jnp.max(jnp.where(low, -jnp.inf, scaled), axis=-1, keepdims=True)
    powers = jnp.exp(scaled - jnp.where(low, top, bottom))
    sums = dot(powers.astype(BF16), half_ones())
    return powers * (live / sums)


def feature_back(feature, grads):
    product = feature * grads
    return product - feature * dot(product.astype(BF16), half_ones())


class Rows:
    def __init__(self, len_ref, rows, h):
        self.first_len = len_ref[0, 0]
        self.both_len = len_ref[0, 0] + len_ref[0, 1]
        self.start = h * rows
        self.rows = rows

    def second(self, row):
        return row >= self.first_len

    def column(self, chunk):
        return self.start + chunk * CHUNK + lax.broadcasted_iota(jnp.int32, (CHUNK, 1), 0)

    def live(self, chunk):
        return (self.column(chunk) < self.both_len).astype(F32)

    def second_column(self, chunk):
        return self.second(self.column(chunk))

    def masks(self, chunk):
        base = self.start + chunk * CHUNK
        down = base + lax.broadcasted_iota(jnp.int32, (CHUNK, CHUNK), 0)
        across = base + lax.broadcasted_iota(jnp.int32, (CHUNK, CHUNK), 1)
        same = (down >= self.first_len) == (across >= self.first_len)
        return same & (across <= down), same & (across >= down)

    def scalar(self, row):
        return jnp.where(self.second(row), 1.0, 0.0).astype(F32)

    def before(self):
        return self.scalar(self.start - 1)

    def first(self):
        return self.scalar(self.start)

    def last(self):
        return self.scalar(self.start + self.rows - 1)

    def after(self):
        return self.scalar(self.start + self.rows)


def with_ones(block, head, low):
    ones = jnp.ones_like(block)
    return jnp.where(low, block, ones) if head % 2 == 0 else jnp.where(low, ones, block)


def by_sequence(values, second):
    zero = jnp.zeros_like(values)
    return jnp.concatenate([jnp.where(second, zero, values), jnp.where(second, values, zero)], axis=1)


class Chain:
    def __init__(self, step, n, h, same, picked, cin, cout, send, recv):
        self.first = h == (0 if step == 1 else n - 1)
        self.final = h == (n - 1 if step == 1 else 0)
        self.neighbour = {"head": lax.rem(h + n + step, n)}
        self.same, self.picked, self.cin, self.cout, self.send, self.recv = same, picked, cin, cout, send, recv

    def copy(self, g):
        return pltpu.make_async_remote_copy(
            src_ref=self.cout.at[g], dst_ref=self.cin.at[g], send_sem=self.send.at[g], recv_sem=self.recv.at[g],
            device_id=self.neighbour, device_id_type=MESH,
        )

    def step(self, g):
        @pl.when(self.first)
        def _():
            self.cin[g] = jnp.zeros_like(self.cin[g])

        @pl.when(jnp.logical_not(self.first))
        def _():
            self.copy(g).wait_recv()

        @pl.when(jnp.logical_not(self.final))
        def _():
            self.cout[g] = (self.picked[g] + self.cin[g].astype(F32) * self.same).astype(BF16)
            self.copy(g).start()

    def finish(self, n):
        @pl.when(jnp.logical_not(self.final))
        def _():
            for g in range(n):
                self.copy(g).wait_send()


def group_at(h, i, n):
    bits = n.bit_length() - 1
    for k in range(bits):
        h = flip_bit(h, bits - 1 - k, lax.rem(i // 2**k, 2))
    return h


def run_at(slots, i, count):
    for k in range(count):
        if slots.get(k):

            @pl.when(i == k)
            def _(items=slots[k]):
                for item in items:
                    item()


def rest_of(slots, count):
    for k in sorted(slots):
        if k >= count:
            for item in slots[k]:
                item()


def equal(a, b):
    return a * b + (1.0 - a) * (1.0 - b)


def attention_forward(
    sizes, heads, depth, len_ref, x_ref, wqkv_ref, wout_ref, wfeat_ref, wfc_ref, wproj_ref, norm_in,
    normed_out, qkv_out, fq_out, fk_out, state_out, mixed_out, rden_out, wo_out, maps_out, middle_out, hidden_out,
    attn_out, fc_out, proj_out,
    normed_ref, qkv_ref, fq_ref, fk_ref, state_ref, mixed_ref, rden_ref, wo_ref, maps_ref, middle_ref, hidden_ref,
    attn_shard, feat_shard, fc_shard, proj_shard, feat_rows, norm_ref,
    w_ref, fc_ref, proj_ref, feat_ref, pairs_ref, total_ref, picked_ref, cin, cout, chain_send, chain_recv, move_sem,
    *sems,
):
    X, Z, groups = sizes
    net = Network(sizes)
    greeted = net.greet(chained=True)
    lanes_here = heads * HD
    for j in range(3):
        attn_shard[:, 256 * j : 256 * j + 128] = wqkv_ref[j, :, 0:128].astype(BF16)
        attn_shard[:, 256 * j + 128 : 256 * j + 256] = jnp.concatenate(
            [wqkv_ref[j, :, 128:lanes_here], wout_ref[HD * j : HD * j + HD].T], axis=1
        ).astype(BF16)
    feat_rows[...] = jnp.zeros_like(feat_rows)
    low_row = low_half((1, 128))
    for j in range(heads):
        for d in range(depth):
            q, k = (wfeat_ref[j, side : side + 1, 128 * (d // 2) : 128 * (d // 2) + 128] for side in range(2))
            row = jnp.where(low_row, q, pltpu.roll(k, HD, 1)) if d % 2 == 0 else jnp.where(low_row, pltpu.roll(q, HD, 1), k)
            feat_rows[depth * j + d : depth * j + d + 1] = row
    feat_shard[...] = feat_rows[...].astype(BF16)
    fc_shard[...] = wfc_ref[...].astype(BF16)
    proj_shard[...] = wproj_ref[...].astype(BF16)
    norm_ref[...] = norm_in[...].astype(BF16).astype(F32)
    h = net.h
    rows, width = x_ref.shape
    chunks = rows // CHUNK
    seq = Rows(len_ref, rows, h)
    low = low_half((CHUNK, 128))
    mover = Mover(move_sem)
    push_normed, push_wo, push_maps, push_attn = (
        mover.plan(*pair)
        for pair in ((normed_ref, normed_out), (wo_ref, wo_out), (maps_ref, maps_out), (w_ref, attn_out))
    )
    push_qkv, push_fq, push_fk, push_state, push_mixed, push_rden = (
        mover.plan(*pair, groups)
        for pair in (
            (qkv_ref, qkv_out), (fq_ref, fq_out), (fk_ref, fk_out), (state_ref, state_out), (mixed_ref, mixed_out),
            (rden_ref, rden_out),
        )
    )
    push_middle, push_hidden = mover.plan(middle_ref, middle_out), mover.plan(hidden_ref, hidden_out)
    push_fc, push_proj = mover.plan(fc_ref, fc_out), mover.plan(proj_ref, proj_out)

    pl.semaphore_wait(pltpu.get_barrier_semaphore(), greeted)
    part = attn_shard.shape[0]
    cuts = [pl.ds(0, part // 2), pl.ds(part // 2, part // 2)] if part % 32 == 0 else [pl.ds(0, part)]
    feat = Gather(net, feat_shard, feat_ref, *sems[0:2])
    fc, proj = Gather(net, fc_shard, fc_ref, *sems[2:4]), Gather(net, proj_shard, proj_ref, *sems[4:6])
    attns = [Gather(net, attn_shard, w_ref, *sems[6 + 2 * i : 8 + 2 * i], rows) for i, rows in enumerate(cuts)]
    feat.begin()
    for attn in attns:
        attn.begin()

    def first_norm(c, _):
        at = pl.ds(pl.multiple_of(c * CHUNK, CHUNK), CHUNK)
        center, scale = norm_stats(x_ref[at].astype(F32))
        normed_ref[at] = (center * scale * norm_ref[0:1] + norm_ref[1:2]).astype(BF16)
        return 0

    for gather in (feat, *attns):
        gather.copy_own().wait()
    feat_on, feat_in = feat.steps()
    attn_rounds, attn_arrivals = zip(*(attn.steps() for attn in attns))
    attn_on = [sum(steps, []) for steps in zip(*attn_rounds)]
    attn_in = sum(attn_arrivals, [])
    lax.fori_loop(0, chunks, first_norm, 0)
    push_normed(0).start()
    ahead = len(attn_on) - (1 if (X, groups) == (2, 4) else 0)
    for k in range(ahead):
        for step in feat_on[k] + attn_on[k]:
            step()
        if k == Z - 2:
            fc.begin()
        if k == len(feat_on) - 2:
            for step in feat_on[-1] + feat_in:
                step()
            maps_ref[...] = jnp.zeros_like(maps_ref)
            low64 = low_half((HD, 128))
            for i in range(X * Z):
                for g in range(groups):
                    block = feat_ref[i // Z, i % Z, g].astype(F32)
                    for j in range(heads):
                        pairs_ref[g * heads + j, depth * i : depth * i + depth] = block[depth * j : depth * j + depth]
            for g in range(groups):
                for j in range(heads):
                    pair = pairs_ref[g * heads + j]
                    swapped = pltpu.roll(pair, HD, 1)
                    at = slice(HD * j, HD * j + HD), slice(128 * j, 128 * j + 128)
                    maps_ref[0, g, at[0], at[1]] = jnp.where(low64, pair, -swapped).astype(BF16)
                    maps_ref[1, g, at[0], at[1]] = jnp.where(low64, swapped, -pair).astype(BF16)
            push_maps(0).start()

    turns = groups * chunks
    slots = {}
    if ahead < len(attn_on):
        slots[2] = list(attn_on[ahead])
        slots[2 * chunks] = list(attn_in)
    else:
        slots[0] = list(attn_in)
    fc_on, fc_in = fc.steps()
    proj_on, proj_in = proj.steps()
    slots.setdefault(PROJ_BEGIN, []).append(proj.begin)
    for on, turns_at in ((fc_on, FC_TURNS), (proj_on, PROJ_TURNS)):
        for k, steps in enumerate(on):
            slots.setdefault(turns_at[min(k, len(turns_at) - 1)], []).extend(steps)
    mix_slots = {k - turns: items for k, items in slots.items() if k >= turns}
    last = seq.last()

    def project(i, _):
        g = group_at(h, i, groups)
        for j in range(heads):
            total_ref[j] = jnp.zeros_like(total_ref[j])

        def part(c, _):
            run_at(slots, i * chunks + c, turns)
            at = pl.ds(pl.multiple_of(c * CHUNK, CHUNK), CHUNK)
            live, second = seq.live(c), seq.second_column(c)
            qkv = dot(normed_ref[at], w_ref[:, :, g].reshape(width, width)).astype(BF16)
            qkv_ref[g, at] = qkv
            scaled_q = dot(qkv[:, 0:256], maps_ref[0, g])
            scaled_k = dot(qkv[:, 256:512], maps_ref[1, g])
            for j in range(heads):
                lanes = slice(128 * j, 128 * j + 128)
                fq_ref[g, at, lanes] = feature_pair(scaled_q[:, lanes], live).astype(BF16)
                fk = feature_pair(scaled_k[:, lanes], live).astype(BF16)
                fk_ref[g, at, lanes] = fk
                block = qkv[:, 512 + 128 * (j // 2) : 640 + 128 * (j // 2)]
                values = by_sequence(with_ones(block, j, low), second)
                state_ref[g, j, c] = total_ref[j].astype(BF16)
                total_ref[j] += dot_tn(fk, values)
            return 0

        lax.fori_loop(0, chunks, part, 0)
        for push in (push_qkv, push_fq, push_fk):
            push(g).start()
        for j in range(heads):
            picked_ref[g, j] = total_ref[j, :, :128] * (1.0 - last) + total_ref[j, :, 128:] * last
        weight = w_ref[:, :, g].reshape(width, width)
        lowd = low_half((width, 128))
        a = swap_halves(weight[:, 128:256].astype(F32))
        b = weight[:, 384:512].astype(F32)
        c_ = swap_halves(weight[:, 640:768].astype(F32))
        wo_ref[g, :, 0:128] = jnp.where(lowd, a, b).astype(BF16)
        wo_ref[g, :, 128:256] = jnp.where(lowd, c_, 0.0).astype(BF16)
        return 0

    lax.fori_loop(0, groups, project, 0)
    push_wo(0).start()
    push_attn(0).start()

    before = seq.before()
    chain = Chain(1, groups, h, equal(before, last), picked_ref, cin, cout, chain_send, chain_recv)

    def mix(g, _):
        chain.step(g)

        def part(c, _):
            run_at(mix_slots, g * chunks + c, turns)
            at = pl.ds(pl.multiple_of(c * CHUNK, CHUNK), CHUNK)
            live, second = seq.live(c), seq.second_column(c)
            lower, _ = seq.masks(c)
            found = []
            for j in range(heads):
                lanes = slice(128 * j, 128 * j + 128)
                fq, fk = fq_ref[g, at, lanes], fk_ref[g, at, lanes]
                carry = cin[g, j].astype(F32)
                prior = jnp.concatenate([carry * (1.0 - before), carry * before], axis=1)
                state = (state_ref[g, j, c].astype(F32) + prior).astype(BF16)
                state_ref[g, j, c] = state
                scores = jnp.where(lower, dot_nt(fq, fk), 0.0).astype(BF16)
                block = qkv_ref[g, at, 512 + 128 * (j // 2) : 640 + 128 * (j // 2)]
                inter = dot(fq, state)
                found.append(
                    dot(scores, with_ones(block, j, low)) + jnp.where(second, inter[:, 128:], inter[:, :128])
                )
            pair = jnp.where(low, found[0], found[1])
            rden = 1.0 / (swap_halves(jnp.where(low, found[1], found[0])) + (1.0 - live))
            mixed_ref[g, at, 0:128] = (pair * rden).astype(BF16)
            rden_ref[g, at, 0:128] = rden.astype(BF16)
            rden = jnp.where(low, 1.0 / (swap_halves(found[2]) + (1.0 - live)), 1.0)
            mixed_ref[g, at, 128:256] = jnp.where(low, found[2] * rden, 0.0).astype(BF16)
            rden_ref[g, at, 128:256] = rden.astype(BF16)
            return 0

        lax.fori_loop(0, chunks, part, 0)
        for push in (push_state, push_mixed, push_rden):
            push(g).start()
        return 0

    lax.fori_loop(0, groups, mix, 0)
    rest_of(mix_slots, turns)

    def close(c, _):
        at = pl.ds(pl.multiple_of(c * CHUNK, CHUNK), CHUNK)
        attended = dot_nt(mixed_ref[0, at], wo_ref[0])
        for g in range(1, groups):
            attended = attended + dot_nt(mixed_ref[g, at], wo_ref[g])
        middle = x_ref[at].astype(F32) + attended
        middle_ref[at] = middle
        center, scale = norm_stats(middle)
        hidden_ref[at] = (center * scale * norm_ref[2:3] + norm_ref[3:4]).astype(BF16)
        return 0

    lax.fori_loop(0, chunks, close, 0)
    push_middle(0).start()
    push_hidden(0).start()
    for step in fc_in:
        step()
    fc.copy_own().wait()
    push_fc(0).start()
    for step in proj_in:
        step()
    proj.copy_own().wait()
    push_proj(0).start()
    chain.finish(groups)
    for gather in (*attns, feat, fc, proj):
        gather.finish()
    for push in (push_normed, push_wo, push_maps, push_attn, push_middle, push_hidden, push_fc, push_proj):
        push(0).wait()
    for push in (push_qkv, push_fq, push_fk, push_state, push_mixed, push_rden):
        for g in range(groups):
            push(g).wait()


def feed_forward(
    sizes, hidden_ref, dy_ref, norm_ref, fc_in, proj_in, middle_in,
    block_out, dmid_out, datt_out, gfc_sums, gproj_sums, gnorm_ref,
    fc_ref, proj_ref, middle_ref, out_ref, datt_ref, gfc_ref, gproj_ref, branch_ref, dhid_ref, act_ref, dpre_ref,
    move_sem, fc_sem, proj_sem, *scratch,
):
    X, Z, H = sizes
    net = Network(sizes)
    chunks, size, width = fc_ref.shape
    part = gfc_ref.shape[3]
    rows = hidden_ref.shape[0]
    tile = 256
    tiles = rows // tile
    paired = (X, H) == (2, 4)
    odd = lax.rem(net.h, 2)

    if paired:
        far, near = (lax.rem(net.dp + 1, 2), net.dp), (flip_bit(net.h, 1), net.h)
        kinds = {"both": (far[0], near[0]), "x": (far[0], near[1]), "y": (far[1], near[0]), "own": (far[1], near[1])}
        plan = [[("both", off) for off in (3, 2, 1, 0)]]
        plan += [[(kind, off) for off in offs for kind in ("x", "y")] for offs in ((3, 2), (1, 0))]
        plan += [[("own", off) for off in (3, 2, 1, 0)]]
        places = []
        for items in plan:
            places.append([])
            for kind, off in items:
                dp, h = kinds[kind]
                places[-1] += [(dp, net.behind(off), h), (dp, net.behind(off), flip_bit(h, 0))]
    else:
        places = [
            [(lax.rem(net.dp + 1 + i, X), b, h) for b in range(Z) for h in range(H)] for i in range(X)
        ]

    def fetch(i, s):
        at = pl.ds(part * s, part)
        return (
            pltpu.make_async_copy(fc_in.at[places[i][s]], fc_ref.at[i, at], fc_sem.at[i, s]),
            pltpu.make_async_copy(proj_in.at[places[i][s]], proj_ref.at[i, at], proj_sem.at[i, s]),
        )

    for i in range(chunks):
        for s in range(size // part):
            for copy in fetch(i, s):
                copy.start()
    mover = Mover(move_sem)
    pull_middle = mover.plan(middle_in, middle_ref)
    pull_middle(0).start()
    net.barrier()
    scatters = [
        Scatter(net, Keep(gfc_sums), gfc_ref, *scratch[:3]),
        Scatter(net, Keep(gproj_sums), gproj_ref, *scratch[3:]),
    ]
    branch_ref[...] = jnp.zeros_like(branch_ref)
    dhid_ref[...] = jnp.zeros_like(dhid_ref)

    turns = chunks * tiles
    slots = {}
    if paired:
        own, first, second, both = scatters[0].early_sets()

        def add(slot, chosen, off):
            for scatter in scatters:
                slots.setdefault(slot, []).append(functools.partial(scatter.step, chosen, off))

        for k in range(Z):
            off = Z - 1 - k
            add(tiles + k, both, off)
            add((2 + k // 2) * tiles + k % 2, second, off)
            add((2 + k // 2) * tiles + 2 + k % 2, first, off)
            add(turns + k, own, off)
    else:
        for scatter in scatters:
            for chosen in reversed(scatter.early_sets()):
                for off in reversed(range(Z)):
                    slots.setdefault(turns, []).append(functools.partial(scatter.step, chosen, off))

    for i in range(chunks):
        for s in range(size // part):
            for copy in fetch(i, s):
                copy.wait()
        here = {k - i * tiles: items for k, items in slots.items() if i * tiles <= k < (i + 1) * tiles}

        def rowed(c, _, i=i, here=here):
            run_at(here, c, tiles)
            at = pl.ds(pl.multiple_of(c * tile, tile), tile)
            fc, proj = fc_ref[i], proj_ref[i]
            pre = dot_nt(hidden_ref[at], fc)
            square = pre * pre
            inner = jnp.tanh(0.7978845608 * pre * (1.0 + 0.044715 * square))
            half = 0.5 * (1.0 + inner)
            act = (pre * half).astype(BF16)
            slope = half + 0.5 * pre * (1.0 - inner * inner) * (0.7978845608 * (1.0 + 3 * 0.044715 * square))
            dpre = (dot_nt(dy_ref[at], proj) * slope).astype(BF16)
            act_ref[at] = act
            dpre_ref[at] = dpre
            branch_ref[at] += dot(act, proj)
            dhid_ref[at] += dot(dpre, fc)
            return 0

        lax.fori_loop(0, tiles, rowed, 0)
        for grads, left, right in ((gproj_ref, act_ref, dy_ref), (gfc_ref, dpre_ref, hidden_ref)):
            half = size // 2
            for at in (0, half):
                grad = dot_tn(left[:, at : at + half], right[...]).astype(BF16)
                for s in range(half // part):
                    grads[places[i][at // part + s]] = grad[part * s : part * s + part]
        for scatter in scatters:
            if not paired:
                scatter.begin(lambda dp_at, h_at, i=i: dp_at == places[i][0][0])
                continue
            for kind, off in plan[i]:
                if kind == "both" or kind == "own":
                    scatter.copy(both if kind == "both" else own, off, scatter.last).start()
                else:
                    chosen = (first, second) if kind == "y" else (second, first)
                    pl.when(odd == 0)(scatter.copy(chosen[0], off, scatter.last).start)
                    pl.when(odd == 1)(scatter.copy(chosen[1], off, scatter.last).start)

    gnorm_ref[...] = jnp.zeros_like(gnorm_ref)
    pull_middle(0).wait()
    late_slots = {min(k - turns, tiles - 1): [] for k in slots if k >= turns}
    for k in sorted(slots):
        if k >= turns:
            late_slots[min(k - turns, tiles - 1)] += slots[k]

    def close(c, _):
        at = pl.ds(pl.multiple_of(c * tile, tile), tile)
        middle = middle_ref[at]
        out_ref[at] = (middle + branch_ref[at]).astype(BF16)
        back, gain, shift = norm_backward(middle, norm_ref[2:3].astype(BF16).astype(F32), dhid_ref[at])
        dmid = dy_ref[at].astype(F32) + back
        middle_ref[at] = dmid
        datt_ref[at] = dmid.astype(BF16)
        gnorm_ref[2:3] += gain
        gnorm_ref[3:4] += shift
        run_at(late_slots, c, tiles)
        return 0

    lax.fori_loop(0, tiles, close, 0)
    pushes = [mover.plan(*pair) for pair in ((out_ref, block_out), (middle_ref, dmid_out), (datt_ref, datt_out))]
    for push in pushes:
        push(0).start()
    for push in pushes:
        push(0).wait()
    for scatter in scatters:
        scatter.finish()


def attention_backward(
    sizes, heads, depth, len_ref, norm_ref, gnorm_in, gfc_sums, gproj_sums, x_in, normed_in, qkv_in, fq_in, fk_in,
    state_in, mixed_in, rden_in, wo_in, maps_in, w_in, datt_in, dmid_in,
    dx_out, gattn_out, gfeat_out, gfc_ref, gproj_ref, sums_out,
    x_ref, normed_ref, qkv_ref, fq_ref, fk_ref, state_ref, mixed_ref, rden_ref, wo_ref, maps_ref, datt_ref, dmid_ref,
    w_ref, gw_ref, gnorm_ref, featsum_ref, featpart_ref,
    dne_ref, back_ref, total_ref, picked_ref, dnormed_ref, gsum_ref, cin, cout, chain_send, chain_recv,
    w_sem, move_sem, *scratch,
):
    X, Z, H = sizes
    groups = H
    net = Network(sizes)
    h = net.h
    rows, width = x_ref.shape
    chunks = rows // CHUNK
    part = w_ref.shape[3]
    seq = Rows(len_ref, rows, h)
    low = low_half((CHUNK, 128))

    mover = Mover(move_sem)
    pull_datt, pull_maps, pull_normed, pull_x, pull_dmid, push_dx = (
        mover.plan(*pair)
        for pair in (
            (datt_in, datt_ref), (maps_in, maps_ref), (normed_in, normed_ref), (x_in, x_ref), (dmid_in, dmid_ref),
            (dmid_ref, dx_out),
        )
    )
    ahead_pulls = [
        mover.plan(*pair, groups)
        for pair in ((wo_in, wo_ref), (rden_in, rden_ref), (mixed_in, mixed_ref), (fq_in, fq_ref))
    ]
    group_pulls = [
        mover.plan(*pair, groups) for pair in ((fk_in, fk_ref), (state_in, state_ref), (qkv_in, qkv_ref))
    ]

    def pull_weight(i):
        slot = lax.rem(i, 2)
        return pltpu.make_async_copy(w_in.at[:, :, backwards(i)], w_ref.at[slot], w_sem.at[slot])

    def backwards(i):
        return group_at(h, groups - 1 - i, groups)

    pull_datt(0).start()
    for g in range(groups):
        for pull in ahead_pulls:
            pull(g).start()
    pull_maps(0).start()
    for i in range(groups):
        for pull in group_pulls:
            pull(backwards(i)).start()
    pull_weight(0).start()
    pull_weight(1).start()
    pull_normed(0).start()
    pull_x(0).start()
    pull_dmid(0).start()
    net.barrier(whole_plane=True)
    fc_along, proj_along = Along(net, gfc_sums, *scratch[0:3]), Along(net, gproj_sums, *scratch[3:6])
    for off in reversed(range(1, Z)):
        fc_along.copy(off).start()
        proj_along.copy(off).start()
    attn_along, feat_along = Along(net, *scratch[6:10]), Along(net, *scratch[10:14])
    attn = Scatter(net, attn_along, gw_ref, *scratch[14:17])
    feat = Scatter(net, feat_along, featpart_ref, *scratch[17:20])
    odd = lax.rem(h, 2)

    down = lax.broadcasted_iota(jnp.int32, (256, 256), 0) // HD
    across = lax.broadcasted_iota(jnp.int32, (256, 256), 1) // HD
    other_half = ((down // 2 == across // 2) & (down != across)).astype(BF16)
    first = seq.first()
    pull_datt(0).wait()

    def ahead(g, _):
        for j in range(heads):
            total_ref[j] = jnp.zeros_like(total_ref[j])
        for pull in ahead_pulls:
            pull(g).wait()

        def piece(i, _):
            c = chunks - 1 - i
            at = pl.ds(pl.multiple_of(c * CHUNK, CHUNK), CHUNK)
            second = seq.second_column(c)
            dm = dot(datt_ref[at], wo_ref[g]).astype(BF16).astype(F32)
            rden = rden_ref[g, at].astype(F32)
            sums = dot((dm * mixed_ref[g, at].astype(F32)).astype(BF16), other_half)
            dnum = dm * rden
            dden = sums * swap_halves(rden) * (-1.0 / HD)
            for j in range(heads):
                lanes = slice(128 * (j // 2), 128 * (j // 2) + 128)
                mine, other = dnum[:, lanes], dden[:, lanes]
                dne = (jnp.where(low, mine, other) if j % 2 == 0 else jnp.where(low, other, mine)).astype(BF16)
                dne_ref[g, j, at] = dne
                back_ref[g, j, c] = total_ref[j].astype(BF16)
                total_ref[j] += dot_tn(fq_ref[g, at, 128 * j : 128 * j + 128], by_sequence(dne, second))
            return 0

        lax.fori_loop(0, chunks, piece, 0)
        for j in range(heads):
            picked_ref[g, j] = total_ref[j, :, :128] * (1.0 - first) + total_ref[j, :, 128:] * first
        return 0

    lax.fori_loop(0, groups, ahead, 0)
    after = seq.after()
    chain = Chain(-1, groups, h, equal(after, first), picked_ref, cin, cout, chain_send, chain_recv)
    lowd = low_half((width, 128))
    shape = (X, Z, part, 128)

    def out_grads(g, _):
        chain.step(g)
        for third in range(3):
            beside = dot_tn(datt_ref[...], mixed_ref[g, :, 128 * (third // 2) : 128 * (third // 2) + 128])
            if third != 1:
                beside = swap_halves(beside)
            gw_ref[:, :, g, :, 256 * third + 128 : 256 * third + 256] = beside.astype(BF16).reshape(shape)
        return 0

    lax.fori_loop(0, groups, out_grads, 0)

    dnormed_ref[...] = jnp.zeros_like(dnormed_ref)
    pull_maps(0).wait()
    pull_normed(0).wait()

    def group(i, _):
        g = backwards(i)
        for pull in group_pulls:
            pull(g).wait()

        gsum_ref[...] = jnp.zeros_like(gsum_ref)

        def piece(c, _):
            at = pl.ds(pl.multiple_of(c * CHUNK, CHUNK), CHUNK)
            second = seq.second_column(c)
            lower, upper = seq.masks(c)
            dus_q, dus_k, dvs = [], [], []
            for j in range(heads):
                lanes = slice(128 * j, 128 * j + 128)
                fq, fk, dne = fq_ref[g, at, lanes], fk_ref[g, at, lanes], dne_ref[g, j, at]
                carry = cin[g, j].astype(F32)
                later = jnp.concatenate([carry * (1.0 - after), carry * after], axis=1)
                back = (back_ref[g, j, c].astype(F32) + later).astype(BF16)
                state = state_ref[g, j, c]
                block = qkv_ref[g, at, 512 + 128 * (j // 2) : 640 + 128 * (j // 2)]
                values = with_ones(block, j, low)
                scores_t = jnp.where(upper, dot_nt(fk, fq), 0.0).astype(BF16)
                weigh = jnp.where(lower, dot_nt(dne, values), 0.0).astype(BF16)
                weigh_t = jnp.where(upper, dot_nt(values, dne), 0.0).astype(BF16)
                dfq = dot(weigh, fk) + dot_nt(by_sequence(dne, second), state)
                dfk = dot(weigh_t, fq) + dot_nt(by_sequence(values, second), back)
                inter = dot(fk, back)
                dvs.append(dot(scores_t, dne) + jnp.where(second, inter[:, 128:], inter[:, :128]))
                dus_q.append(feature_back(fq.astype(F32), dfq.astype(BF16).astype(F32)).astype(BF16))
                dus_k.append(feature_back(fk.astype(F32), dfk.astype(BF16).astype(F32)).astype(BF16))
            du_q, du_k = jnp.concatenate(dus_q, axis=1), jnp.concatenate(dus_k, axis=1)
            dq = dot_nt(du_q, maps_ref[0, g]).astype(BF16)
            dk = dot_nt(du_k, maps_ref[1, g]).astype(BF16)
            dv = jnp.concatenate([jnp.where(low, dvs[0], dvs[1]), jnp.where(low, dvs[2], 0.0)], axis=1).astype(BF16)
            gsum_ref[0] += dot_tn(qkv_ref[g, at, 0:256], du_q)
            gsum_ref[1] += dot_tn(qkv_ref[g, at, 256:512], du_k)
            dqkv = jnp.concatenate([dq, dk, dv], axis=1)
            qkv_ref[g, at] = dqkv
            return 0

        lax.fori_loop(0, chunks, piece, 0)
        if (X, H) == (2, 4):

            @pl.when((i == groups - 1) & (odd == 1))
            def _():
                for off in reversed(range(Z)):
                    attn.step(attn.early_sets()[1], off)

        low64 = low_half((HD, 128))
        for j in range(heads):
            sums = [gsum_ref[side, HD * j : HD * j + HD, 128 * j : 128 * j + 128] for side in range(2)]
            sums = [value - pltpu.roll(value, HD, 1) for value in sums]
            pair = jnp.where(low64, sums[0], -sums[1])
            for k in range(X * Z):
                featsum_ref[k // Z, k % Z, g, depth * j : depth * j + depth] = pair[depth * k : depth * k + depth]
        for third in range(3):
            grad = dot_tn(normed_ref[...], qkv_ref[g, :, 256 * third : 256 * third + 256])
            at = 256 * third
            gw_ref[:, :, g, :, at : at + 128] = grad[:, 0:128].astype(BF16).reshape(shape)
            beside = gw_ref[:, :, g, :, at + 128 : at + 256].reshape(width, 128)
            gw_ref[:, :, g, :, at + 128 : at + 256] = (
                jnp.where(lowd, grad[:, 128:256], beside.astype(F32)).astype(BF16).reshape(shape)
            )
        attn.begin(lambda dp_at, h_at: h_at == g)

        if (X, H) == (2, 4):

            @pl.when(i == groups - 2)
            def _():
                for off in reversed(range(Z)):
                    attn.step(attn.early_sets()[3], off)

                @pl.when(odd == 0)
                def _():
                    for off in reversed(range(Z)):
                        attn.step(attn.early_sets()[2], off)

        return 0

    featsum_ref[...] = jnp.zeros_like(featsum_ref)
    lax.fori_loop(0, groups, group, 0)
    for k in range(X * Z):
        for g in range(groups):
            featpart_ref[k // Z, k % Z, g] = featsum_ref[k // Z, k % Z, g].astype(BF16)
    feat.begin()

    gnorm_ref[...] = gnorm_in[...]
    turns = groups * chunks
    slots = {}
    for scatter in (attn, feat):
        own, *others = scatter.early_sets()
        for off in reversed(range(Z)):
            late = (Z - 1 - off) * turns // Z
            turn = {chosen: functools.partial(scatter.step, chosen, off) for chosen in (own, *others)}
            if scatter is attn and (X, H) == (2, 4):

                def cross(turn=turn):
                    pl.when(odd == 0)(turn[others[0]])
                    pl.when(odd == 1)(turn[others[1]])

                slots.setdefault(1 + late // 4, []).append(cross)
                slots.setdefault(4 + late * 3 // 4, []).append(turn[own])
            else:
                for k, chosen in enumerate(reversed(others)):
                    slots.setdefault(1 + 4 * k if len(others) == 3 else 1, []).append(turn[chosen])
                slots.setdefault(turns - 2, []).append(turn[own])

    def through(i, _):
        slot = lax.rem(i, 2)
        pull_weight(i).wait()

        def piece(c, _):
            run_at(slots, i * chunks + c, turns)
            at = pl.ds(pl.multiple_of(c * CHUNK, CHUNK), CHUNK)
            dnormed_ref[at] += dot_nt(qkv_ref[backwards(i), at], w_ref[slot].reshape(width, width))
            return 0

        lax.fori_loop(0, chunks, piece, 0)

        @pl.when(i < groups - 2)
        def _():
            pull_weight(i + 2).start()

        return 0

    lax.fori_loop(0, groups, through, 0)
    pull_x(0).wait()
    pull_dmid(0).wait()

    def close(c, _):
        at = pl.ds(pl.multiple_of(c * CHUNK, CHUNK), CHUNK)
        gain_row = norm_ref[0:1].astype(BF16).astype(F32)
        back, gain, shift = norm_backward(x_ref[at].astype(F32), gain_row, dnormed_ref[at])
        dmid_ref[at] = dmid_ref[at] + back
        gnorm_ref[0:1] += gain
        gnorm_ref[1:2] += shift
        return 0

    lax.fori_loop(0, chunks, close, 0)
    push_dx(0).start()
    square = jnp.zeros((1, 128), F32)
    gfc_ref[...] = fc_along.result()
    gproj_ref[...] = proj_along.result()
    gattn_out[...] = attn_along.result()
    gfeat_out[...] = feat_along.result()
    for ref in (gattn_out, gfeat_out, gfc_ref, gproj_ref):
        column = jnp.sum(ref[...] * ref[...], axis=0, keepdims=True)
        for at in range(0, column.shape[1], 128):
            square = square + column[:, at : at + 128]
    gnorm_ref[4:5, 0:128] = square
    sums_out[...] = total_over_all(net, gnorm_ref[...], *scratch[20:])
    push_dx(0).wait()
    chain.finish(groups)
    for moving in (attn, feat, fc_along, proj_along, attn_along, feat_along):
        moving.finish()


def adamw_update(master, first_mom, second_mom, grad_in, factor, step_rate, decay_rate):
    clipped = grad_in * factor
    first_new = beta_one * first_mom + (1.0 - beta_one) * clipped
    second_new = beta_two * second_mom + (1.0 - beta_two) * clipped * clipped
    direction = (
        first_new
        / (1.0 - beta_one**STEP)
        / (jnp.sqrt(second_new / (1.0 - beta_two**STEP)) + adam_eps)
    )
    master_new = master - step_rate * (direction + decay_rate * master)
    return (master_new, first_new, second_new)


def update_kernel(heads, depth, sums_ref, gattn_ref, gfeat_ref, gfc_ref, gproj_ref, *refs):
    masters, firsts, seconds = refs[0:6], refs[6:12], refs[12:18]
    block_in, dx_in, norm_out = refs[18:21]
    outs, (block_out, dx_out), (feat_grads, block_ref, dx_ref, sems) = refs[21:46], refs[46:48], refs[48:]
    mover = Mover(sems)
    pulls = [mover.plan(block_in, block_ref)(0), mover.plan(dx_in, dx_ref)(0)]
    pushes = [mover.plan(block_ref, block_out)(0), mover.plan(dx_ref, dx_out)(0)]
    for pull in pulls:
        pull.start()
    norm_grads = sums_ref[0:4]
    squares = jnp.sum(sums_ref[4:5, 0:128], keepdims=True) + jnp.sum(norm_grads * norm_grads, keepdims=True)
    grad_norm = jnp.sqrt(squares)
    norm_out[...] = jnp.broadcast_to(grad_norm, norm_out.shape)
    factor = clip_limit / jnp.maximum(grad_norm, clip_limit)
    rates, decays = (0.02, 0.4, 0.15, 0.02, 0.01, 0.3), (0.1, 0.1, 0.1, 0.1, 0.1, 0.0)

    def update(which, at, grads):
        results = adamw_update(
            masters[which][at], firsts[which][at], seconds[which][at], grads, factor, rates[which], decays[which]
        )
        results += (results[0].astype(BF16),)
        if which < 5:
            for kind, value in enumerate(results):
                outs[6 * kind + which][at] = value
        else:
            outs[5][...], outs[11][...] = results[0], results[1]
            outs[17][...], outs[23][...] = results[2][0:2], results[2][2:4]
            outs[24][...] = results[3]

    low = low_half((1, 128))
    for j in range(heads):
        for d in range(0, depth, 2):
            row, other = (gfeat_ref[depth * j + d + k : depth * j + d + k + 1] for k in range(2))
            at = slice(64 * d, 64 * d + 128)
            feat_grads[j, 0:1, at] = jnp.where(low, row, pltpu.roll(other, HD, 1))
            feat_grads[j, 1:2, at] = jnp.where(low, pltpu.roll(row, HD, 1), other)
    for j in range(3):
        update(0, (j,), gattn_ref[:, 256 * j : 256 * j + heads * HD])
        update(1, (slice(HD * j, HD * j + HD),), gattn_ref[:, 256 * j + heads * HD : 256 * j + 256].T)
    update(2, (slice(None),), feat_grads[...])
    update(3, (slice(None),), gfc_ref[...])
    for pull, push in zip(pulls, pushes):
        pull.wait()
        push.start()
    update(4, (slice(None),), gproj_ref[...])
    update(5, (slice(None),), norm_grads)
    for push in pushes:
        push.wait()


def in_vmem(count):
    return [pl.BlockSpec(memory_space=VMEM)] * count


def struct(shape, dtype):
    return jax.ShapeDtypeStruct(shape, dtype)


def call(kernel, outs, smem, operands, scratch, collective_id, name, flops, hbm_in=0, hbm_out=(), limit=63):
    specs = [pl.BlockSpec(memory_space=pltpu.SMEM)] * smem + in_vmem(len(operands) - smem - hbm_in)
    specs += [pl.BlockSpec(memory_space=pl.ANY)] * hbm_in
    out_specs = [pl.BlockSpec(memory_space=pl.ANY if i in hbm_out else VMEM) for i in range(len(outs))]
    traffic = sum(o.size * o.dtype.itemsize for o in outs) + sum(o.size * o.dtype.itemsize for o in operands)
    extra = {} if collective_id is None else {"collective_id": collective_id, "has_side_effects": True}
    return pl.pallas_call(
        kernel,
        out_shape=tuple(outs),
        in_specs=specs,
        out_specs=tuple(out_specs),
        scratch_shapes=scratch,
        compiler_params=pltpu.CompilerParams(vmem_limit_bytes=limit * 2**20, **extra),
        cost_estimate=pl.CostEstimate(flops=flops, bytes_accessed=traffic, transcendentals=0),
        name=name,
    )(*operands)


def on_device(
    sizes,
    block_in,
    cotangent,
    seq_len,
    w_qkv,
    w_out,
    w_feat,
    w_fc,
    w_proj,
    norm_params,
    first_qkv,
    second_qkv,
    first_out,
    second_out,
    first_feat,
    second_feat,
    first_fc,
    second_fc,
    first_proj,
    second_proj,
    first_norms,
    second_norms,
):
    X, Z, H = sizes
    rows, width = block_in.shape
    part, _, head_width = w_qkv.shape
    heads = w_feat.shape[1]
    depth = w_feat.shape[2] // HD
    chunks = rows // CHUNK

    big = (X, Z, H, part, width)
    small = (X, Z, H, FEAT_ROWS, 2 * HD)
    dma = pltpu.SemaphoreType.DMA
    chain_scratch = [
        VMEM((H, heads, 128, 128), F32),
        VMEM((H, heads, 128, 128), BF16),
        VMEM((H, heads, 128, 128), BF16),
        dma((H,)),
        dma((H,)),
    ]
    held = [
        struct((rows, width), BF16),
        struct((H, rows, width), BF16),
        struct((H, rows, 128 * heads), BF16),
        struct((H, rows, 128 * heads), BF16),
        struct((H, heads, chunks, 128, 256), BF16),
        struct((H, rows, 256), BF16),
        struct((H, rows, 256), BF16),
        struct((H, width, 256), BF16),
        struct((2, H, 256, 128 * heads), BF16),
        struct((rows, width), F32),
        struct((rows, width), BF16),
    ]
    normed, qkv, fq, fk, states, mixed, rden, wo, maps, middle, hidden, attn_w, fc_w, proj_w = call(
        functools.partial(attention_forward, sizes, heads, depth),
        held + [struct(big, BF16)] * 3,
        1,
        [seq_len, block_in, w_qkv.transpose(1, 0, 2), w_out, w_feat.transpose(1, 0, 2), w_fc.T, w_proj, norm_params],
        [VMEM(item.shape, item.dtype) for item in held]
        + [
            VMEM((part, width), BF16),
            VMEM((FEAT_ROWS, 128), BF16),
            VMEM((part, width), BF16),
            VMEM((part, width), BF16),
            VMEM((FEAT_ROWS, 128), F32),
            VMEM((4, width), F32),
        ]
        + [VMEM(big, BF16), VMEM(big, BF16), VMEM(big, BF16), VMEM(small, BF16), VMEM((H * heads, HD, 128), F32), VMEM((heads, 128, 256), F32)]
        + chain_scratch
        + [dma((8 + 6 * H,))]
        + [sem for _ in range(5) for sem in gather_sems(sizes)],
        0,
        "attention_forward",
        10**10,
        hbm_out=range(14),
    )

    turns = 4 if (X, H) == (2, 4) else X
    size = X * Z * H * part // turns
    block_out, d_middle, d_att, fc_sums, proj_sums, g_norm = call(
        functools.partial(feed_forward, sizes),
        [
            struct((rows, width), BF16),
            struct((rows, width), F32),
            struct((rows, width), BF16),
            struct((Z, part, width), BF16),
            struct((Z, part, width), BF16),
            struct((8, width), F32),
        ],
        0,
        [hidden, cotangent, norm_params, fc_w, proj_w, middle],
        [
            VMEM((turns, size, width), BF16),
            VMEM((turns, size, width), BF16),
            VMEM((rows, width), F32),
            VMEM((rows, width), BF16),
            VMEM((rows, width), BF16),
            VMEM(big, BF16),
            VMEM(big, BF16),
            VMEM((rows, width), F32),
            VMEM((rows, width), F32),
            VMEM((rows, size), BF16),
            VMEM((rows, size), BF16),
            dma((4,)),
            dma((turns, size // part)),
            dma((turns, size // part)),
        ]
        + scatter_scratch(sizes, (part, width)) * 2,
        1,
        "feed_forward",
        3 * 10**10,
        hbm_in=3,
        hbm_out=range(3),
    )

    pulled = [struct((rows, width), BF16)] + held[:9] + [struct((rows, width), BF16), struct((rows, width), F32)]
    block_in_grad, g_attn, g_feat, g_fc, g_proj, sums = call(
        functools.partial(attention_backward, sizes, heads, depth),
        [
            struct((rows, width), F32),
            struct((part, width), F32),
            struct((FEAT_ROWS, 128), F32),
            struct((part, width), F32),
            struct((part, width), F32),
            struct((8, width), F32),
        ],
        1,
        [
            seq_len, norm_params, g_norm, fc_sums, proj_sums, block_in, normed, qkv, fq, fk, states, mixed, rden, wo, maps,
            attn_w, d_att, d_middle,
        ],
        [VMEM(item.shape, item.dtype) for item in pulled]
        + [
            VMEM((2, X, Z, part, width), BF16),
            VMEM(big, BF16),
            VMEM((8, width), F32),
            VMEM(small, F32),
            VMEM(small, BF16),
            VMEM((H, heads, rows, 128), BF16),
            VMEM((H, heads, chunks, 128, 256), BF16),
            VMEM((heads, 128, 256), F32),
            chain_scratch[0],
            VMEM((rows, width), F32),
            VMEM((2, 256, 128 * heads), F32),
        ]
        + chain_scratch[1:]
        + [dma((2,)), dma((6 + 7 * H,))]
        + along_scratch(sizes, (part, width)) * 2
        + [VMEM((Z, part, width), BF16)]
        + along_scratch(sizes, (part, width))
        + [VMEM((Z, FEAT_ROWS, 128), BF16)]
        + along_scratch(sizes, (FEAT_ROWS, 128))
        + scatter_scratch(sizes, (part, width))
        + scatter_scratch(sizes, (FEAT_ROWS, 128))
        + total_scratch(sizes, (8, width)),
        2,
        "attention_backward",
        2 * 10**10,
        hbm_in=13,
        hbm_out=(0,),
    )

    def turned(qkv, out, feat, fc, proj, *norms):
        return [qkv.transpose(1, 0, 2), out, feat.transpose(1, 0, 2), fc.T, proj, *norms]

    masters = turned(w_qkv, w_out, w_feat, w_fc, w_proj, norm_params)
    firsts = turned(first_qkv, first_out, first_feat, first_fc, first_proj, first_norms)
    seconds = turned(second_qkv, second_out, second_feat, second_fc, second_proj, second_norms)
    shapes = [item.shape for item in masters]
    halves = (2, width)
    norm_filled, *updated, block_out, block_in_grad = call(
        functools.partial(update_kernel, heads, depth),
        [struct((8, 128), F32)]
        + [struct(shape, F32) for shape in shapes * 2 + shapes[:5] + [halves]]
        + [struct(shape, BF16) for shape in shapes[:5]]
        + [struct(halves, F32), struct(shapes[5], BF16)]
        + [struct((rows, width), BF16), struct((rows, width), F32)],
        0,
        [sums, g_attn, g_feat, g_fc, g_proj] + masters + firsts + seconds + [block_out, block_in_grad],
        [VMEM(shapes[2], F32), VMEM((rows, width), BF16), VMEM((rows, width), F32), dma((4,))],
        None,
        "update",
        10**7,
        hbm_in=2,
        hbm_out=(26, 27),
    )
    new, new_first, new_second = (turned(*updated[6 * kind : 6 * kind + 6]) for kind in range(3))
    copies = turned(*updated[18:23], updated[24])
    return (
        norm_filled[0, 0],
        block_out,
        block_in_grad,
        *new,
        *new_first,
        *new_second[:5],
        new_second[5],
        updated[23],
        *copies,
    )


def solution(mesh):
    everything = ("dp", "batch", "head")
    rows = P(everything, None)
    qkv, out, feat = P(("dp", "batch"), None, "head"), P("head", ("dp", "batch")), P(None, "head", ("dp", "batch"))
    fc, proj, whole = P(None, everything), P(everything, None), P()
    weights = (qkv, out, feat, fc, proj, whole)
    in_specs = (rows, rows, P(("dp", "batch"), None)) + weights
    for spec in weights:
        in_specs += (spec, spec)
    out_specs = (whole, rows, rows) + weights + weights + weights[:5] + (whole, whole) + weights
    sizes = (mesh.shape["dp"], mesh.shape["batch"], mesh.shape["head"])
    return jax.shard_map(
        functools.partial(on_device, sizes), mesh=mesh, in_specs=in_specs, out_specs=out_specs, check_vma=False
    )
```

```python
import functools

import jax
import jax.numpy as jnp
from jax import lax
from jax.experimental import pallas as pl
from jax.experimental.pallas import tpu as pltpu
from jax.sharding import PartitionSpec as P

HD = 64
STEP = 8
CHUNK = 256
FEAT_ROWS = 32
FC_TURNS = ((0, 0, 2, 5), (4, 7, 10, 13), (14, 17, 20, 24))
PROJ_TURNS = ((1, 1, 3, 6), (5, 8, 11, 15), (16, 19, 22, 27))
MESH = pl.DeviceIdType.MESH
VMEM = pltpu.VMEM
F32 = jnp.float32
BF16 = jnp.bfloat16

norm_eps = 1e-05
beta_one = 0.9
beta_two = 0.95
adam_eps = 1e-08
clip_limit = 1.0


def dot(left, right):
    return lax.dot_general(left, right, (((1,), (0,)), ((), ())), preferred_element_type=F32)


def dot_nt(left, right):
    return lax.dot_general(left, right, (((1,), (1,)), ((), ())), preferred_element_type=F32)


def dot_tn(left, right):
    return lax.dot_general(left, right, (((0,), (0,)), ((), ())), preferred_element_type=F32)


def flip_bit(value, bit, on=1):
    low = 2**bit
    return value + on * (low - 2 * low * lax.rem(value // low, 2))


class Network:
    def __init__(self, sizes, swap=0):
        self.X, self.Z, self.H = sizes
        self.dp, self.b, self.h = (lax.axis_index(name) for name in ("dp", "batch", "head"))
        dp_bits, head_bits = self.X.bit_length() - 1, self.H.bit_length() - 1
        if (self.X, self.H) == (2, 4):
            self.odd = lax.rem(self.h + swap, 2)

            def first(dp, h):
                odd = lax.rem(h + swap, 2)
                return flip_bit(dp, 0, 1 - odd), flip_bit(h, 1, odd)

            def second(dp, h):
                odd = lax.rem(h + swap, 2)
                return flip_bit(dp, 0, odd), flip_bit(h, 1, 1 - odd)

            self.flips = [first, second, lambda dp, h: (dp, flip_bit(h, 0))]
        else:
            self.flips = [lambda dp, h, k=k: (flip_bit(dp, k), h) for k in range(dp_bits)]
            self.flips += [lambda dp, h, k=k: (dp, flip_bit(h, k)) for k in reversed(range(head_bits))]
        self.sets = [()]
        for k in range(len(self.flips)):
            self.sets += [s + (k,) for s in self.sets]
        self.index = {s: i for i, s in enumerate(self.sets)}

    def coord(self, chosen):
        dp, h = self.dp, self.h
        for k in sorted(chosen, reverse=True):
            dp, h = self.flips[k](dp, h)
        return dp, h

    def behind(self, off):
        return lax.rem(self.b + self.Z - off, self.Z)

    def ahead(self, off):
        return lax.rem(self.b + off, self.Z)

    def slot(self, chosen, off):
        dp, h = self.coord(chosen)
        return dp, self.behind(off), h

    def partner(self, k):
        dp, h = self.flips[k](self.dp, self.h)
        return {"dp": dp, "batch": self.b, "head": h}

    def along(self, b):
        return {"dp": self.dp, "batch": b, "head": self.h}

    def stages(self, chosen):
        return range(max(chosen) + 1 if chosen else 0, len(self.flips))

    def plane(self):
        count = self.X * self.H
        mine = self.dp * self.H + self.h
        for step in range(1, count):
            other = lax.rem(mine + step, count)
            yield step, {"dp": other // self.H, "batch": self.b, "head": lax.rem(other, self.H)}

    def barrier(self, chained=False, whole_plane=False):
        pl.semaphore_wait(pltpu.get_barrier_semaphore(), self.greet(chained, whole_plane))

    def greet(self, chained=False, whole_plane=False):
        sem = pltpu.get_barrier_semaphore()
        devices = [self.along(self.ahead(off)) for off in range(1, self.Z)]
        if whole_plane:
            devices += [device for _, device in self.plane()]
        else:
            devices += [self.partner(k) for k in range(len(self.flips))]
            if chained:
                devices += [{"head": lax.rem(self.h + step, self.H)} for step in (1, self.H - 1)]
        for device in devices:
            pl.semaphore_signal(sem, inc=1, device_id=device, device_id_type=MESH)
        return len(devices)


def gather_sems(sizes):
    X, Z, H = sizes
    return [pltpu.SemaphoreType.DMA((X * H + 1, Z)), pltpu.SemaphoreType.DMA((X * H, Z))]


class Gather:
    def __init__(self, net, shard, buf, send, recv, rows=None):
        self.net, self.send, self.recv = net, send, recv
        self.rows = pl.ds(0, shard.shape[0]) if rows is None else rows
        self.shard, self.buf = shard.at[self.rows], buf
        self.inner = (net.b == 1) | (net.b == 2)
        self.ends = send.shape[0] - 1

    def near(self, t):
        b = self.net.b
        return (b, flip_bit(b, 0), 2 - b // 2, 3 - 3 * (b // 2))[t]

    def slot(self, chosen, t):
        dp, h = self.net.coord(chosen)
        return dp, self.near(t), h, self.rows

    def source(self, chosen, t):
        return self.shard if chosen == () and t == 0 else self.buf.at[self.slot(chosen, t)]

    def copy(self, chosen, t, k):
        net = self.net
        into = net.index[chosen + (k,)]
        return pltpu.make_async_remote_copy(
            src_ref=self.source(chosen, t), dst_ref=self.buf.at[self.slot(chosen, t)],
            send_sem=self.send.at[into, t], recv_sem=self.recv.at[into, t],
            device_id=net.partner(k), device_id_type=MESH,
        )

    def hop(self, t, outward, arrives, send_sem):
        net = self.net
        return pltpu.make_async_remote_copy(
            src_ref=self.source((), t), dst_ref=self.buf.at[self.slot((), t)],
            send_sem=send_sem, recv_sem=self.recv.at[0, arrives],
            device_id=net.along(flip_bit(net.b, 0) if outward else 3 - net.b), device_id_type=MESH,
        )

    def pair_hop(self):
        return self.hop(0, True, 1, self.send.at[self.ends, 0])

    def inner_hops(self, t):
        ends = self.send.at[self.ends, 1]
        return self.hop(t, t > 1, (2, 3, 2, 3)[t], self.send.at[0, t] if t else ends)

    def copy_own(self):
        return pltpu.make_async_copy(self.shard, self.buf.at[self.slot((), 0)], self.send.at[self.ends, 2])

    def arrived(self, chosen, t):
        net = self.net
        place = self.buf.at[self.slot(chosen, t)]
        into = net.index[chosen]
        pltpu.make_async_remote_copy(
            src_ref=place, dst_ref=place, send_sem=self.send.at[into, t], recv_sem=self.recv.at[into, t],
            device_id=net.partner(0), device_id_type=MESH,
        ).wait_recv()

    def begin(self):
        self.pair_hop().start()
        pl.when(self.inner)(lambda: self.inner_hops(0).start())
        for k in self.net.stages(()):
            self.copy((), 0, k).start()
        self.copy_own().start()

    def step(self, chosen, t):
        self.arrived(chosen, t)
        if chosen == ():
            pl.when(self.inner)(lambda: self.inner_hops(t).start())
        for k in self.net.stages(chosen):
            self.copy(chosen, t, k).start()

    def steps(self):
        net = self.net
        early = net.sets[: len(net.sets) // 2]
        rounds = [[] for _ in range(net.Z + max(len(chosen) for chosen in early))]
        for t in range(net.Z):
            for chosen in early:
                if chosen or t:
                    rounds[t + len(chosen)].append(functools.partial(self.step, chosen, t))
        late = [functools.partial(self.step, chosen, t) for chosen in net.sets[len(early) :] for t in range(net.Z)]
        return rounds[1:], late

    def layers(self):
        early = self.net.sets[: len(self.net.sets) // 2]
        found = [[[] for _ in range(self.net.Z)] for _ in range(1 + max(len(chosen) for chosen in early))]
        for t in range(self.net.Z):
            for chosen in early:
                if chosen or t:
                    found[len(chosen)][t].append(functools.partial(self.step, chosen, t))
        return found

    def finish(self):
        net = self.net
        self.pair_hop().wait_send()

        @pl.when(self.inner)
        def _():
            for t in range(net.Z):
                self.inner_hops(t).wait_send()

        for chosen in net.sets:
            for k in net.stages(chosen):
                for t in range(net.Z):
                    self.copy(chosen, t, k).wait_send()


def scatter_scratch(sizes, shape):
    X, Z, H = sizes
    n = X * H
    return [VMEM((n, Z) + shape, BF16), pltpu.SemaphoreType.DMA((n, Z)), pltpu.SemaphoreType.DMA((n, Z))]


class Scatter:
    def __init__(self, net, along, part, inbox, send, recv):
        self.net, self.along, self.part, self.inbox, self.send, self.recv = net, along, part, inbox, send, recv
        self.last = len(net.flips) - 1

    def sum_at(self, chosen, off):
        return self.inbox.at[self.net.index[chosen + (self.last,)], off]

    def copy(self, chosen, off, k):
        net = self.net
        into = net.index[chosen + (k,)]
        first = k == self.last
        source = self.part.at[net.slot(chosen + (k,), off)] if first else self.sum_at(chosen + (k,), off)
        return pltpu.make_async_remote_copy(
            src_ref=source, dst_ref=self.inbox.at[into, off], send_sem=self.send.at[into, off],
            recv_sem=self.recv.at[into, off], device_id=net.partner(k), device_id_type=MESH,
        )

    def early_sets(self):
        return self.net.sets[: len(self.net.sets) // 2]

    def begin(self, ready=None, offs=None):
        for chosen in reversed(self.early_sets()):

            def start(chosen=chosen):
                for off in range(self.net.Z) if offs is None else offs:
                    self.copy(chosen, off, self.last).start()

            if ready is None:
                start()
            else:
                pl.when(ready(*self.net.coord(chosen + (self.last,))))(start)

    def step(self, chosen, off):
        net = self.net
        total = self.part[net.slot(chosen, off)].astype(F32)
        for k in reversed(net.stages(chosen)):
            self.copy(chosen, off, k).wait_recv()
            total = total + self.inbox[net.index[chosen + (k,)], off].astype(F32)
        if chosen:
            self.sum_at(chosen, off)[...] = total.astype(BF16)
            self.copy(chosen[:-1], off, chosen[-1]).start()
        else:
            self.along.give(off, total.astype(BF16))

    def finish(self):
        net = self.net
        for chosen in net.sets:
            for k in net.stages(chosen):
                for off in range(net.Z):
                    self.copy(chosen, off, k).wait_send()


def along_scratch(sizes, shape):
    X, Z, H = sizes
    return [VMEM((Z,) + shape, BF16), pltpu.SemaphoreType.DMA((Z,)), pltpu.SemaphoreType.DMA((Z,))]


class Along:
    def __init__(self, net, sums, inbox, send, recv):
        self.net, self.sums, self.inbox, self.send, self.recv = net, sums, inbox, send, recv

    def copy(self, off):
        net = self.net
        return pltpu.make_async_remote_copy(
            src_ref=self.sums.at[off], dst_ref=self.inbox.at[off], send_sem=self.send.at[off],
            recv_sem=self.recv.at[off], device_id=net.along(net.behind(off)), device_id_type=MESH,
        )

    def give(self, off, value):
        self.sums[off] = value
        if off:
            self.copy(off).start()

    def result(self):
        total = self.sums[0].astype(F32)
        for off in range(1, self.net.Z):
            self.copy(off).wait_recv()
            total = total + self.inbox[off].astype(F32)
        return total

    def finish(self):
        for off in range(1, self.net.Z):
            self.copy(off).wait_send()


class Keep:
    def __init__(self, sums):
        self.sums = sums

    def give(self, off, value):
        self.sums[off] = value


def total_scratch(sizes, shape):
    X, Z, H = sizes
    count = X * H
    return [
        VMEM((count + Z,) + shape, F32),
        pltpu.SemaphoreType.DMA((count + Z,)),
        pltpu.SemaphoreType.DMA((count + Z,)),
    ]


def total_over_all(net, value, slots, send, recv):
    count, Z = net.X * net.H, net.Z

    def exchange(value, base, mine, size, devices):
        slots[base + mine] = value
        for step, device in devices:
            place = slots.at[base + mine]
            pltpu.make_async_remote_copy(
                src_ref=place, dst_ref=place, send_sem=send.at[base + step], recv_sem=recv.at[base + step],
                device_id=device, device_id_type=MESH,
            ).start()
        for step, device in devices:
            place = slots.at[base + lax.rem(mine + size - step, size)]
            copy = pltpu.make_async_remote_copy(
                src_ref=place, dst_ref=place, send_sem=send.at[base + step], recv_sem=recv.at[base + step],
                device_id=device, device_id_type=MESH,
            )
            copy.wait_recv()
            copy.wait_send()
        total = slots[base]
        for i in range(1, size):
            total = total + slots[base + i]
        return total

    value = exchange(value, 0, net.dp * net.H + net.h, count, list(net.plane()))
    return exchange(value, count, net.b, Z, [(off, net.along(net.ahead(off))) for off in range(1, Z)])


class Mover:
    def __init__(self, sems):
        self.sems, self.used = sems, 0

    def plan(self, source, target, count=None):
        at = self.used
        self.used += 1 if count is None else count

        def make(i):
            if count is None:
                return pltpu.make_async_copy(source, target, self.sems.at[at])
            return pltpu.make_async_copy(source.at[i], target.at[i], self.sems.at[at + i])

        return make


def norm_stats(values):
    mean = jnp.mean(values, axis=-1, keepdims=True)
    center = values - mean
    spread = jnp.mean(center * center, axis=-1, keepdims=True)
    return center, lax.rsqrt(spread + norm_eps)


def norm_backward(values, gain_row, grads):
    center, scale = norm_stats(values)
    normal = center * scale
    inner = grads * gain_row
    part = jnp.mean(inner * normal, axis=-1, keepdims=True)
    back = scale * (inner - jnp.mean(inner, axis=-1, keepdims=True) - normal * part)
    return back, jnp.sum(grads * normal, axis=0, keepdims=True), jnp.sum(grads, axis=0, keepdims=True)


def low_half(shape):
    return lax.rem(lax.broadcasted_iota(jnp.int32, shape, len(shape) - 1), 128) < HD


def swap_halves(values):
    cols = values.shape[1]
    parts = [pltpu.roll(values[:, at : at + 128], HD, 1) for at in range(0, cols, 128)]
    return parts[0] if len(parts) == 1 else jnp.concatenate(parts, axis=1)


def half_ones():
    down = lax.broadcasted_iota(jnp.int32, (128, 128), 0) // HD
    across = lax.broadcasted_iota(jnp.int32, (128, 128), 1) // HD
    return (down == across).astype(BF16)


def feature_pair(scaled, live):
    low = low_half(scaled.shape)
    top = jnp.max(jnp.where(low, scaled, -jnp.inf), axis=-1, keepdims=True)
    bottom = jnp.max(jnp.where(low, -jnp.inf, scaled), axis=-1, keepdims=True)
    powers = jnp.exp(scaled - jnp.where(low, top, bottom))
    sums = dot(powers.astype(BF16), half_ones())
    return powers * (live / sums)


def feature_back(feature, grads):
    product = feature * grads
    return product - feature * dot(product.astype(BF16), half_ones())


class Rows:
    def __init__(self, len_ref, rows, h):
        self.first_len = len_ref[0, 0]
        self.both_len = len_ref[0, 0] + len_ref[0, 1]
        self.start = h * rows
        self.rows = rows

    def second(self, row):
        return row >= self.first_len

    def column(self, chunk):
        return self.start + chunk * CHUNK + lax.broadcasted_iota(jnp.int32, (CHUNK, 1), 0)

    def live(self, chunk):
        return (self.column(chunk) < self.both_len).astype(F32)

    def second_column(self, chunk):
        return self.second(self.column(chunk))

    def masks(self, chunk):
        base = self.start + chunk * CHUNK
        down = base + lax.broadcasted_iota(jnp.int32, (CHUNK, CHUNK), 0)
        across = base + lax.broadcasted_iota(jnp.int32, (CHUNK, CHUNK), 1)
        same = (down >= self.first_len) == (across >= self.first_len)
        return same & (across <= down), same & (across >= down)

    def scalar(self, row):
        return jnp.where(self.second(row), 1.0, 0.0).astype(F32)

    def before(self):
        return self.scalar(self.start - 1)

    def first(self):
        return self.scalar(self.start)

    def last(self):
        return self.scalar(self.start + self.rows - 1)

    def after(self):
        return self.scalar(self.start + self.rows)


def with_ones(block, head, low):
    ones = jnp.ones_like(block)
    return jnp.where(low, block, ones) if head % 2 == 0 else jnp.where(low, ones, block)


def by_sequence(values, second):
    zero = jnp.zeros_like(values)
    return jnp.concatenate([jnp.where(second, zero, values), jnp.where(second, values, zero)], axis=1)


class Chain:
    def __init__(self, step, n, h, same, picked, cin, cout, send, recv):
        self.first = h == (0 if step == 1 else n - 1)
        self.final = h == (n - 1 if step == 1 else 0)
        self.neighbour = {"head": lax.rem(h + n + step, n)}
        self.same, self.picked, self.cin, self.cout, self.send, self.recv = same, picked, cin, cout, send, recv

    def copy(self, g):
        return pltpu.make_async_remote_copy(
            src_ref=self.cout.at[g], dst_ref=self.cin.at[g], send_sem=self.send.at[g], recv_sem=self.recv.at[g],
            device_id=self.neighbour, device_id_type=MESH,
        )

    def step(self, g):
        @pl.when(self.first)
        def _():
            self.cin[g] = jnp.zeros_like(self.cin[g])

        @pl.when(jnp.logical_not(self.first))
        def _():
            self.copy(g).wait_recv()

        @pl.when(jnp.logical_not(self.final))
        def _():
            self.cout[g] = (self.picked[g] + self.cin[g].astype(F32) * self.same).astype(BF16)
            self.copy(g).start()

    def finish(self, n):
        @pl.when(jnp.logical_not(self.final))
        def _():
            for g in range(n):
                self.copy(g).wait_send()


def group_at(h, i, n):
    bits = n.bit_length() - 1
    for k in range(bits):
        h = flip_bit(h, bits - 1 - k, lax.rem(i // 2**k, 2))
    return h


def run_at(slots, i, count):
    for k in range(count):
        if slots.get(k):

            @pl.when(i == k)
            def _(items=slots[k]):
                for item in items:
                    item()


def rest_of(slots, count):
    for k in sorted(slots):
        if k >= count:
            for item in slots[k]:
                item()


def equal(a, b):
    return a * b + (1.0 - a) * (1.0 - b)


def attention_forward(
    sizes, heads, depth, len_ref, x_ref, wqkv_ref, wout_ref, wfeat_ref, wfc_ref, wproj_ref, norm_in,
    normed_out, qkv_out, fq_out, fk_out, state_out, mixed_out, rden_out, wo_out, maps_out, middle_out, hidden_out,
    attn_out, fc_out, proj_out,
    normed_ref, qkv_ref, fq_ref, fk_ref, state_ref, mixed_ref, rden_ref, wo_ref, maps_ref, middle_ref, hidden_ref,
    turned_ref, attn_shard, feat_shard, fc_shard, proj_shard, feat_rows, norm_ref,
    w_ref, fc_ref, proj_ref, feat_ref, pairs_ref, total_ref, picked_ref, cin, cout, chain_send, chain_recv, move_sem,
    *sems,
):
    X, Z, groups = sizes
    net = Network(sizes)
    greeted = net.greet(chained=True)
    lanes_here = heads * HD
    for j in range(3):
        attn_shard[:, 256 * j : 256 * j + 128] = wqkv_ref[j, :, 0:128].astype(BF16)
        attn_shard[:, 256 * j + 128 : 256 * j + 256] = jnp.concatenate(
            [wqkv_ref[j, :, 128:lanes_here], wout_ref[HD * j : HD * j + HD].T], axis=1
        ).astype(BF16)
    feat_rows[...] = jnp.zeros_like(feat_rows)
    low_row = low_half((1, 128))
    for j in range(heads):
        for d in range(depth):
            q, k = (wfeat_ref[j, side : side + 1, 128 * (d // 2) : 128 * (d // 2) + 128] for side in range(2))
            row = jnp.where(low_row, q, pltpu.roll(k, HD, 1)) if d % 2 == 0 else jnp.where(low_row, pltpu.roll(q, HD, 1), k)
            feat_rows[depth * j + d : depth * j + d + 1] = row
    feat_shard[...] = feat_rows[...].astype(BF16)
    fc_shard[...] = wfc_ref[...].astype(BF16)
    proj_shard[...] = wproj_ref[...].astype(BF16)
    norm_ref[...] = norm_in[...].astype(BF16).astype(F32)
    h = net.h
    rows, width = x_ref.shape
    chunks = rows // CHUNK
    seq = Rows(len_ref, rows, h)
    low = low_half((CHUNK, 128))
    mover = Mover(move_sem)
    push_normed, push_wo, push_maps, push_attn = (
        mover.plan(*pair)
        for pair in ((turned_ref, normed_out), (wo_ref, wo_out), (maps_ref, maps_out), (w_ref, attn_out))
    )
    push_qkv, push_fq, push_fk, push_state, push_mixed, push_rden = (
        mover.plan(*pair, groups)
        for pair in (
            (qkv_ref, qkv_out), (fq_ref, fq_out), (fk_ref, fk_out), (state_ref, state_out), (mixed_ref, mixed_out),
            (rden_ref, rden_out),
        )
    )
    push_middle, push_hidden = mover.plan(middle_ref, middle_out), mover.plan(hidden_ref, hidden_out)
    push_fc, push_proj = mover.plan(fc_ref, fc_out), mover.plan(proj_ref, proj_out)

    pl.semaphore_wait(pltpu.get_barrier_semaphore(), greeted)
    part = attn_shard.shape[0]
    cuts = [pl.ds(0, part // 2), pl.ds(part // 2, part // 2)] if part % 32 == 0 else [pl.ds(0, part)]
    feat = Gather(net, feat_shard, feat_ref, *sems[0:2])
    nets = net, Network(sizes, 1)
    fc, proj = Gather(nets[0], fc_shard, fc_ref, *sems[2:4]), Gather(nets[1], proj_shard, proj_ref, *sems[4:6])
    attns = [Gather(nets[i], attn_shard, w_ref, *sems[6 + 2 * i : 8 + 2 * i], rows) for i, rows in enumerate(cuts)]
    feat.begin()
    for attn in attns:
        attn.begin()

    def first_norm(c, _):
        at = pl.ds(pl.multiple_of(c * CHUNK, CHUNK), CHUNK)
        center, scale = norm_stats(x_ref[at].astype(F32))
        normed_ref[at] = (center * scale * norm_ref[0:1] + norm_ref[1:2]).astype(BF16)
        return 0

    for gather in (feat, *attns):
        gather.copy_own().wait()
    feat_on, feat_in = feat.steps()
    attn_rounds, attn_arrivals = zip(*(attn.steps() for attn in attns))
    attn_on = [sum(steps, []) for steps in zip(*attn_rounds)]
    attn_in = sum(attn_arrivals, [])
    lax.fori_loop(0, chunks, first_norm, 0)
    ahead = len(attn_on) - (1 if (X, groups) == (2, 4) else 0)
    for k in range(ahead):
        for step in feat_on[k] + attn_on[k]:
            step()
        if k == Z - 2:
            fc.begin()
            proj.begin()
        if k == len(feat_on) - 2:
            for step in feat_on[-1] + feat_in:
                step()
            maps_ref[...] = jnp.zeros_like(maps_ref)
            low64 = low_half((HD, 128))
            for i in range(X * Z):
                for g in range(groups):
                    block = feat_ref[i // Z, i % Z, g].astype(F32)
                    for j in range(heads):
                        pairs_ref[g * heads + j, depth * i : depth * i + depth] = block[depth * j : depth * j + depth]
            for g in range(groups):
                for j in range(heads):
                    pair = pairs_ref[g * heads + j]
                    swapped = pltpu.roll(pair, HD, 1)
                    at = slice(HD * j, HD * j + HD), slice(128 * j, 128 * j + 128)
                    maps_ref[0, g, at[0], at[1]] = jnp.where(low64, pair, -swapped).astype(BF16)
                    maps_ref[1, g, at[0], at[1]] = jnp.where(low64, swapped, -pair).astype(BF16)
            push_maps(0).start()

    turns = groups * chunks
    slots = {}
    if ahead < len(attn_on):
        slots[2] = list(attn_on[ahead])
        slots[2 * chunks] = list(attn_in)
    else:
        slots[0] = list(attn_in)
    fc_in, proj_in = fc.steps()[1], proj.steps()[1]
    for gather, plan in ((fc, FC_TURNS), (proj, PROJ_TURNS)):
        for k, layer in enumerate(gather.layers()):
            for t, steps in enumerate(layer):
                slots.setdefault(plan[min(k, 2)][t] + 2 * max(k - 2, 0), []).extend(steps)
    mix_slots = {k - turns: items for k, items in slots.items() if k >= turns}
    last = seq.last()

    def project(i, _):
        g = group_at(h, i, groups)
        for j in range(heads):
            total_ref[j] = jnp.zeros_like(total_ref[j])

        def part(c, _):
            run_at(slots, i * chunks + c, turns)
            at = pl.ds(pl.multiple_of(c * CHUNK, CHUNK), CHUNK)
            live, second = seq.live(c), seq.second_column(c)
            qkv = dot(normed_ref[at], w_ref[:, :, g].reshape(width, width)).astype(BF16)
            qkv_ref[g, at] = qkv
            scaled_q = dot(qkv[:, 0:256], maps_ref[0, g])
            scaled_k = dot(qkv[:, 256:512], maps_ref[1, g])
            for j in range(heads):
                lanes = slice(128 * j, 128 * j + 128)
                fq_ref[g, at, lanes] = feature_pair(scaled_q[:, lanes], live).astype(BF16)
                fk = feature_pair(scaled_k[:, lanes], live).astype(BF16)
                fk_ref[g, at, lanes] = fk
                block = qkv[:, 512 + 128 * (j // 2) : 640 + 128 * (j // 2)]
                values = by_sequence(with_ones(block, j, low), second)
                state_ref[g, j, c] = total_ref[j].astype(BF16)
                total_ref[j] += dot_tn(fk, values)
            return 0

        lax.fori_loop(0, chunks, part, 0, unroll=2)
        for push in (push_qkv, push_fq, push_fk):
            push(g).start()
        for j in range(heads):
            picked_ref[g, j] = total_ref[j, :, :128] * (1.0 - last) + total_ref[j, :, 128:] * last
        weight = w_ref[:, :, g].reshape(width, width)
        lowd = low_half((width, 128))
        a = swap_halves(weight[:, 128:256].astype(F32))
        b = weight[:, 384:512].astype(F32)
        c_ = swap_halves(weight[:, 640:768].astype(F32))
        wo_ref[g, :, 0:128] = jnp.where(lowd, a, b).astype(BF16)
        wo_ref[g, :, 128:256] = jnp.where(lowd, c_, 0.0).astype(BF16)
        return 0

    lax.fori_loop(0, groups, project, 0)
    push_wo(0).start()
    push_attn(0).start()

    before = seq.before()
    chain = Chain(1, groups, h, equal(before, last), picked_ref, cin, cout, chain_send, chain_recv)

    def mix(g, _):
        chain.step(g)

        def part(c, _):
            run_at(mix_slots, g * chunks + c, turns)
            at = pl.ds(pl.multiple_of(c * CHUNK, CHUNK), CHUNK)
            live, second = seq.live(c), seq.second_column(c)
            lower, _ = seq.masks(c)
            found = []
            for j in range(heads):
                lanes = slice(128 * j, 128 * j + 128)
                fq, fk = fq_ref[g, at, lanes], fk_ref[g, at, lanes]
                carry = cin[g, j].astype(F32)
                prior = jnp.concatenate([carry * (1.0 - before), carry * before], axis=1)
                state = (state_ref[g, j, c].astype(F32) + prior).astype(BF16)
                state_ref[g, j, c] = state
                scores = jnp.where(lower, dot_nt(fq, fk), 0.0).astype(BF16)
                block = qkv_ref[g, at, 512 + 128 * (j // 2) : 640 + 128 * (j // 2)]
                inter = dot(fq, state)
                found.append(
                    dot(scores, with_ones(block, j, low)) + jnp.where(second, inter[:, 128:], inter[:, :128])
                )
            pair = jnp.where(low, found[0], found[1])
            rden = 1.0 / (swap_halves(jnp.where(low, found[1], found[0])) + (1.0 - live))
            mixed_ref[g, at, 0:128] = (pair * rden).astype(BF16)
            rden_ref[g, at, 0:128] = rden.astype(BF16)
            rden = jnp.where(low, 1.0 / (swap_halves(found[2]) + (1.0 - live)), 1.0)
            mixed_ref[g, at, 128:256] = jnp.where(low, found[2] * rden, 0.0).astype(BF16)
            rden_ref[g, at, 128:256] = rden.astype(BF16)
            return 0

        lax.fori_loop(0, chunks, part, 0, unroll=2)
        for push in (push_state, push_mixed, push_rden):
            push(g).start()
        return 0

    lax.fori_loop(0, groups, mix, 0)
    rest_of(mix_slots, turns)

    def close(c, _):
        at = pl.ds(pl.multiple_of(c * CHUNK, CHUNK), CHUNK)
        attended = dot_nt(mixed_ref[0, at], wo_ref[0])
        for g in range(1, groups):
            attended = attended + dot_nt(mixed_ref[g, at], wo_ref[g])
        middle = x_ref[at].astype(F32) + attended
        middle_ref[at] = middle
        center, scale = norm_stats(middle)
        hidden_ref[at] = (center * scale * norm_ref[2:3] + norm_ref[3:4]).astype(BF16)
        return 0

    lax.fori_loop(0, chunks, close, 0)
    push_middle(0).start()
    push_hidden(0).start()
    def turn(c, _):
        at = pl.ds(pl.multiple_of(c * CHUNK, CHUNK), CHUNK)
        turned_ref[:, at] = normed_ref[at].T
        return 0

    lax.fori_loop(0, chunks, turn, 0)
    push_normed(0).start()
    for step in fc_in:
        step()
    fc.copy_own().wait()
    push_fc(0).start()
    for step in proj_in:
        step()
    proj.copy_own().wait()
    push_proj(0).start()
    chain.finish(groups)
    for gather in (*attns, feat, fc, proj):
        gather.finish()
    for push in (push_normed, push_wo, push_maps, push_attn, push_middle, push_hidden, push_fc, push_proj):
        push(0).wait()
    for push in (push_qkv, push_fq, push_fk, push_state, push_mixed, push_rden):
        for g in range(groups):
            push(g).wait()


def feed_forward(
    sizes, hidden_ref, dy_ref, norm_ref, fc_in, proj_in, middle_in,
    block_out, dmid_out, datt_out, dattt_out, gfc_sums, gproj_sums, gnorm_ref,
    fc_ref, proj_ref, middle_ref, out_ref, datt_ref, dattt_ref, gfc_ref, gproj_ref, branch_ref, dhid_ref, act_ref, dpre_ref,
    move_sem, fc_sem, proj_sem, *scratch,
):
    X, Z, H = sizes
    net = Network(sizes)
    chunks, size, width = fc_ref.shape
    part = gfc_ref.shape[3]
    rows = hidden_ref.shape[0]
    tile = 256
    tiles = rows // tile
    paired = (X, H) == (2, 4)

    if paired:
        far, near = (lax.rem(net.dp + 1, 2), net.dp), (flip_bit(net.h, 1), net.h)
        kinds = {"both": (far[0], near[0]), "x": (far[0], near[1]), "y": (far[1], near[0]), "own": (far[1], near[1])}
        plan = [[("both", off) for off in (3, 2, 1, 0)]]
        plan += [[(kind, off) for off in offs for kind in ("x", "y")] for offs in ((3, 2), (1, 0))]
        plan += [[("own", off) for off in (3, 2, 1, 0)]]
        places = []
        for items in plan:
            places.append([])
            for kind, off in items:
                dp, h = kinds[kind]
                places[-1] += [(dp, net.behind(off), h), (dp, net.behind(off), flip_bit(h, 0))]
    else:
        places = [
            [(lax.rem(net.dp + 1 + i, X), b, h) for b in range(Z) for h in range(H)] for i in range(X)
        ]

    def fetch(i, s):
        at = pl.ds(part * s, part)
        return (
            pltpu.make_async_copy(fc_in.at[places[i][s]], fc_ref.at[i, at], fc_sem.at[i, s]),
            pltpu.make_async_copy(proj_in.at[places[i][s]], proj_ref.at[i, at], proj_sem.at[i, s]),
        )

    for i in range(chunks):
        for s in range(size // part):
            for copy in fetch(i, s):
                copy.start()
    mover = Mover(move_sem)
    pull_middle = mover.plan(middle_in, middle_ref)
    pull_middle(0).start()
    net.barrier()
    scatters = [
        Scatter(net, Keep(gfc_sums), gfc_ref, *scratch[:3]),
        Scatter(Network(sizes, 1), Keep(gproj_sums), gproj_ref, *scratch[3:]),
    ]
    branch_ref[...] = jnp.zeros_like(branch_ref)
    dhid_ref[...] = jnp.zeros_like(dhid_ref)

    turns = chunks * tiles
    slots = {}
    if paired:
        own, first, second, both = scatters[0].early_sets()

        def add(slot, chosen, off):
            for scatter in scatters:
                slots.setdefault(slot, []).append(functools.partial(scatter.step, chosen, off))

        for k in range(Z):
            off = Z - 1 - k
            add(tiles + k // 2, both, off)
            add((2 + k // 2) * tiles, second, off)
            add((2 + k // 2) * tiles + 1, first, off)
            add(turns + k, own, off)
    else:
        for scatter in scatters:
            for chosen in reversed(scatter.early_sets()):
                for off in reversed(range(Z)):
                    slots.setdefault(turns, []).append(functools.partial(scatter.step, chosen, off))

    for i in range(chunks):
        for s in range(size // part):
            for copy in fetch(i, s):
                copy.wait()
        here = {k - i * tiles: items for k, items in slots.items() if i * tiles <= k < (i + 1) * tiles}

        def rowed(c, _, i=i, here=here):
            run_at(here, c, tiles)
            at = pl.ds(pl.multiple_of(c * tile, tile), tile)
            fc, proj = fc_ref[i], proj_ref[i]
            pre = dot_nt(hidden_ref[at], fc)
            square = pre * pre
            inner = jnp.tanh(0.7978845608 * pre * (1.0 + 0.044715 * square))
            half = 0.5 * (1.0 + inner)
            act = (pre * half).astype(BF16)
            slope = half + 0.5 * pre * (1.0 - inner * inner) * (0.7978845608 * (1.0 + 3 * 0.044715 * square))
            dpre = (dot_nt(dy_ref[at], proj) * slope).astype(BF16)
            act_ref[at] = act
            dpre_ref[at] = dpre
            branch_ref[at] += dot(act, proj)
            dhid_ref[at] += dot(dpre, fc)
            return 0

        lax.fori_loop(0, tiles, rowed, 0)
        pieces = ((scatters[1], gproj_ref, act_ref, dy_ref), (scatters[0], gfc_ref, dpre_ref, hidden_ref))
        for scatter, grads, left, right in pieces:
            half = size // 2
            for at in (0, half):
                grad = dot_tn(left[:, at : at + half], right[...]).astype(BF16)
                for s in range(half // part):
                    grads[places[i][at // part + s]] = grad[part * s : part * s + part]
            if not paired:
                scatter.begin(lambda dp_at, h_at, i=i: dp_at == places[i][0][0])
                continue
            for kind, off in plan[i]:
                if kind == "both" or kind == "own":
                    scatter.copy(both if kind == "both" else own, off, scatter.last).start()
                else:
                    chosen = (first, second) if kind == "y" else (second, first)
                    pl.when(scatter.net.odd == 0)(scatter.copy(chosen[0], off, scatter.last).start)
                    pl.when(scatter.net.odd == 1)(scatter.copy(chosen[1], off, scatter.last).start)

    gnorm_ref[...] = jnp.zeros_like(gnorm_ref)
    pull_middle(0).wait()
    late_slots = {min(k - turns, tiles - 1): [] for k in slots if k >= turns}
    for k in sorted(slots):
        if k >= turns:
            late_slots[min(k - turns, tiles - 1)] += slots[k]

    def close(c, _):
        at = pl.ds(pl.multiple_of(c * tile, tile), tile)
        middle = middle_ref[at]
        out_ref[at] = (middle + branch_ref[at]).astype(BF16)
        back, gain, shift = norm_backward(middle, norm_ref[2:3].astype(BF16).astype(F32), dhid_ref[at])
        dmid = dy_ref[at].astype(F32) + back
        middle_ref[at] = dmid
        datt_ref[at] = dmid.astype(BF16)
        dattt_ref[:, at] = dmid.astype(BF16).T
        gnorm_ref[2:3] += gain
        gnorm_ref[3:4] += shift
        run_at(late_slots, c, tiles)
        return 0

    lax.fori_loop(0, tiles, close, 0)
    outs = ((out_ref, block_out), (middle_ref, dmid_out), (datt_ref, datt_out), (dattt_ref, dattt_out))
    pushes = [mover.plan(*pair) for pair in outs]
    for push in pushes:
        push(0).start()
    for push in pushes:
        push(0).wait()
    for scatter in scatters:
        scatter.finish()


def attention_backward(
    sizes, heads, depth, len_ref, norm_ref, gnorm_in, gfc_sums, gproj_sums, x_in, normed_in, qkv_in, fq_in, fk_in,
    state_in, mixed_in, rden_in, wo_in, maps_in, w_in, datt_in, dattt_in, dmid_in,
    dx_out, gattn_out, gfeat_out, gfc_ref, gproj_ref, sums_out,
    x_ref, normed_ref, qkv_ref, fq_ref, fk_ref, state_ref, mixed_ref, rden_ref, wo_ref, maps_ref, datt_ref, dattt_ref, dmid_ref,
    w_ref, gw_ref, gnorm_ref, featsum_ref, featpart_ref,
    dne_ref, back_ref, total_ref, picked_ref, dnormed_ref, gsum_ref, cin, cout, chain_send, chain_recv,
    w_sem, move_sem, *scratch,
):
    X, Z, H = sizes
    groups = H
    net = Network(sizes)
    h = net.h
    rows, width = x_ref.shape
    chunks = rows // CHUNK
    part = w_ref.shape[3]
    seq = Rows(len_ref, rows, h)
    low = low_half((CHUNK, 128))

    mover = Mover(move_sem)
    pull_datt, pull_dattt, pull_maps, pull_normed, pull_x, pull_dmid, push_dx = (
        mover.plan(*pair)
        for pair in (
            (datt_in, datt_ref), (dattt_in, dattt_ref), (maps_in, maps_ref), (normed_in, normed_ref), (x_in, x_ref), (dmid_in, dmid_ref),
            (dmid_ref, dx_out),
        )
    )
    ahead_pulls = [
        mover.plan(*pair, groups)
        for pair in ((wo_in, wo_ref), (rden_in, rden_ref), (mixed_in, mixed_ref), (fq_in, fq_ref))
    ]
    group_pulls = [
        mover.plan(*pair, groups) for pair in ((fk_in, fk_ref), (state_in, state_ref), (qkv_in, qkv_ref))
    ]

    def pull_weight(i):
        slot = lax.rem(i, 2)
        return pltpu.make_async_copy(w_in.at[:, :, backwards(i)], w_ref.at[slot], w_sem.at[slot])

    def backwards(i):
        return group_at(h, groups - 1 - i, groups)

    pull_datt(0).start()
    for g in range(groups):
        for pull in ahead_pulls:
            pull(g).start()
    pull_dattt(0).start()
    pull_maps(0).start()
    for i in range(groups):
        for pull in group_pulls:
            pull(backwards(i)).start()
    pull_weight(0).start()
    pull_weight(1).start()
    pull_normed(0).start()
    pull_x(0).start()
    pull_dmid(0).start()
    net.barrier(whole_plane=True)
    fc_along, proj_along = Along(net, gfc_sums, *scratch[0:3]), Along(net, gproj_sums, *scratch[3:6])
    for off in reversed(range(1, Z)):
        fc_along.copy(off).start()
        proj_along.copy(off).start()
    attn_along, feat_along = Along(net, *scratch[6:10]), Along(net, *scratch[10:14])
    attn = Scatter(net, attn_along, gw_ref, *scratch[14:17])
    feat = Scatter(net, feat_along, featpart_ref, *scratch[17:20])
    odd = lax.rem(h, 2)

    down = lax.broadcasted_iota(jnp.int32, (256, 256), 0) // HD
    across = lax.broadcasted_iota(jnp.int32, (256, 256), 1) // HD
    other_half = ((down // 2 == across // 2) & (down != across)).astype(BF16)
    first = seq.first()
    pull_datt(0).wait()

    def ahead(g, _):
        for j in range(heads):
            total_ref[j] = jnp.zeros_like(total_ref[j])
        for pull in ahead_pulls:
            pull(g).wait()

        def piece(i, _):
            c = chunks - 1 - i
            at = pl.ds(pl.multiple_of(c * CHUNK, CHUNK), CHUNK)
            second = seq.second_column(c)
            dm = dot(datt_ref[at], wo_ref[g]).astype(BF16).astype(F32)
            rden = rden_ref[g, at].astype(F32)
            sums = dot((dm * mixed_ref[g, at].astype(F32)).astype(BF16), other_half)
            dnum = dm * rden
            dden = sums * swap_halves(rden) * (-1.0 / HD)
            for j in range(heads):
                lanes = slice(128 * (j // 2), 128 * (j // 2) + 128)
                mine, other = dnum[:, lanes], dden[:, lanes]
                dne = (jnp.where(low, mine, other) if j % 2 == 0 else jnp.where(low, other, mine)).astype(BF16)
                dne_ref[g, j, at] = dne
                back_ref[g, j, c] = total_ref[j].astype(BF16)
                total_ref[j] += dot_tn(fq_ref[g, at, 128 * j : 128 * j + 128], by_sequence(dne, second))
            return 0

        lax.fori_loop(0, chunks, piece, 0, unroll=2)
        for j in range(heads):
            picked_ref[g, j] = total_ref[j, :, :128] * (1.0 - first) + total_ref[j, :, 128:] * first
        return 0

    lax.fori_loop(0, groups, ahead, 0)
    after = seq.after()
    chain = Chain(-1, groups, h, equal(after, first), picked_ref, cin, cout, chain_send, chain_recv)
    lowd = low_half((width, 128))
    shape = (X, Z, part, 128)

    def out_grads(g, _):
        chain.step(g)
        beside = dot(dattt_ref[...], mixed_ref[g])
        for third, value in enumerate((swap_halves(beside[:, :128]), beside[:, :128], swap_halves(beside[:, 128:]))):
            gw_ref[:, :, g, :, 256 * third + 128 : 256 * third + 256] = value.astype(BF16).reshape(shape)
        return 0

    pull_dattt(0).wait()
    lax.fori_loop(0, groups, out_grads, 0)

    dnormed_ref[...] = jnp.zeros_like(dnormed_ref)
    pull_maps(0).wait()
    pull_normed(0).wait()

    def group(i, _):
        g = backwards(i)
        for pull in group_pulls:
            pull(g).wait()

        gsum_ref[...] = jnp.zeros_like(gsum_ref)

        def piece(c, _):
            at = pl.ds(pl.multiple_of(c * CHUNK, CHUNK), CHUNK)
            second = seq.second_column(c)
            lower, upper = seq.masks(c)
            dus_q, dus_k, dvs = [], [], []
            for j in range(heads):
                lanes = slice(128 * j, 128 * j + 128)
                fq, fk, dne = fq_ref[g, at, lanes], fk_ref[g, at, lanes], dne_ref[g, j, at]
                carry = cin[g, j].astype(F32)
                later = jnp.concatenate([carry * (1.0 - after), carry * after], axis=1)
                back = (back_ref[g, j, c].astype(F32) + later).astype(BF16)
                state = state_ref[g, j, c]
                block = qkv_ref[g, at, 512 + 128 * (j // 2) : 640 + 128 * (j // 2)]
                values = with_ones(block, j, low)
                scores_t = jnp.where(upper, dot_nt(fk, fq), 0.0).astype(BF16)
                weigh = jnp.where(lower, dot_nt(dne, values), 0.0).astype(BF16)
                weigh_t = jnp.where(upper, dot_nt(values, dne), 0.0).astype(BF16)
                dfq = dot(weigh, fk) + dot_nt(by_sequence(dne, second), state)
                dfk = dot(weigh_t, fq) + dot_nt(by_sequence(values, second), back)
                inter = dot(fk, back)
                dvs.append(dot(scores_t, dne) + jnp.where(second, inter[:, 128:], inter[:, :128]))
                dus_q.append(feature_back(fq.astype(F32), dfq.astype(BF16).astype(F32)).astype(BF16))
                dus_k.append(feature_back(fk.astype(F32), dfk.astype(BF16).astype(F32)).astype(BF16))
            du_q, du_k = jnp.concatenate(dus_q, axis=1), jnp.concatenate(dus_k, axis=1)
            dq = dot_nt(du_q, maps_ref[0, g]).astype(BF16)
            dk = dot_nt(du_k, maps_ref[1, g]).astype(BF16)
            dv = jnp.concatenate([jnp.where(low, dvs[0], dvs[1]), jnp.where(low, dvs[2], 0.0)], axis=1).astype(BF16)
            gsum_ref[0] += dot_tn(qkv_ref[g, at, 0:256], du_q)
            gsum_ref[1] += dot_tn(qkv_ref[g, at, 256:512], du_k)
            dqkv = jnp.concatenate([dq, dk, dv], axis=1)
            qkv_ref[g, at] = dqkv
            return 0

        lax.fori_loop(0, chunks, piece, 0, unroll=2)
        if (X, H) == (2, 4):

            @pl.when((i == groups - 1) & (odd == 1))
            def _():
                for off in reversed(range(Z)):
                    attn.step(attn.early_sets()[1], off)

        low64 = low_half((HD, 128))
        for j in range(heads):
            sums = [gsum_ref[side, HD * j : HD * j + HD, 128 * j : 128 * j + 128] for side in range(2)]
            sums = [value - pltpu.roll(value, HD, 1) for value in sums]
            pair = jnp.where(low64, sums[0], -sums[1])
            for k in range(X * Z):
                featsum_ref[k // Z, k % Z, g, depth * j : depth * j + depth] = pair[depth * k : depth * k + depth]
        for third in range(3):
            grad = dot(normed_ref[...], qkv_ref[g, :, 256 * third : 256 * third + 256])
            at = 256 * third
            gw_ref[:, :, g, :, at : at + 128] = grad[:, 0:128].astype(BF16).reshape(shape)
            beside = gw_ref[:, :, g, :, at + 128 : at + 256].reshape(width, 128)
            gw_ref[:, :, g, :, at + 128 : at + 256] = (
                jnp.where(lowd, grad[:, 128:256], beside.astype(F32)).astype(BF16).reshape(shape)
            )
        attn.begin(lambda dp_at, h_at: h_at == g)

        if (X, H) == (2, 4):

            @pl.when(i == groups - 2)
            def _():
                for off in reversed(range(Z)):
                    attn.step(attn.early_sets()[3], off)

                @pl.when(odd == 0)
                def _():
                    for off in reversed(range(Z)):
                        attn.step(attn.early_sets()[2], off)

        return 0

    featsum_ref[...] = jnp.zeros_like(featsum_ref)
    lax.fori_loop(0, groups, group, 0)
    for k in range(X * Z):
        for g in range(groups):
            featpart_ref[k // Z, k % Z, g] = featsum_ref[k // Z, k % Z, g].astype(BF16)
    feat.begin()

    gnorm_ref[...] = gnorm_in[...]
    turns = groups * chunks
    slots = {}
    for scatter in (attn, feat):
        own, *others = scatter.early_sets()
        for off in reversed(range(Z)):
            late = (Z - 1 - off) * turns // Z
            turn = {chosen: functools.partial(scatter.step, chosen, off) for chosen in (own, *others)}
            if scatter is attn and (X, H) == (2, 4):

                def cross(turn=turn):
                    pl.when(odd == 0)(turn[others[0]])
                    pl.when(odd == 1)(turn[others[1]])

                slots.setdefault(1 + late // 4, []).append(cross)
                slots.setdefault(4 + late * 3 // 4, []).append(turn[own])
            else:
                for k, chosen in enumerate(reversed(others)):
                    slots.setdefault(1 + 4 * k if len(others) == 3 else 1, []).append(turn[chosen])
                slots.setdefault(turns - 2, []).append(turn[own])

    def through(i, _):
        slot = lax.rem(i, 2)
        pull_weight(i).wait()

        def piece(c, _):
            run_at(slots, i * chunks + c, turns)
            at = pl.ds(pl.multiple_of(c * CHUNK, CHUNK), CHUNK)
            dnormed_ref[at] += dot_nt(qkv_ref[backwards(i), at], w_ref[slot].reshape(width, width))
            return 0

        lax.fori_loop(0, chunks, piece, 0, unroll=2)

        @pl.when(i < groups - 2)
        def _():
            pull_weight(i + 2).start()

        return 0

    lax.fori_loop(0, groups, through, 0)
    pull_x(0).wait()
    pull_dmid(0).wait()

    def close(c, _):
        at = pl.ds(pl.multiple_of(c * CHUNK, CHUNK), CHUNK)
        gain_row = norm_ref[0:1].astype(BF16).astype(F32)
        back, gain, shift = norm_backward(x_ref[at].astype(F32), gain_row, dnormed_ref[at])
        dmid_ref[at] = dmid_ref[at] + back
        gnorm_ref[0:1] += gain
        gnorm_ref[1:2] += shift
        return 0

    lax.fori_loop(0, chunks, close, 0)
    push_dx(0).start()
    square = jnp.zeros((1, 128), F32)
    gfc_ref[...] = fc_along.result()
    gproj_ref[...] = proj_along.result()
    gattn_out[...] = attn_along.result()
    gfeat_out[...] = feat_along.result()
    for ref in (gattn_out, gfeat_out, gfc_ref, gproj_ref):
        column = jnp.sum(ref[...] * ref[...], axis=0, keepdims=True)
        for at in range(0, column.shape[1], 128):
            square = square + column[:, at : at + 128]
    gnorm_ref[4:5, 0:128] = square
    sums_out[...] = total_over_all(net, gnorm_ref[...], *scratch[20:])
    push_dx(0).wait()
    chain.finish(groups)
    for moving in (attn, feat, fc_along, proj_along, attn_along, feat_along):
        moving.finish()


def adamw_update(master, first_mom, second_mom, grad_in, factor, step_rate, decay_rate):
    clipped = grad_in * factor
    first_new = beta_one * first_mom + (1.0 - beta_one) * clipped
    second_new = beta_two * second_mom + (1.0 - beta_two) * clipped * clipped
    direction = (
        first_new
        / (1.0 - beta_one**STEP)
        / (jnp.sqrt(second_new / (1.0 - beta_two**STEP)) + adam_eps)
    )
    master_new = master - step_rate * (direction + decay_rate * master)
    return (master_new, first_new, second_new)


def update_kernel(heads, depth, sums_ref, gattn_ref, gfeat_ref, gfc_ref, gproj_ref, *refs):
    masters, firsts, seconds = refs[0:6], refs[6:12], refs[12:18]
    block_in, dx_in, norm_out = refs[18:21]
    outs, (block_out, dx_out), (feat_grads, block_ref, dx_ref, sems) = refs[21:46], refs[46:48], refs[48:]
    mover = Mover(sems)
    pulls = [mover.plan(block_in, block_ref)(0), mover.plan(dx_in, dx_ref)(0)]
    pushes = [mover.plan(block_ref, block_out)(0), mover.plan(dx_ref, dx_out)(0)]
    for pull in pulls:
        pull.start()
    norm_grads = sums_ref[0:4]
    squares = jnp.sum(sums_ref[4:5, 0:128], keepdims=True) + jnp.sum(norm_grads * norm_grads, keepdims=True)
    grad_norm = jnp.sqrt(squares)
    norm_out[...] = grad_norm
    factor = clip_limit / jnp.maximum(grad_norm, clip_limit)
    rates, decays = (0.02, 0.4, 0.15, 0.02, 0.01, 0.3), (0.1, 0.1, 0.1, 0.1, 0.1, 0.0)

    def update(which, at, grads):
        results = adamw_update(
            masters[which][at], firsts[which][at], seconds[which][at], grads, factor, rates[which], decays[which]
        )
        results += (results[0].astype(BF16),)
        if which < 5:
            for kind, value in enumerate(results):
                outs[6 * kind + which][at] = value
        else:
            outs[5][...], outs[11][...] = results[0], results[1]
            outs[17][...], outs[23][...] = results[2][0:2], results[2][2:4]
            outs[24][...] = results[3]

    low = low_half((1, 128))
    for j in range(heads):
        for d in range(0, depth, 2):
            row, other = (gfeat_ref[depth * j + d + k : depth * j + d + k + 1] for k in range(2))
            at = slice(64 * d, 64 * d + 128)
            feat_grads[j, 0:1, at] = jnp.where(low, row, pltpu.roll(other, HD, 1))
            feat_grads[j, 1:2, at] = jnp.where(low, pltpu.roll(row, HD, 1), other)
    for j in range(3):
        update(0, (j,), gattn_ref[:, 256 * j : 256 * j + heads * HD])
        update(1, (slice(HD * j, HD * j + HD),), gattn_ref[:, 256 * j + heads * HD : 256 * j + 256].T)
    update(2, (slice(None),), feat_grads[...])
    update(3, (slice(None),), gfc_ref[...])
    for pull, push in zip(pulls, pushes):
        pull.wait()
        push.start()
    update(4, (slice(None),), gproj_ref[...])
    update(5, (slice(None),), norm_grads)
    for push in pushes:
        push.wait()


def in_vmem(count):
    return [pl.BlockSpec(memory_space=VMEM)] * count


def struct(shape, dtype):
    return jax.ShapeDtypeStruct(shape, dtype)


def call(kernel, outs, smem, operands, scratch, collective_id, name, flops, hbm_in=0, hbm_out=(), limit=63):
    specs = [pl.BlockSpec(memory_space=pltpu.SMEM)] * smem + in_vmem(len(operands) - smem - hbm_in)
    specs += [pl.BlockSpec(memory_space=pl.ANY)] * hbm_in
    out_specs = [pl.BlockSpec(memory_space=pl.ANY if i in hbm_out else VMEM) for i in range(len(outs))]
    traffic = sum(o.size * o.dtype.itemsize for o in outs) + sum(o.size * o.dtype.itemsize for o in operands)
    extra = {} if collective_id is None else {"collective_id": collective_id, "has_side_effects": True}
    return pl.pallas_call(
        kernel,
        out_shape=tuple(outs),
        in_specs=specs,
        out_specs=tuple(out_specs),
        scratch_shapes=scratch,
        compiler_params=pltpu.CompilerParams(vmem_limit_bytes=limit * 2**20, **extra),
        cost_estimate=pl.CostEstimate(flops=flops, bytes_accessed=traffic, transcendentals=0),
        name=name,
    )(*operands)


def on_device(
    sizes,
    block_in,
    cotangent,
    seq_len,
    w_qkv,
    w_out,
    w_feat,
    w_fc,
    w_proj,
    norm_params,
    first_qkv,
    second_qkv,
    first_out,
    second_out,
    first_feat,
    second_feat,
    first_fc,
    second_fc,
    first_proj,
    second_proj,
    first_norms,
    second_norms,
):
    X, Z, H = sizes
    rows, width = block_in.shape
    part, _, head_width = w_qkv.shape
    heads = w_feat.shape[1]
    depth = w_feat.shape[2] // HD
    chunks = rows // CHUNK

    big = (X, Z, H, part, width)
    small = (X, Z, H, FEAT_ROWS, 2 * HD)
    dma = pltpu.SemaphoreType.DMA
    chain_scratch = [
        VMEM((H, heads, 128, 128), F32),
        VMEM((H, heads, 128, 128), BF16),
        VMEM((H, heads, 128, 128), BF16),
        dma((H,)),
        dma((H,)),
    ]
    turned = struct((width, rows), BF16)
    held = [
        struct((rows, width), BF16),
        struct((H, rows, width), BF16),
        struct((H, rows, 128 * heads), BF16),
        struct((H, rows, 128 * heads), BF16),
        struct((H, heads, chunks, 128, 256), BF16),
        struct((H, rows, 256), BF16),
        struct((H, rows, 256), BF16),
        struct((H, width, 256), BF16),
        struct((2, H, 256, 128 * heads), BF16),
        struct((rows, width), F32),
        struct((rows, width), BF16),
    ]
    normed, qkv, fq, fk, states, mixed, rden, wo, maps, middle, hidden, attn_w, fc_w, proj_w = call(
        functools.partial(attention_forward, sizes, heads, depth),
        [turned] + held[1:] + [struct(big, BF16)] * 3,
        1,
        [seq_len, block_in, w_qkv.transpose(1, 0, 2), w_out, w_feat.transpose(1, 0, 2), w_fc.T, w_proj, norm_params],
        [VMEM(item.shape, item.dtype) for item in held]
        + [
            VMEM(turned.shape, BF16),
            VMEM((part, width), BF16),
            VMEM((FEAT_ROWS, 128), BF16),
            VMEM((part, width), BF16),
            VMEM((part, width), BF16),
            VMEM((FEAT_ROWS, 128), F32),
            VMEM((4, width), F32),
        ]
        + [VMEM(big, BF16), VMEM(big, BF16), VMEM(big, BF16), VMEM(small, BF16), VMEM((H * heads, HD, 128), F32), VMEM((heads, 128, 256), F32)]
        + chain_scratch
        + [dma((8 + 6 * H,))]
        + [sem for _ in range(5) for sem in gather_sems(sizes)],
        0,
        "attention_forward",
        10**10,
        hbm_out=range(14),
    )

    turns = 4 if (X, H) == (2, 4) else X
    size = X * Z * H * part // turns
    block_out, d_middle, d_att, d_att_t, fc_sums, proj_sums, g_norm = call(
        functools.partial(feed_forward, sizes),
        [
            struct((rows, width), BF16),
            struct((rows, width), F32),
            struct((rows, width), BF16),
            turned,
            struct((Z, part, width), BF16),
            struct((Z, part, width), BF16),
            struct((8, width), F32),
        ],
        0,
        [hidden, cotangent, norm_params, fc_w, proj_w, middle],
        [
            VMEM((turns, size, width), BF16),
            VMEM((turns, size, width), BF16),
            VMEM((rows, width), F32),
            VMEM((rows, width), BF16),
            VMEM((rows, width), BF16),
            VMEM(turned.shape, BF16),
            VMEM(big, BF16),
            VMEM(big, BF16),
            VMEM((rows, width), F32),
            VMEM((rows, width), F32),
            VMEM((rows, size), BF16),
            VMEM((rows, size), BF16),
            dma((5,)),
            dma((turns, size // part)),
            dma((turns, size // part)),
        ]
        + scatter_scratch(sizes, (part, width)) * 2,
        1,
        "feed_forward",
        3 * 10**10,
        hbm_in=3,
        hbm_out=range(4),
    )

    pulled = [struct((rows, width), BF16), turned] + held[1:9] + [struct((rows, width), BF16), turned, struct((rows, width), F32)]
    block_in_grad, g_attn, g_feat, g_fc, g_proj, sums = call(
        functools.partial(attention_backward, sizes, heads, depth),
        [
            struct((rows, width), F32),
            struct((part, width), F32),
            struct((FEAT_ROWS, 128), F32),
            struct((part, width), F32),
            struct((part, width), F32),
            struct((8, width), F32),
        ],
        1,
        [
            seq_len, norm_params, g_norm, fc_sums, proj_sums, block_in, normed, qkv, fq, fk, states, mixed, rden, wo, maps,
            attn_w, d_att, d_att_t, d_middle,
        ],
        [VMEM(item.shape, item.dtype) for item in pulled]
        + [
            VMEM((2, X, Z, part, width), BF16),
            VMEM(big, BF16),
            VMEM((8, width), F32),
            VMEM(small, F32),
            VMEM(small, BF16),
            VMEM((H, heads, rows, 128), BF16),
            VMEM((H, heads, chunks, 128, 256), BF16),
            VMEM((heads, 128, 256), F32),
            chain_scratch[0],
            VMEM((rows, width), F32),
            VMEM((2, 256, 128 * heads), F32),
        ]
        + chain_scratch[1:]
        + [dma((2,)), dma((7 + 7 * H,))]
        + along_scratch(sizes, (part, width)) * 2
        + [VMEM((Z, part, width), BF16)]
        + along_scratch(sizes, (part, width))
        + [VMEM((Z, FEAT_ROWS, 128), BF16)]
        + along_scratch(sizes, (FEAT_ROWS, 128))
        + scatter_scratch(sizes, (part, width))
        + scatter_scratch(sizes, (FEAT_ROWS, 128))
        + total_scratch(sizes, (8, width)),
        2,
        "attention_backward",
        2 * 10**10,
        hbm_in=14,
        hbm_out=(0,),
    )

    def turned(qkv, out, feat, fc, proj, *norms):
        return [qkv.transpose(1, 0, 2), out, feat.transpose(1, 0, 2), fc.T, proj, *norms]

    masters = turned(w_qkv, w_out, w_feat, w_fc, w_proj, norm_params)
    firsts = turned(first_qkv, first_out, first_feat, first_fc, first_proj, first_norms)
    seconds = turned(second_qkv, second_out, second_feat, second_fc, second_proj, second_norms)
    shapes = [item.shape for item in masters]
    halves = (2, width)
    norm_filled, *updated, block_out, block_in_grad = call(
        functools.partial(update_kernel, heads, depth),
        [struct((1, 1), F32)]
        + [struct(shape, F32) for shape in shapes * 2 + shapes[:5] + [halves]]
        + [struct(shape, BF16) for shape in shapes[:5]]
        + [struct(halves, F32), struct(shapes[5], BF16)]
        + [struct((rows, width), BF16), struct((rows, width), F32)],
        0,
        [sums, g_attn, g_feat, g_fc, g_proj] + masters + firsts + seconds + [block_out, block_in_grad],
        [VMEM(shapes[2], F32), VMEM((rows, width), BF16), VMEM((rows, width), F32), dma((4,))],
        None,
        "update",
        10**7,
        hbm_in=2,
        hbm_out=(26, 27),
    )
    new, new_first, new_second = (turned(*updated[6 * kind : 6 * kind + 6]) for kind in range(3))
    copies = turned(*updated[18:23], updated[24])
    return (
        norm_filled.reshape(()),
        block_out,
        block_in_grad,
        *new,
        *new_first,
        *new_second[:5],
        new_second[5],
        updated[23],
        *copies,
    )


def solution(mesh):
    everything = ("dp", "batch", "head")
    rows = P(everything, None)
    qkv, out, feat = P(("dp", "batch"), None, "head"), P("head", ("dp", "batch")), P(None, "head", ("dp", "batch"))
    fc, proj, whole = P(None, everything), P(everything, None), P()
    weights = (qkv, out, feat, fc, proj, whole)
    in_specs = (rows, rows, P(("dp", "batch"), None)) + weights
    for spec in weights:
        in_specs += (spec, spec)
    out_specs = (whole, rows, rows) + weights + weights + weights[:5] + (whole, whole) + weights
    sizes = (mesh.shape["dp"], mesh.shape["batch"], mesh.shape["head"])
    return jax.shard_map(
        functools.partial(on_device, sizes), mesh=mesh, in_specs=in_specs, out_specs=out_specs, check_vma=False
    )
```

```python
import functools

import jax
import jax.numpy as jnp
from jax import lax
from jax.experimental import pallas as pl
from jax.experimental.pallas import tpu as pltpu
from jax.sharding import PartitionSpec as P

HD = 64
STEP = 8
CHUNK = 256
FEAT_ROWS = 32
FC_TURNS = (0, 4, 8, 12, 16)
PROJ_BEGIN = 0
PROJ_TURNS = (2, 6, 10, 14, 18)
MESH = pl.DeviceIdType.MESH
VMEM = pltpu.VMEM
F32 = jnp.float32
BF16 = jnp.bfloat16

norm_eps = 1e-05
beta_one = 0.9
beta_two = 0.95
adam_eps = 1e-08
clip_limit = 1.0


def dot(left, right):
    return lax.dot_general(left, right, (((1,), (0,)), ((), ())), preferred_element_type=F32)


def dot_nt(left, right):
    return lax.dot_general(left, right, (((1,), (1,)), ((), ())), preferred_element_type=F32)


def dot_tn(left, right):
    return lax.dot_general(left, right, (((0,), (0,)), ((), ())), preferred_element_type=F32)


def flip_bit(value, bit, on=1):
    low = 2**bit
    return value + on * (low - 2 * low * lax.rem(value // low, 2))


class Network:
    def __init__(self, sizes, swap=0):
        self.X, self.Z, self.H = sizes
        self.dp, self.b, self.h = (lax.axis_index(name) for name in ("dp", "batch", "head"))
        dp_bits, head_bits = self.X.bit_length() - 1, self.H.bit_length() - 1
        if (self.X, self.H) == (2, 4):
            self.odd = lax.rem(self.h + swap, 2)

            def first(dp, h):
                odd = lax.rem(h + swap, 2)
                return flip_bit(dp, 0, 1 - odd), flip_bit(h, 1, odd)

            def second(dp, h):
                odd = lax.rem(h + swap, 2)
                return flip_bit(dp, 0, odd), flip_bit(h, 1, 1 - odd)

            self.flips = [first, second, lambda dp, h: (dp, flip_bit(h, 0))]
        else:
            self.flips = [lambda dp, h, k=k: (flip_bit(dp, k), h) for k in range(dp_bits)]
            self.flips += [lambda dp, h, k=k: (dp, flip_bit(h, k)) for k in reversed(range(head_bits))]
        self.sets = [()]
        for k in range(len(self.flips)):
            self.sets += [s + (k,) for s in self.sets]
        self.index = {s: i for i, s in enumerate(self.sets)}

    def coord(self, chosen):
        dp, h = self.dp, self.h
        for k in sorted(chosen, reverse=True):
            dp, h = self.flips[k](dp, h)
        return dp, h

    def behind(self, off):
        return lax.rem(self.b + self.Z - off, self.Z)

    def ahead(self, off):
        return lax.rem(self.b + off, self.Z)

    def slot(self, chosen, off):
        dp, h = self.coord(chosen)
        return dp, self.behind(off), h

    def partner(self, k):
        dp, h = self.flips[k](self.dp, self.h)
        return {"dp": dp, "batch": self.b, "head": h}

    def along(self, b):
        return {"dp": self.dp, "batch": b, "head": self.h}

    def stages(self, chosen):
        return range(max(chosen) + 1 if chosen else 0, len(self.flips))

    def plane(self):
        count = self.X * self.H
        mine = self.dp * self.H + self.h
        for step in range(1, count):
            other = lax.rem(mine + step, count)
            yield step, {"dp": other // self.H, "batch": self.b, "head": lax.rem(other, self.H)}

    def barrier(self, chained=False, whole_plane=False):
        pl.semaphore_wait(pltpu.get_barrier_semaphore(), self.greet(chained, whole_plane))

    def greet(self, chained=False, whole_plane=False):
        sem = pltpu.get_barrier_semaphore()
        devices = [self.along(self.ahead(off)) for off in range(1, self.Z)]
        if whole_plane:
            devices += [device for _, device in self.plane()]
        else:
            devices += [self.partner(k) for k in range(len(self.flips))]
            if chained:
                devices += [{"head": lax.rem(self.h + step, self.H)} for step in (1, self.H - 1)]
        for device in devices:
            pl.semaphore_signal(sem, inc=1, device_id=device, device_id_type=MESH)
        return len(devices)


def gather_sems(sizes):
    X, Z, H = sizes
    return [pltpu.SemaphoreType.DMA((X * H + 1, Z)), pltpu.SemaphoreType.DMA((X * H, Z))]


class Gather:
    def __init__(self, net, shard, buf, send, recv, rows=None):
        self.net, self.send, self.recv = net, send, recv
        self.rows = pl.ds(0, shard.shape[0]) if rows is None else rows
        self.shard, self.buf = shard.at[self.rows], buf
        self.inner = (net.b == 1) | (net.b == 2)
        self.ends = send.shape[0] - 1

    def near(self, t):
        b = self.net.b
        return (b, flip_bit(b, 0), 2 - b // 2, 3 - 3 * (b // 2))[t]

    def slot(self, chosen, t):
        dp, h = self.net.coord(chosen)
        return dp, self.near(t), h, self.rows

    def source(self, chosen, t):
        return self.shard if chosen == () and t == 0 else self.buf.at[self.slot(chosen, t)]

    def copy(self, chosen, t, k):
        net = self.net
        into = net.index[chosen + (k,)]
        return pltpu.make_async_remote_copy(
            src_ref=self.source(chosen, t), dst_ref=self.buf.at[self.slot(chosen, t)],
            send_sem=self.send.at[into, t], recv_sem=self.recv.at[into, t],
            device_id=net.partner(k), device_id_type=MESH,
        )

    def hop(self, t, outward, arrives, send_sem):
        net = self.net
        return pltpu.make_async_remote_copy(
            src_ref=self.source((), t), dst_ref=self.buf.at[self.slot((), t)],
            send_sem=send_sem, recv_sem=self.recv.at[0, arrives],
            device_id=net.along(flip_bit(net.b, 0) if outward else 3 - net.b), device_id_type=MESH,
        )

    def pair_hop(self):
        return self.hop(0, True, 1, self.send.at[self.ends, 0])

    def inner_hops(self, t):
        ends = self.send.at[self.ends, 1]
        return self.hop(t, t > 1, (2, 3, 2, 3)[t], self.send.at[0, t] if t else ends)

    def copy_own(self):
        return pltpu.make_async_copy(self.shard, self.buf.at[self.slot((), 0)], self.send.at[self.ends, 2])

    def arrived(self, chosen, t):
        net = self.net
        place = self.buf.at[self.slot(chosen, t)]
        into = net.index[chosen]
        pltpu.make_async_remote_copy(
            src_ref=place, dst_ref=place, send_sem=self.send.at[into, t], recv_sem=self.recv.at[into, t],
            device_id=net.partner(0), device_id_type=MESH,
        ).wait_recv()

    def begin(self):
        self.pair_hop().start()
        pl.when(self.inner)(lambda: self.inner_hops(0).start())
        for k in self.net.stages(()):
            self.copy((), 0, k).start()
        self.copy_own().start()

    def step(self, chosen, t):
        self.arrived(chosen, t)
        if chosen == ():
            pl.when(self.inner)(lambda: self.inner_hops(t).start())
        for k in self.net.stages(chosen):
            self.copy(chosen, t, k).start()

    def steps(self):
        net = self.net
        early = net.sets[: len(net.sets) // 2]
        rounds = [[] for _ in range(net.Z + max(len(chosen) for chosen in early))]
        for t in range(net.Z):
            for chosen in early:
                if chosen or t:
                    rounds[t + len(chosen)].append(functools.partial(self.step, chosen, t))
        late = [functools.partial(self.step, chosen, t) for chosen in net.sets[len(early) :] for t in range(net.Z)]
        return rounds[1:], late

    def layers(self):
        early = self.net.sets[: len(self.net.sets) // 2]
        found = [[[] for _ in range(self.net.Z)] for _ in range(1 + max(len(chosen) for chosen in early))]
        for t in range(self.net.Z):
            for chosen in early:
                if chosen or t:
                    found[len(chosen)][t].append(functools.partial(self.step, chosen, t))
        return found

    def finish(self):
        net = self.net
        self.pair_hop().wait_send()

        @pl.when(self.inner)
        def _():
            for t in range(net.Z):
                self.inner_hops(t).wait_send()

        for chosen in net.sets:
            for k in net.stages(chosen):
                for t in range(net.Z):
                    self.copy(chosen, t, k).wait_send()


def scatter_scratch(sizes, shape):
    X, Z, H = sizes
    n = X * H
    return [VMEM((n, Z) + shape, BF16), pltpu.SemaphoreType.DMA((n, Z)), pltpu.SemaphoreType.DMA((n, Z))]


class Scatter:
    def __init__(self, net, along, part, inbox, send, recv):
        self.net, self.along, self.part, self.inbox, self.send, self.recv = net, along, part, inbox, send, recv
        self.last = len(net.flips) - 1

    def sum_at(self, chosen, off):
        return self.inbox.at[self.net.index[chosen + (self.last,)], off]

    def copy(self, chosen, off, k):
        net = self.net
        into = net.index[chosen + (k,)]
        first = k == self.last
        source = self.part.at[net.slot(chosen + (k,), off)] if first else self.sum_at(chosen + (k,), off)
        return pltpu.make_async_remote_copy(
            src_ref=source, dst_ref=self.inbox.at[into, off], send_sem=self.send.at[into, off],
            recv_sem=self.recv.at[into, off], device_id=net.partner(k), device_id_type=MESH,
        )

    def early_sets(self):
        return self.net.sets[: len(self.net.sets) // 2]

    def begin(self, ready=None, offs=None):
        for chosen in reversed(self.early_sets()):

            def start(chosen=chosen):
                for off in range(self.net.Z) if offs is None else offs:
                    self.copy(chosen, off, self.last).start()

            if ready is None:
                start()
            else:
                pl.when(ready(*self.net.coord(chosen + (self.last,))))(start)

    def step(self, chosen, off):
        net = self.net
        total = self.part[net.slot(chosen, off)].astype(F32)
        for k in reversed(net.stages(chosen)):
            self.copy(chosen, off, k).wait_recv()
            total = total + self.inbox[net.index[chosen + (k,)], off].astype(F32)
        if chosen:
            self.sum_at(chosen, off)[...] = total.astype(BF16)
            self.copy(chosen[:-1], off, chosen[-1]).start()
        else:
            self.along.give(off, total.astype(BF16))

    def finish(self):
        net = self.net
        for chosen in net.sets:
            for k in net.stages(chosen):
                for off in range(net.Z):
                    self.copy(chosen, off, k).wait_send()


def along_scratch(sizes, shape):
    X, Z, H = sizes
    return [VMEM((Z,) + shape, BF16), pltpu.SemaphoreType.DMA((Z,)), pltpu.SemaphoreType.DMA((Z,))]


class Along:
    def __init__(self, net, sums, inbox, send, recv):
        self.net, self.sums, self.inbox, self.send, self.recv = net, sums, inbox, send, recv

    def copy(self, off):
        net = self.net
        return pltpu.make_async_remote_copy(
            src_ref=self.sums.at[off], dst_ref=self.inbox.at[off], send_sem=self.send.at[off],
            recv_sem=self.recv.at[off], device_id=net.along(net.behind(off)), device_id_type=MESH,
        )

    def give(self, off, value):
        self.sums[off] = value
        if off:
            self.copy(off).start()

    def result(self):
        total = self.sums[0].astype(F32)
        for off in range(1, self.net.Z):
            self.copy(off).wait_recv()
            total = total + self.inbox[off].astype(F32)
        return total

    def finish(self):
        for off in range(1, self.net.Z):
            self.copy(off).wait_send()


class Keep:
    def __init__(self, sums):
        self.sums = sums

    def give(self, off, value):
        self.sums[off] = value


def total_scratch(sizes, shape):
    X, Z, H = sizes
    count = X * H
    return [
        VMEM((count + Z,) + shape, F32),
        pltpu.SemaphoreType.DMA((count + Z,)),
        pltpu.SemaphoreType.DMA((count + Z,)),
    ]


def total_over_all(net, value, slots, send, recv):
    count, Z = net.X * net.H, net.Z

    def exchange(value, base, mine, size, devices):
        slots[base + mine] = value
        for step, device in devices:
            place = slots.at[base + mine]
            pltpu.make_async_remote_copy(
                src_ref=place, dst_ref=place, send_sem=send.at[base + step], recv_sem=recv.at[base + step],
                device_id=device, device_id_type=MESH,
            ).start()
        for step, device in devices:
            place = slots.at[base + lax.rem(mine + size - step, size)]
            copy = pltpu.make_async_remote_copy(
                src_ref=place, dst_ref=place, send_sem=send.at[base + step], recv_sem=recv.at[base + step],
                device_id=device, device_id_type=MESH,
            )
            copy.wait_recv()
            copy.wait_send()
        total = slots[base]
        for i in range(1, size):
            total = total + slots[base + i]
        return total

    value = exchange(value, 0, net.dp * net.H + net.h, count, list(net.plane()))
    return exchange(value, count, net.b, Z, [(off, net.along(net.ahead(off))) for off in range(1, Z)])


class Mover:
    def __init__(self, sems):
        self.sems, self.used = sems, 0

    def plan(self, source, target, count=None):
        at = self.used
        self.used += 1 if count is None else count

        def make(i):
            if count is None:
                return pltpu.make_async_copy(source, target, self.sems.at[at])
            return pltpu.make_async_copy(source.at[i], target.at[i], self.sems.at[at + i])

        return make


def norm_stats(values):
    mean = jnp.mean(values, axis=-1, keepdims=True)
    center = values - mean
    spread = jnp.mean(center * center, axis=-1, keepdims=True)
    return center, lax.rsqrt(spread + norm_eps)


def norm_backward(values, gain_row, grads):
    center, scale = norm_stats(values)
    normal = center * scale
    inner = grads * gain_row
    part = jnp.mean(inner * normal, axis=-1, keepdims=True)
    back = scale * (inner - jnp.mean(inner, axis=-1, keepdims=True) - normal * part)
    return back, jnp.sum(grads * normal, axis=0, keepdims=True), jnp.sum(grads, axis=0, keepdims=True)


def low_half(shape):
    return lax.rem(lax.broadcasted_iota(jnp.int32, shape, len(shape) - 1), 128) < HD


def swap_halves(values):
    cols = values.shape[1]
    parts = [pltpu.roll(values[:, at : at + 128], HD, 1) for at in range(0, cols, 128)]
    return parts[0] if len(parts) == 1 else jnp.concatenate(parts, axis=1)


def half_ones():
    down = lax.broadcasted_iota(jnp.int32, (128, 128), 0) // HD
    across = lax.broadcasted_iota(jnp.int32, (128, 128), 1) // HD
    return (down == across).astype(BF16)


def feature_pair(scaled, live):
    low = low_half(scaled.shape)
    top = jnp.max(jnp.where(low, scaled, -jnp.inf), axis=-1, keepdims=True)
    bottom = jnp.max(jnp.where(low, -jnp.inf, scaled), axis=-1, keepdims=True)
    powers = jnp.exp(scaled - jnp.where(low, top, bottom))
    sums = dot(powers.astype(BF16), half_ones())
    return powers * (live / sums)


def feature_back(feature, grads):
    product = feature * grads
    return product - feature * dot(product.astype(BF16), half_ones())


class Rows:
    def __init__(self, len_ref, rows, h):
        self.first_len = len_ref[0, 0]
        self.both_len = len_ref[0, 0] + len_ref[0, 1]
        self.start = h * rows
        self.rows = rows

    def second(self, row):
        return row >= self.first_len

    def column(self, chunk):
        return self.start + chunk * CHUNK + lax.broadcasted_iota(jnp.int32, (CHUNK, 1), 0)

    def live(self, chunk):
        return (self.column(chunk) < self.both_len).astype(F32)

    def second_column(self, chunk):
        return self.second(self.column(chunk))

    def masks(self, chunk):
        base = self.start + chunk * CHUNK
        down = base + lax.broadcasted_iota(jnp.int32, (CHUNK, CHUNK), 0)
        across = base + lax.broadcasted_iota(jnp.int32, (CHUNK, CHUNK), 1)
        same = (down >= self.first_len) == (across >= self.first_len)
        return same & (across <= down), same & (across >= down)

    def scalar(self, row):
        return jnp.where(self.second(row), 1.0, 0.0).astype(F32)

    def before(self):
        return self.scalar(self.start - 1)

    def first(self):
        return self.scalar(self.start)

    def last(self):
        return self.scalar(self.start + self.rows - 1)

    def after(self):
        return self.scalar(self.start + self.rows)


def with_ones(block, head, low):
    ones = jnp.ones_like(block)
    return jnp.where(low, block, ones) if head % 2 == 0 else jnp.where(low, ones, block)


def by_sequence(values, second):
    zero = jnp.zeros_like(values)
    return jnp.concatenate([jnp.where(second, zero, values), jnp.where(second, values, zero)], axis=1)


class Chain:
    def __init__(self, step, n, h, same, picked, cin, cout, send, recv):
        self.first = h == (0 if step == 1 else n - 1)
        self.final = h == (n - 1 if step == 1 else 0)
        self.neighbour = {"head": lax.rem(h + n + step, n)}
        self.same, self.picked, self.cin, self.cout, self.send, self.recv = same, picked, cin, cout, send, recv

    def copy(self, g):
        return pltpu.make_async_remote_copy(
            src_ref=self.cout.at[g], dst_ref=self.cin.at[g], send_sem=self.send.at[g], recv_sem=self.recv.at[g],
            device_id=self.neighbour, device_id_type=MESH,
        )

    def step(self, g):
        @pl.when(self.first)
        def _():
            self.cin[g] = jnp.zeros_like(self.cin[g])

        @pl.when(jnp.logical_not(self.first))
        def _():
            self.copy(g).wait_recv()

        @pl.when(jnp.logical_not(self.final))
        def _():
            self.cout[g] = (self.picked[g] + self.cin[g].astype(F32) * self.same).astype(BF16)
            self.copy(g).start()

    def finish(self, n):
        @pl.when(jnp.logical_not(self.final))
        def _():
            for g in range(n):
                self.copy(g).wait_send()


def group_at(h, i, n):
    bits = n.bit_length() - 1
    for k in range(bits):
        h = flip_bit(h, bits - 1 - k, lax.rem(i // 2**k, 2))
    return h


def run_at(slots, i, count):
    for k in range(count):
        if slots.get(k):

            @pl.when(i == k)
            def _(items=slots[k]):
                for item in items:
                    item()


def rest_of(slots, count):
    for k in sorted(slots):
        if k >= count:
            for item in slots[k]:
                item()


def equal(a, b):
    return a * b + (1.0 - a) * (1.0 - b)


def attention_forward(
    sizes, heads, depth, len_ref, x_ref, wqkv_ref, wout_ref, wfeat_ref, wfc_ref, wproj_ref, norm_in,
    normed_out, qkv_out, fq_out, fk_out, state_out, mixed_out, rden_out, wo_out, maps_out, middle_out, hidden_out,
    attn_out, fc_out, proj_out,
    normed_ref, qkv_ref, fq_ref, fk_ref, state_ref, mixed_ref, rden_ref, wo_ref, maps_ref, middle_ref, hidden_ref,
    turned_ref, attn_shard, feat_shard, fc_shard, proj_shard, feat_rows, norm_ref,
    w_ref, fc_ref, proj_ref, feat_ref, pairs_ref, total_ref, picked_ref, cin, cout, chain_send, chain_recv, move_sem,
    *sems,
):
    X, Z, groups = sizes
    net = Network(sizes)
    greeted = net.greet(chained=True)
    lanes_here = heads * HD
    for j in range(3):
        attn_shard[:, 256 * j : 256 * j + 128] = wqkv_ref[j, :, 0:128].astype(BF16)
        attn_shard[:, 256 * j + 128 : 256 * j + 256] = jnp.concatenate(
            [wqkv_ref[j, :, 128:lanes_here], wout_ref[HD * j : HD * j + HD].T], axis=1
        ).astype(BF16)
    feat_rows[...] = jnp.zeros_like(feat_rows)
    low_row = low_half((1, 128))
    for j in range(heads):
        for d in range(depth):
            q, k = (wfeat_ref[j, side : side + 1, 128 * (d // 2) : 128 * (d // 2) + 128] for side in range(2))
            row = jnp.where(low_row, q, pltpu.roll(k, HD, 1)) if d % 2 == 0 else jnp.where(low_row, pltpu.roll(q, HD, 1), k)
            feat_rows[depth * j + d : depth * j + d + 1] = row
    feat_shard[...] = feat_rows[...].astype(BF16)
    fc_shard[...] = wfc_ref[...].astype(BF16)
    proj_shard[...] = wproj_ref[...].astype(BF16)
    norm_ref[...] = norm_in[...].astype(BF16).astype(F32)
    h = net.h
    rows, width = x_ref.shape
    chunks = rows // CHUNK
    seq = Rows(len_ref, rows, h)
    low = low_half((CHUNK, 128))
    mover = Mover(move_sem)
    push_normed, push_wo, push_maps, push_attn = (
        mover.plan(*pair)
        for pair in ((turned_ref, normed_out), (wo_ref, wo_out), (maps_ref, maps_out), (w_ref, attn_out))
    )
    push_qkv, push_fq, push_fk, push_state, push_mixed, push_rden = (
        mover.plan(*pair, groups)
        for pair in (
            (qkv_ref, qkv_out), (fq_ref, fq_out), (fk_ref, fk_out), (state_ref, state_out), (mixed_ref, mixed_out),
            (rden_ref, rden_out),
        )
    )
    push_middle, push_hidden = mover.plan(middle_ref, middle_out), mover.plan(hidden_ref, hidden_out)
    push_fc, push_proj = mover.plan(fc_ref, fc_out), mover.plan(proj_ref, proj_out)

    pl.semaphore_wait(pltpu.get_barrier_semaphore(), greeted)
    part = attn_shard.shape[0]
    cuts = [pl.ds(0, part // 2), pl.ds(part // 2, part // 2)] if part % 32 == 0 else [pl.ds(0, part)]
    feat = Gather(net, feat_shard, feat_ref, *sems[0:2])
    nets = net, Network(sizes, 1)
    fc, proj = Gather(nets[0], fc_shard, fc_ref, *sems[2:4]), Gather(nets[1], proj_shard, proj_ref, *sems[4:6])
    attns = [Gather(nets[i], attn_shard, w_ref, *sems[6 + 2 * i : 8 + 2 * i], rows) for i, rows in enumerate(cuts)]
    feat.begin()
    for attn in attns:
        attn.begin()

    def first_norm(c, _):
        at = pl.ds(pl.multiple_of(c * CHUNK, CHUNK), CHUNK)
        center, scale = norm_stats(x_ref[at].astype(F32))
        normed_ref[at] = (center * scale * norm_ref[0:1] + norm_ref[1:2]).astype(BF16)
        return 0

    for gather in (feat, *attns):
        gather.copy_own().wait()
    feat_on, feat_in = feat.steps()
    attn_rounds, attn_arrivals = zip(*(attn.steps() for attn in attns))
    attn_on = [sum(steps, []) for steps in zip(*attn_rounds)]
    attn_in = sum(attn_arrivals, [])
    lax.fori_loop(0, chunks, first_norm, 0)
    ahead = len(attn_on) - (1 if (X, groups) == (2, 4) else 0)
    for k in range(ahead):
        for step in feat_on[k] + attn_on[k]:
            step()
        if k == Z - 2:
            fc.begin()
        if k == len(feat_on) - 2:
            for step in feat_on[-1] + feat_in:
                step()
            maps_ref[...] = jnp.zeros_like(maps_ref)
            low64 = low_half((HD, 128))
            for i in range(X * Z):
                for g in range(groups):
                    block = feat_ref[i // Z, i % Z, g].astype(F32)
                    for j in range(heads):
                        pairs_ref[g * heads + j, depth * i : depth * i + depth] = block[depth * j : depth * j + depth]
            for g in range(groups):
                for j in range(heads):
                    pair = pairs_ref[g * heads + j]
                    swapped = pltpu.roll(pair, HD, 1)
                    at = slice(HD * j, HD * j + HD), slice(128 * j, 128 * j + 128)
                    maps_ref[0, g, at[0], at[1]] = jnp.where(low64, pair, -swapped).astype(BF16)
                    maps_ref[1, g, at[0], at[1]] = jnp.where(low64, swapped, -pair).astype(BF16)
            push_maps(0).start()

    turns = groups * chunks
    slots = {}
    if ahead < len(attn_on):
        slots[2] = list(attn_on[ahead])
        slots[2 * chunks] = list(attn_in)
    else:
        slots[0] = list(attn_in)
    fc_on, fc_in = fc.steps()
    proj_on, proj_in = proj.steps()
    slots.setdefault(PROJ_BEGIN, []).append(proj.begin)
    for on, turns_at in ((fc_on, FC_TURNS), (proj_on, PROJ_TURNS)):
        for k, steps in enumerate(on):
            slots.setdefault(turns_at[min(k, len(turns_at) - 1)], []).extend(steps)
    mix_slots = {k - turns: items for k, items in slots.items() if k >= turns}
    last = seq.last()

    def project(i, _):
        g = group_at(h, i, groups)
        for j in range(heads):
            total_ref[j] = jnp.zeros_like(total_ref[j])

        def part(c, _):
            run_at(slots, i * chunks + c, turns)
            at = pl.ds(pl.multiple_of(c * CHUNK, CHUNK), CHUNK)
            live, second = seq.live(c), seq.second_column(c)
            qkv = dot(normed_ref[at], w_ref[:, :, g].reshape(width, width)).astype(BF16)
            qkv_ref[g, at] = qkv
            scaled_q = dot(qkv[:, 0:256], maps_ref[0, g])
            scaled_k = dot(qkv[:, 256:512], maps_ref[1, g])
            for j in range(heads):
                lanes = slice(128 * j, 128 * j + 128)
                fq_ref[g, at, lanes] = feature_pair(scaled_q[:, lanes], live).astype(BF16)
                fk = feature_pair(scaled_k[:, lanes], live).astype(BF16)
                fk_ref[g, at, lanes] = fk
                block = qkv[:, 512 + 128 * (j // 2) : 640 + 128 * (j // 2)]
                values = by_sequence(with_ones(block, j, low), second)
                state_ref[g, j, c] = total_ref[j].astype(BF16)
                total_ref[j] += dot_tn(fk, values)
            return 0

        lax.fori_loop(0, chunks, part, 0, unroll=2)
        for push in (push_qkv, push_fq, push_fk):
            push(g).start()
        for j in range(heads):
            picked_ref[g, j] = total_ref[j, :, :128] * (1.0 - last) + total_ref[j, :, 128:] * last
        weight = w_ref[:, :, g].reshape(width, width)
        lowd = low_half((width, 128))
        a = swap_halves(weight[:, 128:256].astype(F32))
        b = weight[:, 384:512].astype(F32)
        c_ = swap_halves(weight[:, 640:768].astype(F32))
        wo_ref[g, :, 0:128] = jnp.where(lowd, a, b).astype(BF16)
        wo_ref[g, :, 128:256] = jnp.where(lowd, c_, 0.0).astype(BF16)
        return 0

    lax.fori_loop(0, groups, project, 0)
    push_wo(0).start()
    push_attn(0).start()

    before = seq.before()
    chain = Chain(1, groups, h, equal(before, last), picked_ref, cin, cout, chain_send, chain_recv)

    def mix(g, _):
        chain.step(g)

        def part(c, _):
            run_at(mix_slots, g * chunks + c, turns)
            at = pl.ds(pl.multiple_of(c * CHUNK, CHUNK), CHUNK)
            live, second = seq.live(c), seq.second_column(c)
            lower, _ = seq.masks(c)
            found = []
            for j in range(heads):
                lanes = slice(128 * j, 128 * j + 128)
                fq, fk = fq_ref[g, at, lanes], fk_ref[g, at, lanes]
                carry = cin[g, j].astype(F32)
                prior = jnp.concatenate([carry * (1.0 - before), carry * before], axis=1)
                state = (state_ref[g, j, c].astype(F32) + prior).astype(BF16)
                state_ref[g, j, c] = state
                scores = jnp.where(lower, dot_nt(fq, fk), 0.0).astype(BF16)
                block = qkv_ref[g, at, 512 + 128 * (j // 2) : 640 + 128 * (j // 2)]
                inter = dot(fq, state)
                found.append(
                    dot(scores, with_ones(block, j, low)) + jnp.where(second, inter[:, 128:], inter[:, :128])
                )
            pair = jnp.where(low, found[0], found[1])
            rden = 1.0 / (swap_halves(jnp.where(low, found[1], found[0])) + (1.0 - live))
            mixed_ref[g, at, 0:128] = (pair * rden).astype(BF16)
            rden_ref[g, at, 0:128] = rden.astype(BF16)
            rden = jnp.where(low, 1.0 / (swap_halves(found[2]) + (1.0 - live)), 1.0)
            mixed_ref[g, at, 128:256] = jnp.where(low, found[2] * rden, 0.0).astype(BF16)
            rden_ref[g, at, 128:256] = rden.astype(BF16)
            return 0

        lax.fori_loop(0, chunks, part, 0, unroll=2)
        for push in (push_state, push_mixed, push_rden):
            push(g).start()
        return 0

    lax.fori_loop(0, groups, mix, 0)
    rest_of(mix_slots, turns)

    def close(c, _):
        at = pl.ds(pl.multiple_of(c * CHUNK, CHUNK), CHUNK)
        attended = dot_nt(mixed_ref[0, at], wo_ref[0])
        for g in range(1, groups):
            attended = attended + dot_nt(mixed_ref[g, at], wo_ref[g])
        middle = x_ref[at].astype(F32) + attended
        middle_ref[at] = middle
        center, scale = norm_stats(middle)
        hidden_ref[at] = (center * scale * norm_ref[2:3] + norm_ref[3:4]).astype(BF16)
        return 0

    lax.fori_loop(0, chunks, close, 0)
    push_middle(0).start()
    push_hidden(0).start()
    def turn(c, _):
        at = pl.ds(pl.multiple_of(c * CHUNK, CHUNK), CHUNK)
        turned_ref[:, at] = normed_ref[at].T
        return 0

    lax.fori_loop(0, chunks, turn, 0)
    push_normed(0).start()
    for step in fc_in:
        step()
    fc.copy_own().wait()
    push_fc(0).start()
    for step in proj_in:
        step()
    proj.copy_own().wait()
    push_proj(0).start()
    chain.finish(groups)
    for gather in (*attns, feat, fc, proj):
        gather.finish()
    for push in (push_normed, push_wo, push_maps, push_attn, push_middle, push_hidden, push_fc, push_proj):
        push(0).wait()
    for push in (push_qkv, push_fq, push_fk, push_state, push_mixed, push_rden):
        for g in range(groups):
            push(g).wait()


def feed_forward(
    sizes, hidden_ref, dy_ref, norm_ref, fc_in, proj_in, middle_in,
    block_out, dmid_out, datt_out, dattt_out, gfc_sums, gproj_sums, gnorm_ref,
    fc_ref, proj_ref, middle_ref, out_ref, datt_ref, dattt_ref, gfc_ref, gproj_ref, branch_ref, dhid_ref, act_ref, dpre_ref,
    move_sem, fc_sem, proj_sem, *scratch,
):
    X, Z, H = sizes
    net = Network(sizes)
    chunks, size, width = fc_ref.shape
    part = gfc_ref.shape[3]
    rows = hidden_ref.shape[0]
    tile = 256
    tiles = rows // tile
    paired = (X, H) == (2, 4)

    if paired:
        far, near = (lax.rem(net.dp + 1, 2), net.dp), (flip_bit(net.h, 1), net.h)
        kinds = {"both": (far[0], near[0]), "x": (far[0], near[1]), "y": (far[1], near[0]), "own": (far[1], near[1])}
        plan = [[("both", off) for off in (3, 2, 1, 0)]]
        plan += [[(kind, off) for off in offs for kind in ("x", "y")] for offs in ((3, 2), (1, 0))]
        plan += [[("own", off) for off in (3, 2, 1, 0)]]
        places = []
        for items in plan:
            places.append([])
            for kind, off in items:
                dp, h = kinds[kind]
                places[-1] += [(dp, net.behind(off), h), (dp, net.behind(off), flip_bit(h, 0))]
    else:
        places = [
            [(lax.rem(net.dp + 1 + i, X), b, h) for b in range(Z) for h in range(H)] for i in range(X)
        ]

    def fetch(i, s):
        at = pl.ds(part * s, part)
        return (
            pltpu.make_async_copy(fc_in.at[places[i][s]], fc_ref.at[i, at], fc_sem.at[i, s]),
            pltpu.make_async_copy(proj_in.at[places[i][s]], proj_ref.at[i, at], proj_sem.at[i, s]),
        )

    for i in range(chunks):
        for s in range(size // part):
            for copy in fetch(i, s):
                copy.start()
    mover = Mover(move_sem)
    pull_middle = mover.plan(middle_in, middle_ref)
    pull_middle(0).start()
    net.barrier()
    scatters = [
        Scatter(net, Keep(gfc_sums), gfc_ref, *scratch[:3]),
        Scatter(Network(sizes, 1), Keep(gproj_sums), gproj_ref, *scratch[3:]),
    ]
    branch_ref[...] = jnp.zeros_like(branch_ref)
    dhid_ref[...] = jnp.zeros_like(dhid_ref)

    turns = chunks * tiles
    slots = {}
    if paired:
        own, first, second, both = scatters[0].early_sets()

        def add(slot, chosen, off):
            for scatter in scatters:
                slots.setdefault(slot, []).append(functools.partial(scatter.step, chosen, off))

        for k in range(Z):
            off = Z - 1 - k
            add(tiles + k // 2, both, off)
            add((2 + k // 2) * tiles, second, off)
            add((2 + k // 2) * tiles + 1, first, off)
            add(turns + k, own, off)
    else:
        for scatter in scatters:
            for chosen in reversed(scatter.early_sets()):
                for off in reversed(range(Z)):
                    slots.setdefault(turns, []).append(functools.partial(scatter.step, chosen, off))

    for i in range(chunks):
        for s in range(size // part):
            for copy in fetch(i, s):
                copy.wait()
        here = {k - i * tiles: items for k, items in slots.items() if i * tiles <= k < (i + 1) * tiles}

        def rowed(c, _, i=i, here=here):
            run_at(here, c, tiles)
            at = pl.ds(pl.multiple_of(c * tile, tile), tile)
            fc, proj = fc_ref[i], proj_ref[i]
            pre = dot_nt(hidden_ref[at], fc)
            square = pre * pre
            inner = jnp.tanh(0.7978845608 * pre * (1.0 + 0.044715 * square))
            half = 0.5 * (1.0 + inner)
            act = (pre * half).astype(BF16)
            slope = half + 0.5 * pre * (1.0 - inner * inner) * (0.7978845608 * (1.0 + 3 * 0.044715 * square))
            dpre = (dot_nt(dy_ref[at], proj) * slope).astype(BF16)
            act_ref[at] = act
            dpre_ref[at] = dpre
            branch_ref[at] += dot(act, proj)
            dhid_ref[at] += dot(dpre, fc)
            return 0

        lax.fori_loop(0, tiles, rowed, 0)
        pieces = ((scatters[1], gproj_ref, act_ref, dy_ref), (scatters[0], gfc_ref, dpre_ref, hidden_ref))
        for scatter, grads, left, right in pieces:
            half = size // 2
            for at in (0, half):
                grad = dot_tn(left[:, at : at + half], right[...]).astype(BF16)
                for s in range(half // part):
                    grads[places[i][at // part + s]] = grad[part * s : part * s + part]
            if not paired:
                scatter.begin(lambda dp_at, h_at, i=i: dp_at == places[i][0][0])
                continue
            for kind, off in plan[i]:
                if kind == "both" or kind == "own":
                    scatter.copy(both if kind == "both" else own, off, scatter.last).start()
                else:
                    chosen = (first, second) if kind == "y" else (second, first)
                    pl.when(scatter.net.odd == 0)(scatter.copy(chosen[0], off, scatter.last).start)
                    pl.when(scatter.net.odd == 1)(scatter.copy(chosen[1], off, scatter.last).start)

    gnorm_ref[...] = jnp.zeros_like(gnorm_ref)
    pull_middle(0).wait()
    late_slots = {min(k - turns, tiles - 1): [] for k in slots if k >= turns}
    for k in sorted(slots):
        if k >= turns:
            late_slots[min(k - turns, tiles - 1)] += slots[k]

    def close(c, _):
        at = pl.ds(pl.multiple_of(c * tile, tile), tile)
        middle = middle_ref[at]
        out_ref[at] = (middle + branch_ref[at]).astype(BF16)
        back, gain, shift = norm_backward(middle, norm_ref[2:3].astype(BF16).astype(F32), dhid_ref[at])
        dmid = dy_ref[at].astype(F32) + back
        middle_ref[at] = dmid
        datt_ref[at] = dmid.astype(BF16)
        dattt_ref[:, at] = dmid.astype(BF16).T
        gnorm_ref[2:3] += gain
        gnorm_ref[3:4] += shift
        run_at(late_slots, c, tiles)
        return 0

    lax.fori_loop(0, tiles, close, 0)
    outs = ((out_ref, block_out), (middle_ref, dmid_out), (datt_ref, datt_out), (dattt_ref, dattt_out))
    pushes = [mover.plan(*pair) for pair in outs]
    for push in pushes:
        push(0).start()
    for push in pushes:
        push(0).wait()
    for scatter in scatters:
        scatter.finish()


def attention_backward(
    sizes, heads, depth, len_ref, norm_ref, gnorm_in, gfc_sums, gproj_sums, x_in, normed_in, qkv_in, fq_in, fk_in,
    state_in, mixed_in, rden_in, wo_in, maps_in, w_in, datt_in, dattt_in, dmid_in,
    dx_out, gattn_out, gfeat_out, gfc_ref, gproj_ref, sums_out,
    x_ref, normed_ref, qkv_ref, fq_ref, fk_ref, state_ref, mixed_ref, rden_ref, wo_ref, maps_ref, datt_ref, dattt_ref, dmid_ref,
    w_ref, gw_ref, gnorm_ref, featsum_ref, featpart_ref,
    dne_ref, back_ref, total_ref, picked_ref, dnormed_ref, gsum_ref, cin, cout, chain_send, chain_recv,
    w_sem, move_sem, *scratch,
):
    X, Z, H = sizes
    groups = H
    net = Network(sizes)
    h = net.h
    rows, width = x_ref.shape
    chunks = rows // CHUNK
    part = w_ref.shape[3]
    seq = Rows(len_ref, rows, h)
    low = low_half((CHUNK, 128))

    mover = Mover(move_sem)
    pull_datt, pull_dattt, pull_maps, pull_normed, pull_x, pull_dmid, push_dx = (
        mover.plan(*pair)
        for pair in (
            (datt_in, datt_ref), (dattt_in, dattt_ref), (maps_in, maps_ref), (normed_in, normed_ref), (x_in, x_ref), (dmid_in, dmid_ref),
            (dmid_ref, dx_out),
        )
    )
    ahead_pulls = [
        mover.plan(*pair, groups)
        for pair in ((wo_in, wo_ref), (rden_in, rden_ref), (mixed_in, mixed_ref), (fq_in, fq_ref))
    ]
    group_pulls = [
        mover.plan(*pair, groups) for pair in ((fk_in, fk_ref), (state_in, state_ref), (qkv_in, qkv_ref))
    ]

    def pull_weight(i):
        slot = lax.rem(i, 2)
        return pltpu.make_async_copy(w_in.at[:, :, backwards(i)], w_ref.at[slot], w_sem.at[slot])

    def backwards(i):
        return group_at(h, groups - 1 - i, groups)

    pull_datt(0).start()
    for g in range(groups):
        for pull in ahead_pulls:
            pull(g).start()
    pull_dattt(0).start()
    pull_maps(0).start()
    for i in range(groups):
        for pull in group_pulls:
            pull(backwards(i)).start()
    pull_weight(0).start()
    pull_weight(1).start()
    pull_normed(0).start()
    pull_x(0).start()
    pull_dmid(0).start()
    net.barrier(whole_plane=True)
    fc_along, proj_along = Along(net, gfc_sums, *scratch[0:3]), Along(net, gproj_sums, *scratch[3:6])
    for off in reversed(range(1, Z)):
        fc_along.copy(off).start()
        proj_along.copy(off).start()
    attn_along, feat_along = Along(net, *scratch[6:10]), Along(net, *scratch[10:14])
    attn = Scatter(net, attn_along, gw_ref, *scratch[14:17])
    feat = Scatter(net, feat_along, featpart_ref, *scratch[17:20])
    odd = lax.rem(h, 2)

    down = lax.broadcasted_iota(jnp.int32, (256, 256), 0) // HD
    across = lax.broadcasted_iota(jnp.int32, (256, 256), 1) // HD
    other_half = ((down // 2 == across // 2) & (down != across)).astype(BF16)
    first = seq.first()
    pull_datt(0).wait()

    def ahead(g, _):
        for j in range(heads):
            total_ref[j] = jnp.zeros_like(total_ref[j])
        for pull in ahead_pulls:
            pull(g).wait()

        def piece(i, _):
            c = chunks - 1 - i
            at = pl.ds(pl.multiple_of(c * CHUNK, CHUNK), CHUNK)
            second = seq.second_column(c)
            dm = dot(datt_ref[at], wo_ref[g]).astype(BF16).astype(F32)
            rden = rden_ref[g, at].astype(F32)
            sums = dot((dm * mixed_ref[g, at].astype(F32)).astype(BF16), other_half)
            dnum = dm * rden
            dden = sums * swap_halves(rden) * (-1.0 / HD)
            for j in range(heads):
                lanes = slice(128 * (j // 2), 128 * (j // 2) + 128)
                mine, other = dnum[:, lanes], dden[:, lanes]
                dne = (jnp.where(low, mine, other) if j % 2 == 0 else jnp.where(low, other, mine)).astype(BF16)
                dne_ref[g, j, at] = dne
                back_ref[g, j, c] = total_ref[j].astype(BF16)
                total_ref[j] += dot_tn(fq_ref[g, at, 128 * j : 128 * j + 128], by_sequence(dne, second))
            return 0

        lax.fori_loop(0, chunks, piece, 0, unroll=2)
        for j in range(heads):
            picked_ref[g, j] = total_ref[j, :, :128] * (1.0 - first) + total_ref[j, :, 128:] * first
        return 0

    lax.fori_loop(0, groups, ahead, 0)
    after = seq.after()
    chain = Chain(-1, groups, h, equal(after, first), picked_ref, cin, cout, chain_send, chain_recv)
    lowd = low_half((width, 128))
    shape = (X, Z, part, 128)

    def out_grads(g, _):
        chain.step(g)
        beside = dot(dattt_ref[...], mixed_ref[g])
        for third, value in enumerate((swap_halves(beside[:, :128]), beside[:, :128], swap_halves(beside[:, 128:]))):
            gw_ref[:, :, g, :, 256 * third + 128 : 256 * third + 256] = value.astype(BF16).reshape(shape)
        return 0

    pull_dattt(0).wait()
    lax.fori_loop(0, groups, out_grads, 0)

    dnormed_ref[...] = jnp.zeros_like(dnormed_ref)
    pull_maps(0).wait()
    pull_normed(0).wait()

    def group(i, _):
        g = backwards(i)
        for pull in group_pulls:
            pull(g).wait()

        gsum_ref[...] = jnp.zeros_like(gsum_ref)

        def piece(c, _):
            at = pl.ds(pl.multiple_of(c * CHUNK, CHUNK), CHUNK)
            second = seq.second_column(c)
            lower, upper = seq.masks(c)
            dus_q, dus_k, dvs = [], [], []
            for j in range(heads):
                lanes = slice(128 * j, 128 * j + 128)
                fq, fk, dne = fq_ref[g, at, lanes], fk_ref[g, at, lanes], dne_ref[g, j, at]
                carry = cin[g, j].astype(F32)
                later = jnp.concatenate([carry * (1.0 - after), carry * after], axis=1)
                back = (back_ref[g, j, c].astype(F32) + later).astype(BF16)
                state = state_ref[g, j, c]
                block = qkv_ref[g, at, 512 + 128 * (j // 2) : 640 + 128 * (j // 2)]
                values = with_ones(block, j, low)
                scores_t = jnp.where(upper, dot_nt(fk, fq), 0.0).astype(BF16)
                weigh = jnp.where(lower, dot_nt(dne, values), 0.0).astype(BF16)
                weigh_t = jnp.where(upper, dot_nt(values, dne), 0.0).astype(BF16)
                dfq = dot(weigh, fk) + dot_nt(by_sequence(dne, second), state)
                dfk = dot(weigh_t, fq) + dot_nt(by_sequence(values, second), back)
                inter = dot(fk, back)
                dvs.append(dot(scores_t, dne) + jnp.where(second, inter[:, 128:], inter[:, :128]))
                dus_q.append(feature_back(fq.astype(F32), dfq.astype(BF16).astype(F32)).astype(BF16))
                dus_k.append(feature_back(fk.astype(F32), dfk.astype(BF16).astype(F32)).astype(BF16))
            du_q, du_k = jnp.concatenate(dus_q, axis=1), jnp.concatenate(dus_k, axis=1)
            dq = dot_nt(du_q, maps_ref[0, g]).astype(BF16)
            dk = dot_nt(du_k, maps_ref[1, g]).astype(BF16)
            dv = jnp.concatenate([jnp.where(low, dvs[0], dvs[1]), jnp.where(low, dvs[2], 0.0)], axis=1).astype(BF16)
            gsum_ref[0] += dot_tn(qkv_ref[g, at, 0:256], du_q)
            gsum_ref[1] += dot_tn(qkv_ref[g, at, 256:512], du_k)
            dqkv = jnp.concatenate([dq, dk, dv], axis=1)
            qkv_ref[g, at] = dqkv
            return 0

        lax.fori_loop(0, chunks, piece, 0, unroll=2)
        if (X, H) == (2, 4):

            @pl.when((i == groups - 1) & (odd == 1))
            def _():
                for off in reversed(range(Z)):
                    attn.step(attn.early_sets()[1], off)

        low64 = low_half((HD, 128))
        for j in range(heads):
            sums = [gsum_ref[side, HD * j : HD * j + HD, 128 * j : 128 * j + 128] for side in range(2)]
            sums = [value - pltpu.roll(value, HD, 1) for value in sums]
            pair = jnp.where(low64, sums[0], -sums[1])
            for k in range(X * Z):
                featsum_ref[k // Z, k % Z, g, depth * j : depth * j + depth] = pair[depth * k : depth * k + depth]
        for third in range(3):
            grad = dot(normed_ref[...], qkv_ref[g, :, 256 * third : 256 * third + 256])
            at = 256 * third
            gw_ref[:, :, g, :, at : at + 128] = grad[:, 0:128].astype(BF16).reshape(shape)
            beside = gw_ref[:, :, g, :, at + 128 : at + 256].reshape(width, 128)
            gw_ref[:, :, g, :, at + 128 : at + 256] = (
                jnp.where(lowd, grad[:, 128:256], beside.astype(F32)).astype(BF16).reshape(shape)
            )
        attn.begin(lambda dp_at, h_at: h_at == g)

        if (X, H) == (2, 4):

            @pl.when(i == groups - 2)
            def _():
                for off in reversed(range(Z)):
                    attn.step(attn.early_sets()[3], off)

                @pl.when(odd == 0)
                def _():
                    for off in reversed(range(Z)):
                        attn.step(attn.early_sets()[2], off)

        return 0

    featsum_ref[...] = jnp.zeros_like(featsum_ref)
    lax.fori_loop(0, groups, group, 0)
    for k in range(X * Z):
        for g in range(groups):
            featpart_ref[k // Z, k % Z, g] = featsum_ref[k // Z, k % Z, g].astype(BF16)
    feat.begin()

    gnorm_ref[...] = gnorm_in[...]
    turns = groups * chunks
    slots = {}
    for scatter in (attn, feat):
        own, *others = scatter.early_sets()
        for off in reversed(range(Z)):
            late = (Z - 1 - off) * turns // Z
            turn = {chosen: functools.partial(scatter.step, chosen, off) for chosen in (own, *others)}
            if scatter is attn and (X, H) == (2, 4):

                def cross(turn=turn):
                    pl.when(odd == 0)(turn[others[0]])
                    pl.when(odd == 1)(turn[others[1]])

                slots.setdefault(1 + late // 4, []).append(cross)
                slots.setdefault(4 + late * 3 // 4, []).append(turn[own])
            else:
                for k, chosen in enumerate(reversed(others)):
                    slots.setdefault(1 + 4 * k if len(others) == 3 else 1, []).append(turn[chosen])
                slots.setdefault(turns - 2, []).append(turn[own])

    def through(i, _):
        slot = lax.rem(i, 2)
        pull_weight(i).wait()

        def piece(c, _):
            run_at(slots, i * chunks + c, turns)
            at = pl.ds(pl.multiple_of(c * CHUNK, CHUNK), CHUNK)
            dnormed_ref[at] += dot_nt(qkv_ref[backwards(i), at], w_ref[slot].reshape(width, width))
            return 0

        lax.fori_loop(0, chunks, piece, 0, unroll=2)

        @pl.when(i < groups - 2)
        def _():
            pull_weight(i + 2).start()

        return 0

    lax.fori_loop(0, groups, through, 0)
    pull_x(0).wait()
    pull_dmid(0).wait()

    def close(c, _):
        at = pl.ds(pl.multiple_of(c * CHUNK, CHUNK), CHUNK)
        gain_row = norm_ref[0:1].astype(BF16).astype(F32)
        back, gain, shift = norm_backward(x_ref[at].astype(F32), gain_row, dnormed_ref[at])
        dmid_ref[at] = dmid_ref[at] + back
        gnorm_ref[0:1] += gain
        gnorm_ref[1:2] += shift
        return 0

    lax.fori_loop(0, chunks, close, 0)
    push_dx(0).start()
    square = jnp.zeros((1, 128), F32)
    gfc_ref[...] = fc_along.result()
    gproj_ref[...] = proj_along.result()
    gattn_out[...] = attn_along.result()
    gfeat_out[...] = feat_along.result()
    for ref in (gattn_out, gfeat_out, gfc_ref, gproj_ref):
        column = jnp.sum(ref[...] * ref[...], axis=0, keepdims=True)
        for at in range(0, column.shape[1], 128):
            square = square + column[:, at : at + 128]
    gnorm_ref[4:5, 0:128] = square
    sums_out[...] = total_over_all(net, gnorm_ref[...], *scratch[20:])
    push_dx(0).wait()
    chain.finish(groups)
    for moving in (attn, feat, fc_along, proj_along, attn_along, feat_along):
        moving.finish()


def adamw_update(master, first_mom, second_mom, grad_in, factor, step_rate, decay_rate):
    clipped = grad_in * factor
    first_new = beta_one * first_mom + (1.0 - beta_one) * clipped
    second_new = beta_two * second_mom + (1.0 - beta_two) * clipped * clipped
    direction = (
        first_new
        / (1.0 - beta_one**STEP)
        / (jnp.sqrt(second_new / (1.0 - beta_two**STEP)) + adam_eps)
    )
    master_new = master - step_rate * (direction + decay_rate * master)
    return (master_new, first_new, second_new)


def update_kernel(heads, depth, sums_ref, gattn_ref, gfeat_ref, gfc_ref, gproj_ref, *refs):
    masters, firsts, seconds = refs[0:6], refs[6:12], refs[12:18]
    block_in, dx_in, norm_out = refs[18:21]
    outs, (block_out, dx_out), (feat_grads, block_ref, dx_ref, sems) = refs[21:46], refs[46:48], refs[48:]
    mover = Mover(sems)
    pulls = [mover.plan(block_in, block_ref)(0), mover.plan(dx_in, dx_ref)(0)]
    pushes = [mover.plan(block_ref, block_out)(0), mover.plan(dx_ref, dx_out)(0)]
    for pull in pulls:
        pull.start()
    norm_grads = sums_ref[0:4]
    squares = jnp.sum(sums_ref[4:5, 0:128], keepdims=True) + jnp.sum(norm_grads * norm_grads, keepdims=True)
    grad_norm = jnp.sqrt(squares)
    norm_out[...] = jnp.broadcast_to(grad_norm, norm_out.shape)
    factor = clip_limit / jnp.maximum(grad_norm, clip_limit)
    rates, decays = (0.02, 0.4, 0.15, 0.02, 0.01, 0.3), (0.1, 0.1, 0.1, 0.1, 0.1, 0.0)

    def update(which, at, grads):
        results = adamw_update(
            masters[which][at], firsts[which][at], seconds[which][at], grads, factor, rates[which], decays[which]
        )
        results += (results[0].astype(BF16),)
        if which < 5:
            for kind, value in enumerate(results):
                outs[6 * kind + which][at] = value
        else:
            outs[5][...], outs[11][...] = results[0], results[1]
            outs[17][...], outs[23][...] = results[2][0:2], results[2][2:4]
            outs[24][...] = results[3]

    low = low_half((1, 128))
    for j in range(heads):
        for d in range(0, depth, 2):
            row, other = (gfeat_ref[depth * j + d + k : depth * j + d + k + 1] for k in range(2))
            at = slice(64 * d, 64 * d + 128)
            feat_grads[j, 0:1, at] = jnp.where(low, row, pltpu.roll(other, HD, 1))
            feat_grads[j, 1:2, at] = jnp.where(low, pltpu.roll(row, HD, 1), other)
    for j in range(3):
        update(0, (j,), gattn_ref[:, 256 * j : 256 * j + heads * HD])
        update(1, (slice(HD * j, HD * j + HD),), gattn_ref[:, 256 * j + heads * HD : 256 * j + 256].T)
    update(2, (slice(None),), feat_grads[...])
    update(3, (slice(None),), gfc_ref[...])
    for pull, push in zip(pulls, pushes):
        pull.wait()
        push.start()
    update(4, (slice(None),), gproj_ref[...])
    update(5, (slice(None),), norm_grads)
    for push in pushes:
        push.wait()


def in_vmem(count):
    return [pl.BlockSpec(memory_space=VMEM)] * count


def struct(shape, dtype):
    return jax.ShapeDtypeStruct(shape, dtype)


def call(kernel, outs, smem, operands, scratch, collective_id, name, flops, hbm_in=0, hbm_out=(), limit=63):
    specs = [pl.BlockSpec(memory_space=pltpu.SMEM)] * smem + in_vmem(len(operands) - smem - hbm_in)
    specs += [pl.BlockSpec(memory_space=pl.ANY)] * hbm_in
    out_specs = [pl.BlockSpec(memory_space=pl.ANY if i in hbm_out else VMEM) for i in range(len(outs))]
    traffic = sum(o.size * o.dtype.itemsize for o in outs) + sum(o.size * o.dtype.itemsize for o in operands)
    extra = {} if collective_id is None else {"collective_id": collective_id, "has_side_effects": True}
    return pl.pallas_call(
        kernel,
        out_shape=tuple(outs),
        in_specs=specs,
        out_specs=tuple(out_specs),
        scratch_shapes=scratch,
        compiler_params=pltpu.CompilerParams(vmem_limit_bytes=limit * 2**20, **extra),
        cost_estimate=pl.CostEstimate(flops=flops, bytes_accessed=traffic, transcendentals=0),
        name=name,
    )(*operands)


def on_device(
    sizes,
    block_in,
    cotangent,
    seq_len,
    w_qkv,
    w_out,
    w_feat,
    w_fc,
    w_proj,
    norm_params,
    first_qkv,
    second_qkv,
    first_out,
    second_out,
    first_feat,
    second_feat,
    first_fc,
    second_fc,
    first_proj,
    second_proj,
    first_norms,
    second_norms,
):
    X, Z, H = sizes
    rows, width = block_in.shape
    part, _, head_width = w_qkv.shape
    heads = w_feat.shape[1]
    depth = w_feat.shape[2] // HD
    chunks = rows // CHUNK

    big = (X, Z, H, part, width)
    small = (X, Z, H, FEAT_ROWS, 2 * HD)
    dma = pltpu.SemaphoreType.DMA
    chain_scratch = [
        VMEM((H, heads, 128, 128), F32),
        VMEM((H, heads, 128, 128), BF16),
        VMEM((H, heads, 128, 128), BF16),
        dma((H,)),
        dma((H,)),
    ]
    turned = struct((width, rows), BF16)
    held = [
        struct((rows, width), BF16),
        struct((H, rows, width), BF16),
        struct((H, rows, 128 * heads), BF16),
        struct((H, rows, 128 * heads), BF16),
        struct((H, heads, chunks, 128, 256), BF16),
        struct((H, rows, 256), BF16),
        struct((H, rows, 256), BF16),
        struct((H, width, 256), BF16),
        struct((2, H, 256, 128 * heads), BF16),
        struct((rows, width), F32),
        struct((rows, width), BF16),
    ]
    normed, qkv, fq, fk, states, mixed, rden, wo, maps, middle, hidden, attn_w, fc_w, proj_w = call(
        functools.partial(attention_forward, sizes, heads, depth),
        [turned] + held[1:] + [struct(big, BF16)] * 3,
        1,
        [seq_len, block_in, w_qkv.transpose(1, 0, 2), w_out, w_feat.transpose(1, 0, 2), w_fc.T, w_proj, norm_params],
        [VMEM(item.shape, item.dtype) for item in held]
        + [
            VMEM(turned.shape, BF16),
            VMEM((part, width), BF16),
            VMEM((FEAT_ROWS, 128), BF16),
            VMEM((part, width), BF16),
            VMEM((part, width), BF16),
            VMEM((FEAT_ROWS, 128), F32),
            VMEM((4, width), F32),
        ]
        + [VMEM(big, BF16), VMEM(big, BF16), VMEM(big, BF16), VMEM(small, BF16), VMEM((H * heads, HD, 128), F32), VMEM((heads, 128, 256), F32)]
        + chain_scratch
        + [dma((8 + 6 * H,))]
        + [sem for _ in range(5) for sem in gather_sems(sizes)],
        0,
        "attention_forward",
        10**10,
        hbm_out=range(14),
    )

    turns = 4 if (X, H) == (2, 4) else X
    size = X * Z * H * part // turns
    block_out, d_middle, d_att, d_att_t, fc_sums, proj_sums, g_norm = call(
        functools.partial(feed_forward, sizes),
        [
            struct((rows, width), BF16),
            struct((rows, width), F32),
            struct((rows, width), BF16),
            turned,
            struct((Z, part, width), BF16),
            struct((Z, part, width), BF16),
            struct((8, width), F32),
        ],
        0,
        [hidden, cotangent, norm_params, fc_w, proj_w, middle],
        [
            VMEM((turns, size, width), BF16),
            VMEM((turns, size, width), BF16),
            VMEM((rows, width), F32),
            VMEM((rows, width), BF16),
            VMEM((rows, width), BF16),
            VMEM(turned.shape, BF16),
            VMEM(big, BF16),
            VMEM(big, BF16),
            VMEM((rows, width), F32),
            VMEM((rows, width), F32),
            VMEM((rows, size), BF16),
            VMEM((rows, size), BF16),
            dma((5,)),
            dma((turns, size // part)),
            dma((turns, size // part)),
        ]
        + scatter_scratch(sizes, (part, width)) * 2,
        1,
        "feed_forward",
        3 * 10**10,
        hbm_in=3,
        hbm_out=range(4),
    )

    pulled = [struct((rows, width), BF16), turned] + held[1:9] + [struct((rows, width), BF16), turned, struct((rows, width), F32)]
    block_in_grad, g_attn, g_feat, g_fc, g_proj, sums = call(
        functools.partial(attention_backward, sizes, heads, depth),
        [
            struct((rows, width), F32),
            struct((part, width), F32),
            struct((FEAT_ROWS, 128), F32),
            struct((part, width), F32),
            struct((part, width), F32),
            struct((8, width), F32),
        ],
        1,
        [
            seq_len, norm_params, g_norm, fc_sums, proj_sums, block_in, normed, qkv, fq, fk, states, mixed, rden, wo, maps,
            attn_w, d_att, d_att_t, d_middle,
        ],
        [VMEM(item.shape, item.dtype) for item in pulled]
        + [
            VMEM((2, X, Z, part, width), BF16),
            VMEM(big, BF16),
            VMEM((8, width), F32),
            VMEM(small, F32),
            VMEM(small, BF16),
            VMEM((H, heads, rows, 128), BF16),
            VMEM((H, heads, chunks, 128, 256), BF16),
            VMEM((heads, 128, 256), F32),
            chain_scratch[0],
            VMEM((rows, width), F32),
            VMEM((2, 256, 128 * heads), F32),
        ]
        + chain_scratch[1:]
        + [dma((2,)), dma((7 + 7 * H,))]
        + along_scratch(sizes, (part, width)) * 2
        + [VMEM((Z, part, width), BF16)]
        + along_scratch(sizes, (part, width))
        + [VMEM((Z, FEAT_ROWS, 128), BF16)]
        + along_scratch(sizes, (FEAT_ROWS, 128))
        + scatter_scratch(sizes, (part, width))
        + scatter_scratch(sizes, (FEAT_ROWS, 128))
        + total_scratch(sizes, (8, width)),
        2,
        "attention_backward",
        2 * 10**10,
        hbm_in=14,
        hbm_out=(0,),
    )

    def turned(qkv, out, feat, fc, proj, *norms):
        return [qkv.transpose(1, 0, 2), out, feat.transpose(1, 0, 2), fc.T, proj, *norms]

    masters = turned(w_qkv, w_out, w_feat, w_fc, w_proj, norm_params)
    firsts = turned(first_qkv, first_out, first_feat, first_fc, first_proj, first_norms)
    seconds = turned(second_qkv, second_out, second_feat, second_fc, second_proj, second_norms)
    shapes = [item.shape for item in masters]
    halves = (2, width)
    norm_filled, *updated, block_out, block_in_grad = call(
        functools.partial(update_kernel, heads, depth),
        [struct((8, 128), F32)]
        + [struct(shape, F32) for shape in shapes * 2 + shapes[:5] + [halves]]
        + [struct(shape, BF16) for shape in shapes[:5]]
        + [struct(halves, F32), struct(shapes[5], BF16)]
        + [struct((rows, width), BF16), struct((rows, width), F32)],
        0,
        [sums, g_attn, g_feat, g_fc, g_proj] + masters + firsts + seconds + [block_out, block_in_grad],
        [VMEM(shapes[2], F32), VMEM((rows, width), BF16), VMEM((rows, width), F32), dma((4,))],
        None,
        "update",
        10**7,
        hbm_in=2,
        hbm_out=(26, 27),
    )
    new, new_first, new_second = (turned(*updated[6 * kind : 6 * kind + 6]) for kind in range(3))
    copies = turned(*updated[18:23], updated[24])
    return (
        norm_filled[0, 0],
        block_out,
        block_in_grad,
        *new,
        *new_first,
        *new_second[:5],
        new_second[5],
        updated[23],
        *copies,
    )


def solution(mesh):
    everything = ("dp", "batch", "head")
    rows = P(everything, None)
    qkv, out, feat = P(("dp", "batch"), None, "head"), P("head", ("dp", "batch")), P(None, "head", ("dp", "batch"))
    fc, proj, whole = P(None, everything), P(everything, None), P()
    weights = (qkv, out, feat, fc, proj, whole)
    in_specs = (rows, rows, P(("dp", "batch"), None)) + weights
    for spec in weights:
        in_specs += (spec, spec)
    out_specs = (whole, rows, rows) + weights + weights + weights[:5] + (whole, whole) + weights
    sizes = (mesh.shape["dp"], mesh.shape["batch"], mesh.shape["head"])
    return jax.shard_map(
        functools.partial(on_device, sizes), mesh=mesh, in_specs=in_specs, out_specs=out_specs, check_vma=False
    )
```

```python
import functools

import jax
import jax.numpy as jnp
from jax import lax
from jax.experimental import pallas as pl
from jax.experimental.pallas import tpu as pltpu
from jax.sharding import PartitionSpec as P

HD = 64
STEP = 8
CHUNK = 256
FEAT_ROWS = 32
FC_TURNS = (0, 4, 8, 12, 16)
PROJ_BEGIN = 0
PROJ_TURNS = (2, 6, 10, 14, 18)
MESH = pl.DeviceIdType.MESH
VMEM = pltpu.VMEM
F32 = jnp.float32
BF16 = jnp.bfloat16

norm_eps = 1e-05
beta_one = 0.9
beta_two = 0.95
adam_eps = 1e-08
clip_limit = 1.0


def dot(left, right):
    return lax.dot_general(left, right, (((1,), (0,)), ((), ())), preferred_element_type=F32)


def dot_nt(left, right):
    return lax.dot_general(left, right, (((1,), (1,)), ((), ())), preferred_element_type=F32)


def dot_tn(left, right):
    return lax.dot_general(left, right, (((0,), (0,)), ((), ())), preferred_element_type=F32)


def flip_bit(value, bit, on=1):
    low = 2**bit
    return value + on * (low - 2 * low * lax.rem(value // low, 2))


class Network:
    def __init__(self, sizes, swap=0):
        self.X, self.Z, self.H = sizes
        self.dp, self.b, self.h = (lax.axis_index(name) for name in ("dp", "batch", "head"))
        dp_bits, head_bits = self.X.bit_length() - 1, self.H.bit_length() - 1
        if (self.X, self.H) == (2, 4):
            self.odd = lax.rem(self.h + swap, 2)

            def first(dp, h):
                odd = lax.rem(h + swap, 2)
                return flip_bit(dp, 0, 1 - odd), flip_bit(h, 1, odd)

            def second(dp, h):
                odd = lax.rem(h + swap, 2)
                return flip_bit(dp, 0, odd), flip_bit(h, 1, 1 - odd)

            self.flips = [first, second, lambda dp, h: (dp, flip_bit(h, 0))]
        else:
            self.flips = [lambda dp, h, k=k: (flip_bit(dp, k), h) for k in range(dp_bits)]
            self.flips += [lambda dp, h, k=k: (dp, flip_bit(h, k)) for k in reversed(range(head_bits))]
        self.sets = [()]
        for k in range(len(self.flips)):
            self.sets += [s + (k,) for s in self.sets]
        self.index = {s: i for i, s in enumerate(self.sets)}

    def coord(self, chosen):
        dp, h = self.dp, self.h
        for k in sorted(chosen, reverse=True):
            dp, h = self.flips[k](dp, h)
        return dp, h

    def behind(self, off):
        return lax.rem(self.b + self.Z - off, self.Z)

    def ahead(self, off):
        return lax.rem(self.b + off, self.Z)

    def slot(self, chosen, off):
        dp, h = self.coord(chosen)
        return dp, self.behind(off), h

    def partner(self, k):
        dp, h = self.flips[k](self.dp, self.h)
        return {"dp": dp, "batch": self.b, "head": h}

    def along(self, b):
        return {"dp": self.dp, "batch": b, "head": self.h}

    def stages(self, chosen):
        return range(max(chosen) + 1 if chosen else 0, len(self.flips))

    def plane(self):
        count = self.X * self.H
        mine = self.dp * self.H + self.h
        for step in range(1, count):
            other = lax.rem(mine + step, count)
            yield step, {"dp": other // self.H, "batch": self.b, "head": lax.rem(other, self.H)}

    def barrier(self, chained=False, whole_plane=False):
        pl.semaphore_wait(pltpu.get_barrier_semaphore(), self.greet(chained, whole_plane))

    def greet(self, chained=False, whole_plane=False):
        sem = pltpu.get_barrier_semaphore()
        devices = [self.along(self.ahead(off)) for off in range(1, self.Z)]
        if whole_plane:
            devices += [device for _, device in self.plane()]
        else:
            devices += [self.partner(k) for k in range(len(self.flips))]
            if chained:
                devices += [{"head": lax.rem(self.h + step, self.H)} for step in (1, self.H - 1)]
        for device in devices:
            pl.semaphore_signal(sem, inc=1, device_id=device, device_id_type=MESH)
        return len(devices)


def gather_sems(sizes):
    X, Z, H = sizes
    return [pltpu.SemaphoreType.DMA((X * H + 1, Z)), pltpu.SemaphoreType.DMA((X * H, Z))]


class Gather:
    def __init__(self, net, shard, buf, send, recv, rows=None):
        self.net, self.send, self.recv = net, send, recv
        self.rows = pl.ds(0, shard.shape[0]) if rows is None else rows
        self.shard, self.buf = shard.at[self.rows], buf
        self.inner = (net.b == 1) | (net.b == 2)
        self.ends = send.shape[0] - 1

    def near(self, t):
        b = self.net.b
        return (b, flip_bit(b, 0), 2 - b // 2, 3 - 3 * (b // 2))[t]

    def slot(self, chosen, t):
        dp, h = self.net.coord(chosen)
        return dp, self.near(t), h, self.rows

    def source(self, chosen, t):
        return self.shard if chosen == () and t == 0 else self.buf.at[self.slot(chosen, t)]

    def copy(self, chosen, t, k):
        net = self.net
        into = net.index[chosen + (k,)]
        return pltpu.make_async_remote_copy(
            src_ref=self.source(chosen, t), dst_ref=self.buf.at[self.slot(chosen, t)],
            send_sem=self.send.at[into, t], recv_sem=self.recv.at[into, t],
            device_id=net.partner(k), device_id_type=MESH,
        )

    def hop(self, t, outward, arrives, send_sem):
        net = self.net
        return pltpu.make_async_remote_copy(
            src_ref=self.source((), t), dst_ref=self.buf.at[self.slot((), t)],
            send_sem=send_sem, recv_sem=self.recv.at[0, arrives],
            device_id=net.along(flip_bit(net.b, 0) if outward else 3 - net.b), device_id_type=MESH,
        )

    def pair_hop(self):
        return self.hop(0, True, 1, self.send.at[self.ends, 0])

    def inner_hops(self, t):
        ends = self.send.at[self.ends, 1]
        return self.hop(t, t > 1, (2, 3, 2, 3)[t], self.send.at[0, t] if t else ends)

    def copy_own(self):
        return pltpu.make_async_copy(self.shard, self.buf.at[self.slot((), 0)], self.send.at[self.ends, 2])

    def arrived(self, chosen, t):
        net = self.net
        place = self.buf.at[self.slot(chosen, t)]
        into = net.index[chosen]
        pltpu.make_async_remote_copy(
            src_ref=place, dst_ref=place, send_sem=self.send.at[into, t], recv_sem=self.recv.at[into, t],
            device_id=net.partner(0), device_id_type=MESH,
        ).wait_recv()

    def begin(self):
        self.pair_hop().start()
        pl.when(self.inner)(lambda: self.inner_hops(0).start())
        for k in self.net.stages(()):
            self.copy((), 0, k).start()
        self.copy_own().start()

    def step(self, chosen, t):
        self.arrived(chosen, t)
        if chosen == ():
            pl.when(self.inner)(lambda: self.inner_hops(t).start())
        for k in self.net.stages(chosen):
            self.copy(chosen, t, k).start()

    def steps(self):
        net = self.net
        early = net.sets[: len(net.sets) // 2]
        rounds = [[] for _ in range(net.Z + max(len(chosen) for chosen in early))]
        for t in range(net.Z):
            for chosen in early:
                if chosen or t:
                    rounds[t + len(chosen)].append(functools.partial(self.step, chosen, t))
        late = [functools.partial(self.step, chosen, t) for chosen in net.sets[len(early) :] for t in range(net.Z)]
        return rounds[1:], late

    def layers(self):
        early = self.net.sets[: len(self.net.sets) // 2]
        found = [[[] for _ in range(self.net.Z)] for _ in range(1 + max(len(chosen) for chosen in early))]
        for t in range(self.net.Z):
            for chosen in early:
                if chosen or t:
                    found[len(chosen)][t].append(functools.partial(self.step, chosen, t))
        return found

    def finish(self):
        net = self.net
        self.pair_hop().wait_send()

        @pl.when(self.inner)
        def _():
            for t in range(net.Z):
                self.inner_hops(t).wait_send()

        for chosen in net.sets:
            for k in net.stages(chosen):
                for t in range(net.Z):
                    self.copy(chosen, t, k).wait_send()


def scatter_scratch(sizes, shape):
    X, Z, H = sizes
    n = X * H
    return [VMEM((n, Z) + shape, BF16), pltpu.SemaphoreType.DMA((n, Z)), pltpu.SemaphoreType.DMA((n, Z))]


class Scatter:
    def __init__(self, net, along, part, inbox, send, recv):
        self.net, self.along, self.part, self.inbox, self.send, self.recv = net, along, part, inbox, send, recv
        self.last = len(net.flips) - 1

    def sum_at(self, chosen, off):
        return self.inbox.at[self.net.index[chosen + (self.last,)], off]

    def copy(self, chosen, off, k):
        net = self.net
        into = net.index[chosen + (k,)]
        first = k == self.last
        source = self.part.at[net.slot(chosen + (k,), off)] if first else self.sum_at(chosen + (k,), off)
        return pltpu.make_async_remote_copy(
            src_ref=source, dst_ref=self.inbox.at[into, off], send_sem=self.send.at[into, off],
            recv_sem=self.recv.at[into, off], device_id=net.partner(k), device_id_type=MESH,
        )

    def early_sets(self):
        return self.net.sets[: len(self.net.sets) // 2]

    def begin(self, ready=None, offs=None):
        for chosen in reversed(self.early_sets()):

            def start(chosen=chosen):
                for off in range(self.net.Z) if offs is None else offs:
                    self.copy(chosen, off, self.last).start()

            if ready is None:
                start()
            else:
                pl.when(ready(*self.net.coord(chosen + (self.last,))))(start)

    def step(self, chosen, off):
        net = self.net
        total = self.part[net.slot(chosen, off)].astype(F32)
        for k in reversed(net.stages(chosen)):
            self.copy(chosen, off, k).wait_recv()
            total = total + self.inbox[net.index[chosen + (k,)], off].astype(F32)
        if chosen:
            self.sum_at(chosen, off)[...] = total.astype(BF16)
            self.copy(chosen[:-1], off, chosen[-1]).start()
        else:
            self.along.give(off, total.astype(BF16))

    def finish(self):
        net = self.net
        for chosen in net.sets:
            for k in net.stages(chosen):
                for off in range(net.Z):
                    self.copy(chosen, off, k).wait_send()


def along_scratch(sizes, shape):
    X, Z, H = sizes
    return [VMEM((Z,) + shape, BF16), pltpu.SemaphoreType.DMA((Z,)), pltpu.SemaphoreType.DMA((Z,))]


class Along:
    def __init__(self, net, sums, inbox, send, recv):
        self.net, self.sums, self.inbox, self.send, self.recv = net, sums, inbox, send, recv

    def copy(self, off):
        net = self.net
        return pltpu.make_async_remote_copy(
            src_ref=self.sums.at[off], dst_ref=self.inbox.at[off], send_sem=self.send.at[off],
            recv_sem=self.recv.at[off], device_id=net.along(net.behind(off)), device_id_type=MESH,
        )

    def give(self, off, value):
        self.sums[off] = value
        if off:
            self.copy(off).start()

    def result(self):
        total = self.sums[0].astype(F32)
        for off in range(1, self.net.Z):
            self.copy(off).wait_recv()
            total = total + self.inbox[off].astype(F32)
        return total

    def finish(self):
        for off in range(1, self.net.Z):
            self.copy(off).wait_send()


class Keep:
    def __init__(self, sums):
        self.sums = sums

    def give(self, off, value):
        self.sums[off] = value


def total_scratch(sizes, shape):
    X, Z, H = sizes
    count = X * H
    return [
        VMEM((count + Z,) + shape, F32),
        pltpu.SemaphoreType.DMA((count + Z,)),
        pltpu.SemaphoreType.DMA((count + Z,)),
    ]


def total_over_all(net, value, slots, send, recv):
    count, Z = net.X * net.H, net.Z

    def exchange(value, base, mine, size, devices):
        slots[base + mine] = value
        for step, device in devices:
            place = slots.at[base + mine]
            pltpu.make_async_remote_copy(
                src_ref=place, dst_ref=place, send_sem=send.at[base + step], recv_sem=recv.at[base + step],
                device_id=device, device_id_type=MESH,
            ).start()
        for step, device in devices:
            place = slots.at[base + lax.rem(mine + size - step, size)]
            copy = pltpu.make_async_remote_copy(
                src_ref=place, dst_ref=place, send_sem=send.at[base + step], recv_sem=recv.at[base + step],
                device_id=device, device_id_type=MESH,
            )
            copy.wait_recv()
            copy.wait_send()
        total = slots[base]
        for i in range(1, size):
            total = total + slots[base + i]
        return total

    value = exchange(value, 0, net.dp * net.H + net.h, count, list(net.plane()))
    return exchange(value, count, net.b, Z, [(off, net.along(net.ahead(off))) for off in range(1, Z)])


class Mover:
    def __init__(self, sems):
        self.sems, self.used = sems, 0

    def plan(self, source, target, count=None):
        at = self.used
        self.used += 1 if count is None else count

        def make(i):
            if count is None:
                return pltpu.make_async_copy(source, target, self.sems.at[at])
            return pltpu.make_async_copy(source.at[i], target.at[i], self.sems.at[at + i])

        return make


def norm_stats(values):
    mean = jnp.mean(values, axis=-1, keepdims=True)
    center = values - mean
    spread = jnp.mean(center * center, axis=-1, keepdims=True)
    return center, lax.rsqrt(spread + norm_eps)


def norm_backward(values, gain_row, grads):
    center, scale = norm_stats(values)
    normal = center * scale
    inner = grads * gain_row
    part = jnp.mean(inner * normal, axis=-1, keepdims=True)
    back = scale * (inner - jnp.mean(inner, axis=-1, keepdims=True) - normal * part)
    return back, jnp.sum(grads * normal, axis=0, keepdims=True), jnp.sum(grads, axis=0, keepdims=True)


def low_half(shape):
    return lax.rem(lax.broadcasted_iota(jnp.int32, shape, len(shape) - 1), 128) < HD


def swap_halves(values):
    cols = values.shape[1]
    parts = [pltpu.roll(values[:, at : at + 128], HD, 1) for at in range(0, cols, 128)]
    return parts[0] if len(parts) == 1 else jnp.concatenate(parts, axis=1)


def half_ones():
    down = lax.broadcasted_iota(jnp.int32, (128, 128), 0) // HD
    across = lax.broadcasted_iota(jnp.int32, (128, 128), 1) // HD
    return (down == across).astype(BF16)


def feature_pair(scaled, live):
    low = low_half(scaled.shape)
    top = jnp.max(jnp.where(low, scaled, -jnp.inf), axis=-1, keepdims=True)
    bottom = jnp.max(jnp.where(low, -jnp.inf, scaled), axis=-1, keepdims=True)
    powers = jnp.exp(scaled - jnp.where(low, top, bottom))
    sums = dot(powers.astype(BF16), half_ones())
    return powers * (live / sums)


def feature_back(feature, grads):
    product = feature * grads
    return product - feature * dot(product.astype(BF16), half_ones())


class Rows:
    def __init__(self, len_ref, rows, h):
        self.first_len = len_ref[0, 0]
        self.both_len = len_ref[0, 0] + len_ref[0, 1]
        self.start = h * rows
        self.rows = rows

    def second(self, row):
        return row >= self.first_len

    def column(self, chunk):
        return self.start + chunk * CHUNK + lax.broadcasted_iota(jnp.int32, (CHUNK, 1), 0)

    def live(self, chunk):
        return (self.column(chunk) < self.both_len).astype(F32)

    def second_column(self, chunk):
        return self.second(self.column(chunk))

    def masks(self, chunk):
        base = self.start + chunk * CHUNK
        down = base + lax.broadcasted_iota(jnp.int32, (CHUNK, CHUNK), 0)
        across = base + lax.broadcasted_iota(jnp.int32, (CHUNK, CHUNK), 1)
        same = (down >= self.first_len) == (across >= self.first_len)
        return same & (across <= down), same & (across >= down)

    def scalar(self, row):
        return jnp.where(self.second(row), 1.0, 0.0).astype(F32)

    def before(self):
        return self.scalar(self.start - 1)

    def first(self):
        return self.scalar(self.start)

    def last(self):
        return self.scalar(self.start + self.rows - 1)

    def after(self):
        return self.scalar(self.start + self.rows)


def with_ones(block, head, low):
    ones = jnp.ones_like(block)
    return jnp.where(low, block, ones) if head % 2 == 0 else jnp.where(low, ones, block)


def by_sequence(values, second):
    zero = jnp.zeros_like(values)
    return jnp.concatenate([jnp.where(second, zero, values), jnp.where(second, values, zero)], axis=1)


class Chain:
    def __init__(self, step, n, h, same, picked, cin, cout, send, recv):
        self.first = h == (0 if step == 1 else n - 1)
        self.final = h == (n - 1 if step == 1 else 0)
        self.neighbour = {"head": lax.rem(h + n + step, n)}
        self.same, self.picked, self.cin, self.cout, self.send, self.recv = same, picked, cin, cout, send, recv

    def copy(self, g):
        return pltpu.make_async_remote_copy(
            src_ref=self.cout.at[g], dst_ref=self.cin.at[g], send_sem=self.send.at[g], recv_sem=self.recv.at[g],
            device_id=self.neighbour, device_id_type=MESH,
        )

    def step(self, g):
        @pl.when(self.first)
        def _():
            self.cin[g] = jnp.zeros_like(self.cin[g])

        @pl.when(jnp.logical_not(self.first))
        def _():
            self.copy(g).wait_recv()

        @pl.when(jnp.logical_not(self.final))
        def _():
            self.cout[g] = (self.picked[g] + self.cin[g].astype(F32) * self.same).astype(BF16)
            self.copy(g).start()

    def finish(self, n):
        @pl.when(jnp.logical_not(self.final))
        def _():
            for g in range(n):
                self.copy(g).wait_send()


def group_at(h, i, n):
    bits = n.bit_length() - 1
    for k in range(bits):
        h = flip_bit(h, bits - 1 - k, lax.rem(i // 2**k, 2))
    return h


def run_at(slots, i, count):
    for k in range(count):
        if slots.get(k):

            @pl.when(i == k)
            def _(items=slots[k]):
                for item in items:
                    item()


def rest_of(slots, count):
    for k in sorted(slots):
        if k >= count:
            for item in slots[k]:
                item()


def equal(a, b):
    return a * b + (1.0 - a) * (1.0 - b)


def attention_forward(
    sizes, heads, depth, len_ref, x_ref, wqkv_ref, wout_ref, wfeat_ref, wfc_ref, wproj_ref, norm_in,
    normed_out, qkv_out, fq_out, fk_out, state_out, mixed_out, rden_out, wo_out, maps_out, middle_out, hidden_out,
    attn_out, fc_out, proj_out,
    normed_ref, qkv_ref, fq_ref, fk_ref, state_ref, mixed_ref, rden_ref, wo_ref, maps_ref, middle_ref, hidden_ref,
    turned_ref, attn_shard, feat_shard, fc_shard, proj_shard, feat_rows, norm_ref,
    w_ref, fc_ref, proj_ref, feat_ref, pairs_ref, total_ref, picked_ref, cin, cout, chain_send, chain_recv, move_sem,
    *sems,
):
    X, Z, groups = sizes
    net = Network(sizes)
    greeted = net.greet(chained=True)
    lanes_here = heads * HD
    for j in range(3):
        attn_shard[:, 256 * j : 256 * j + 128] = wqkv_ref[j, :, 0:128].astype(BF16)
        attn_shard[:, 256 * j + 128 : 256 * j + 256] = jnp.concatenate(
            [wqkv_ref[j, :, 128:lanes_here], wout_ref[HD * j : HD * j + HD].T], axis=1
        ).astype(BF16)
    feat_rows[...] = jnp.zeros_like(feat_rows)
    low_row = low_half((1, 128))
    for j in range(heads):
        for d in range(depth):
            q, k = (wfeat_ref[j, side : side + 1, 128 * (d // 2) : 128 * (d // 2) + 128] for side in range(2))
            row = jnp.where(low_row, q, pltpu.roll(k, HD, 1)) if d % 2 == 0 else jnp.where(low_row, pltpu.roll(q, HD, 1), k)
            feat_rows[depth * j + d : depth * j + d + 1] = row
    feat_shard[...] = feat_rows[...].astype(BF16)
    fc_shard[...] = wfc_ref[...].astype(BF16)
    proj_shard[...] = wproj_ref[...].astype(BF16)
    norm_ref[...] = norm_in[...].astype(BF16).astype(F32)
    h = net.h
    rows, width = x_ref.shape
    chunks = rows // CHUNK
    seq = Rows(len_ref, rows, h)
    low = low_half((CHUNK, 128))
    mover = Mover(move_sem)
    push_normed, push_wo, push_maps, push_attn = (
        mover.plan(*pair)
        for pair in ((turned_ref, normed_out), (wo_ref, wo_out), (maps_ref, maps_out), (w_ref, attn_out))
    )
    push_qkv, push_fq, push_fk, push_state, push_mixed, push_rden = (
        mover.plan(*pair, groups)
        for pair in (
            (qkv_ref, qkv_out), (fq_ref, fq_out), (fk_ref, fk_out), (state_ref, state_out), (mixed_ref, mixed_out),
            (rden_ref, rden_out),
        )
    )
    push_middle, push_hidden = mover.plan(middle_ref, middle_out), mover.plan(hidden_ref, hidden_out)
    push_fc, push_proj = mover.plan(fc_ref, fc_out), mover.plan(proj_ref, proj_out)

    pl.semaphore_wait(pltpu.get_barrier_semaphore(), greeted)
    part = attn_shard.shape[0]
    cuts = [pl.ds(0, part // 2), pl.ds(part // 2, part // 2)] if part % 32 == 0 else [pl.ds(0, part)]
    feat = Gather(net, feat_shard, feat_ref, *sems[0:2])
    nets = net, Network(sizes, 1)
    fc, proj = Gather(nets[0], fc_shard, fc_ref, *sems[2:4]), Gather(nets[1], proj_shard, proj_ref, *sems[4:6])
    attns = [Gather(nets[i], attn_shard, w_ref, *sems[6 + 2 * i : 8 + 2 * i], rows) for i, rows in enumerate(cuts)]
    feat.begin()
    for attn in attns:
        attn.begin()

    def first_norm(c, _):
        at = pl.ds(pl.multiple_of(c * CHUNK, CHUNK), CHUNK)
        center, scale = norm_stats(x_ref[at].astype(F32))
        normed_ref[at] = (center * scale * norm_ref[0:1] + norm_ref[1:2]).astype(BF16)
        return 0

    for gather in (feat, *attns):
        gather.copy_own().wait()
    feat_on, feat_in = feat.steps()
    attn_rounds, attn_arrivals = zip(*(attn.steps() for attn in attns))
    attn_on = [sum(steps, []) for steps in zip(*attn_rounds)]
    attn_in = sum(attn_arrivals, [])
    lax.fori_loop(0, chunks, first_norm, 0)
    ahead = len(attn_on) - (1 if (X, groups) == (2, 4) else 0)
    for k in range(ahead):
        for step in feat_on[k] + attn_on[k]:
            step()
        if k == Z - 2:
            fc.begin()
        if k == len(feat_on) - 2:
            for step in feat_on[-1] + feat_in:
                step()
            maps_ref[...] = jnp.zeros_like(maps_ref)
            low64 = low_half((HD, 128))
            for i in range(X * Z):
                for g in range(groups):
                    block = feat_ref[i // Z, i % Z, g].astype(F32)
                    for j in range(heads):
                        pairs_ref[g * heads + j, depth * i : depth * i + depth] = block[depth * j : depth * j + depth]
            for g in range(groups):
                for j in range(heads):
                    pair = pairs_ref[g * heads + j]
                    swapped = pltpu.roll(pair, HD, 1)
                    at = slice(HD * j, HD * j + HD), slice(128 * j, 128 * j + 128)
                    maps_ref[0, g, at[0], at[1]] = jnp.where(low64, pair, -swapped).astype(BF16)
                    maps_ref[1, g, at[0], at[1]] = jnp.where(low64, swapped, -pair).astype(BF16)
            push_maps(0).start()

    turns = groups * chunks
    slots = {}
    if ahead < len(attn_on):
        slots[2] = list(attn_on[ahead])
        slots[2 * chunks] = list(attn_in)
    else:
        slots[0] = list(attn_in)
    fc_on, fc_in = fc.steps()
    proj_on, proj_in = proj.steps()
    slots.setdefault(PROJ_BEGIN, []).append(proj.begin)
    for on, turns_at in ((fc_on, FC_TURNS), (proj_on, PROJ_TURNS)):
        for k, steps in enumerate(on):
            slots.setdefault(turns_at[min(k, len(turns_at) - 1)], []).extend(steps)
    mix_slots = {k - turns: items for k, items in slots.items() if k >= turns}
    last = seq.last()

    def project(i, _):
        g = group_at(h, i, groups)
        for j in range(heads):
            total_ref[j] = jnp.zeros_like(total_ref[j])

        def part(c, _):
            run_at(slots, i * chunks + c, turns)
            at = pl.ds(pl.multiple_of(c * CHUNK, CHUNK), CHUNK)
            live, second = seq.live(c), seq.second_column(c)
            qkv = dot(normed_ref[at], w_ref[:, :, g].reshape(width, width)).astype(BF16)
            qkv_ref[g, at] = qkv
            scaled_q = dot(qkv[:, 0:256], maps_ref[0, g])
            scaled_k = dot(qkv[:, 256:512], maps_ref[1, g])
            for j in range(heads):
                lanes = slice(128 * j, 128 * j + 128)
                fq_ref[g, at, lanes] = feature_pair(scaled_q[:, lanes], live).astype(BF16)
                fk = feature_pair(scaled_k[:, lanes], live).astype(BF16)
                fk_ref[g, at, lanes] = fk
                block = qkv[:, 512 + 128 * (j // 2) : 640 + 128 * (j // 2)]
                values = by_sequence(with_ones(block, j, low), second)
                state_ref[g, j, c] = total_ref[j].astype(BF16)
                total_ref[j] += dot_tn(fk, values)
            return 0

        lax.fori_loop(0, chunks, part, 0)
        for push in (push_qkv, push_fq, push_fk):
            push(g).start()
        for j in range(heads):
            picked_ref[g, j] = total_ref[j, :, :128] * (1.0 - last) + total_ref[j, :, 128:] * last
        weight = w_ref[:, :, g].reshape(width, width)
        lowd = low_half((width, 128))
        a = swap_halves(weight[:, 128:256].astype(F32))
        b = weight[:, 384:512].astype(F32)
        c_ = swap_halves(weight[:, 640:768].astype(F32))
        wo_ref[g, :, 0:128] = jnp.where(lowd, a, b).astype(BF16)
        wo_ref[g, :, 128:256] = jnp.where(lowd, c_, 0.0).astype(BF16)
        return 0

    lax.fori_loop(0, groups, project, 0)
    push_wo(0).start()
    push_attn(0).start()

    before = seq.before()
    chain = Chain(1, groups, h, equal(before, last), picked_ref, cin, cout, chain_send, chain_recv)

    def mix(g, _):
        chain.step(g)

        def part(c, _):
            run_at(mix_slots, g * chunks + c, turns)
            at = pl.ds(pl.multiple_of(c * CHUNK, CHUNK), CHUNK)
            live, second = seq.live(c), seq.second_column(c)
            lower, _ = seq.masks(c)
            found = []
            for j in range(heads):
                lanes = slice(128 * j, 128 * j + 128)
                fq, fk = fq_ref[g, at, lanes], fk_ref[g, at, lanes]
                carry = cin[g, j].astype(F32)
                prior = jnp.concatenate([carry * (1.0 - before), carry * before], axis=1)
                state = (state_ref[g, j, c].astype(F32) + prior).astype(BF16)
                state_ref[g, j, c] = state
                scores = jnp.where(lower, dot_nt(fq, fk), 0.0).astype(BF16)
                block = qkv_ref[g, at, 512 + 128 * (j // 2) : 640 + 128 * (j // 2)]
                inter = dot(fq, state)
                found.append(
                    dot(scores, with_ones(block, j, low)) + jnp.where(second, inter[:, 128:], inter[:, :128])
                )
            pair = jnp.where(low, found[0], found[1])
            rden = 1.0 / (swap_halves(jnp.where(low, found[1], found[0])) + (1.0 - live))
            mixed_ref[g, at, 0:128] = (pair * rden).astype(BF16)
            rden_ref[g, at, 0:128] = rden.astype(BF16)
            rden = jnp.where(low, 1.0 / (swap_halves(found[2]) + (1.0 - live)), 1.0)
            mixed_ref[g, at, 128:256] = jnp.where(low, found[2] * rden, 0.0).astype(BF16)
            rden_ref[g, at, 128:256] = rden.astype(BF16)
            return 0

        lax.fori_loop(0, chunks, part, 0)
        for push in (push_state, push_mixed, push_rden):
            push(g).start()
        return 0

    lax.fori_loop(0, groups, mix, 0)
    rest_of(mix_slots, turns)

    def close(c, _):
        at = pl.ds(pl.multiple_of(c * CHUNK, CHUNK), CHUNK)
        attended = dot_nt(mixed_ref[0, at], wo_ref[0])
        for g in range(1, groups):
            attended = attended + dot_nt(mixed_ref[g, at], wo_ref[g])
        middle = x_ref[at].astype(F32) + attended
        middle_ref[at] = middle
        center, scale = norm_stats(middle)
        hidden_ref[at] = (center * scale * norm_ref[2:3] + norm_ref[3:4]).astype(BF16)
        return 0

    lax.fori_loop(0, chunks, close, 0)
    push_middle(0).start()
    push_hidden(0).start()
    def turn(c, _):
        at = pl.ds(pl.multiple_of(c * CHUNK, CHUNK), CHUNK)
        turned_ref[:, at] = normed_ref[at].T
        return 0

    lax.fori_loop(0, chunks, turn, 0)
    push_normed(0).start()
    for step in fc_in:
        step()
    fc.copy_own().wait()
    push_fc(0).start()
    for step in proj_in:
        step()
    proj.copy_own().wait()
    push_proj(0).start()
    chain.finish(groups)
    for gather in (*attns, feat, fc, proj):
        gather.finish()
    for push in (push_normed, push_wo, push_maps, push_attn, push_middle, push_hidden, push_fc, push_proj):
        push(0).wait()
    for push in (push_qkv, push_fq, push_fk, push_state, push_mixed, push_rden):
        for g in range(groups):
            push(g).wait()


def feed_forward(
    sizes, hidden_ref, dy_ref, norm_ref, fc_in, proj_in, middle_in,
    block_out, dmid_out, datt_out, dattt_out, gfc_sums, gproj_sums, gnorm_ref,
    fc_ref, proj_ref, middle_ref, out_ref, datt_ref, dattt_ref, gfc_ref, gproj_ref, branch_ref, dhid_ref, act_ref, dpre_ref,
    move_sem, fc_sem, proj_sem, *scratch,
):
    X, Z, H = sizes
    net = Network(sizes)
    chunks, size, width = fc_ref.shape
    part = gfc_ref.shape[3]
    rows = hidden_ref.shape[0]
    tile = 256
    tiles = rows // tile
    paired = (X, H) == (2, 4)

    if paired:
        far, near = (lax.rem(net.dp + 1, 2), net.dp), (flip_bit(net.h, 1), net.h)
        kinds = {"both": (far[0], near[0]), "x": (far[0], near[1]), "y": (far[1], near[0]), "own": (far[1], near[1])}
        plan = [[("both", off) for off in (3, 2, 1, 0)]]
        plan += [[(kind, off) for off in offs for kind in ("x", "y")] for offs in ((3, 2), (1, 0))]
        plan += [[("own", off) for off in (3, 2, 1, 0)]]
        places = []
        for items in plan:
            places.append([])
            for kind, off in items:
                dp, h = kinds[kind]
                places[-1] += [(dp, net.behind(off), h), (dp, net.behind(off), flip_bit(h, 0))]
    else:
        places = [
            [(lax.rem(net.dp + 1 + i, X), b, h) for b in range(Z) for h in range(H)] for i in range(X)
        ]

    def fetch(i, s):
        at = pl.ds(part * s, part)
        return (
            pltpu.make_async_copy(fc_in.at[places[i][s]], fc_ref.at[i, at], fc_sem.at[i, s]),
            pltpu.make_async_copy(proj_in.at[places[i][s]], proj_ref.at[i, at], proj_sem.at[i, s]),
        )

    for i in range(chunks):
        for s in range(size // part):
            for copy in fetch(i, s):
                copy.start()
    mover = Mover(move_sem)
    pull_middle = mover.plan(middle_in, middle_ref)
    pull_middle(0).start()
    net.barrier()
    scatters = [
        Scatter(net, Keep(gfc_sums), gfc_ref, *scratch[:3]),
        Scatter(Network(sizes, 1), Keep(gproj_sums), gproj_ref, *scratch[3:]),
    ]
    branch_ref[...] = jnp.zeros_like(branch_ref)
    dhid_ref[...] = jnp.zeros_like(dhid_ref)

    turns = chunks * tiles
    slots = {}
    if paired:
        own, first, second, both = scatters[0].early_sets()

        def add(slot, chosen, off):
            for scatter in scatters:
                slots.setdefault(slot, []).append(functools.partial(scatter.step, chosen, off))

        for k in range(Z):
            off = Z - 1 - k
            add(tiles + k // 2, both, off)
            add((2 + k // 2) * tiles, second, off)
            add((2 + k // 2) * tiles + 1, first, off)
            add(turns + k, own, off)
    else:
        for scatter in scatters:
            for chosen in reversed(scatter.early_sets()):
                for off in reversed(range(Z)):
                    slots.setdefault(turns, []).append(functools.partial(scatter.step, chosen, off))

    for i in range(chunks):
        for s in range(size // part):
            for copy in fetch(i, s):
                copy.wait()
        here = {k - i * tiles: items for k, items in slots.items() if i * tiles <= k < (i + 1) * tiles}

        def rowed(c, _, i=i, here=here):
            run_at(here, c, tiles)
            at = pl.ds(pl.multiple_of(c * tile, tile), tile)
            fc, proj = fc_ref[i], proj_ref[i]
            pre = dot_nt(hidden_ref[at], fc)
            square = pre * pre
            inner = jnp.tanh(0.7978845608 * pre * (1.0 + 0.044715 * square))
            half = 0.5 * (1.0 + inner)
            act = (pre * half).astype(BF16)
            slope = half + 0.5 * pre * (1.0 - inner * inner) * (0.7978845608 * (1.0 + 3 * 0.044715 * square))
            dpre = (dot_nt(dy_ref[at], proj) * slope).astype(BF16)
            act_ref[at] = act
            dpre_ref[at] = dpre
            branch_ref[at] += dot(act, proj)
            dhid_ref[at] += dot(dpre, fc)
            return 0

        lax.fori_loop(0, tiles, rowed, 0)
        pieces = ((scatters[1], gproj_ref, act_ref, dy_ref), (scatters[0], gfc_ref, dpre_ref, hidden_ref))
        for scatter, grads, left, right in pieces:
            half = size // 2
            for at in (0, half):
                grad = dot_tn(left[:, at : at + half], right[...]).astype(BF16)
                for s in range(half // part):
                    grads[places[i][at // part + s]] = grad[part * s : part * s + part]
            if not paired:
                scatter.begin(lambda dp_at, h_at, i=i: dp_at == places[i][0][0])
                continue
            for kind, off in plan[i]:
                if kind == "both" or kind == "own":
                    scatter.copy(both if kind == "both" else own, off, scatter.last).start()
                else:
                    chosen = (first, second) if kind == "y" else (second, first)
                    pl.when(scatter.net.odd == 0)(scatter.copy(chosen[0], off, scatter.last).start)
                    pl.when(scatter.net.odd == 1)(scatter.copy(chosen[1], off, scatter.last).start)

    gnorm_ref[...] = jnp.zeros_like(gnorm_ref)
    pull_middle(0).wait()
    late_slots = {min(k - turns, tiles - 1): [] for k in slots if k >= turns}
    for k in sorted(slots):
        if k >= turns:
            late_slots[min(k - turns, tiles - 1)] += slots[k]

    def close(c, _):
        at = pl.ds(pl.multiple_of(c * tile, tile), tile)
        middle = middle_ref[at]
        out_ref[at] = (middle + branch_ref[at]).astype(BF16)
        back, gain, shift = norm_backward(middle, norm_ref[2:3].astype(BF16).astype(F32), dhid_ref[at])
        dmid = dy_ref[at].astype(F32) + back
        middle_ref[at] = dmid
        datt_ref[at] = dmid.astype(BF16)
        dattt_ref[:, at] = dmid.astype(BF16).T
        gnorm_ref[2:3] += gain
        gnorm_ref[3:4] += shift
        run_at(late_slots, c, tiles)
        return 0

    lax.fori_loop(0, tiles, close, 0)
    outs = ((out_ref, block_out), (middle_ref, dmid_out), (datt_ref, datt_out), (dattt_ref, dattt_out))
    pushes = [mover.plan(*pair) for pair in outs]
    for push in pushes:
        push(0).start()
    for push in pushes:
        push(0).wait()
    for scatter in scatters:
        scatter.finish()


def attention_backward(
    sizes, heads, depth, len_ref, norm_ref, gnorm_in, gfc_sums, gproj_sums, x_in, normed_in, qkv_in, fq_in, fk_in,
    state_in, mixed_in, rden_in, wo_in, maps_in, w_in, datt_in, dattt_in, dmid_in,
    dx_out, gattn_out, gfeat_out, gfc_ref, gproj_ref, sums_out,
    x_ref, normed_ref, qkv_ref, fq_ref, fk_ref, state_ref, mixed_ref, rden_ref, wo_ref, maps_ref, datt_ref, dattt_ref, dmid_ref,
    w_ref, gw_ref, gnorm_ref, featsum_ref, featpart_ref,
    dne_ref, back_ref, total_ref, picked_ref, dnormed_ref, gsum_ref, cin, cout, chain_send, chain_recv,
    w_sem, move_sem, *scratch,
):
    X, Z, H = sizes
    groups = H
    net = Network(sizes)
    h = net.h
    rows, width = x_ref.shape
    chunks = rows // CHUNK
    part = w_ref.shape[3]
    seq = Rows(len_ref, rows, h)
    low = low_half((CHUNK, 128))

    mover = Mover(move_sem)
    pull_datt, pull_dattt, pull_maps, pull_normed, pull_x, pull_dmid, push_dx = (
        mover.plan(*pair)
        for pair in (
            (datt_in, datt_ref), (dattt_in, dattt_ref), (maps_in, maps_ref), (normed_in, normed_ref), (x_in, x_ref), (dmid_in, dmid_ref),
            (dmid_ref, dx_out),
        )
    )
    ahead_pulls = [
        mover.plan(*pair, groups)
        for pair in ((wo_in, wo_ref), (rden_in, rden_ref), (mixed_in, mixed_ref), (fq_in, fq_ref))
    ]
    group_pulls = [
        mover.plan(*pair, groups) for pair in ((fk_in, fk_ref), (state_in, state_ref), (qkv_in, qkv_ref))
    ]

    def pull_weight(i):
        slot = lax.rem(i, 2)
        return pltpu.make_async_copy(w_in.at[:, :, backwards(i)], w_ref.at[slot], w_sem.at[slot])

    def backwards(i):
        return group_at(h, groups - 1 - i, groups)

    pull_datt(0).start()
    for g in range(groups):
        for pull in ahead_pulls:
            pull(g).start()
    pull_dattt(0).start()
    pull_maps(0).start()
    for i in range(groups):
        for pull in group_pulls:
            pull(backwards(i)).start()
    pull_weight(0).start()
    pull_weight(1).start()
    pull_normed(0).start()
    pull_x(0).start()
    pull_dmid(0).start()
    net.barrier(whole_plane=True)
    fc_along, proj_along = Along(net, gfc_sums, *scratch[0:3]), Along(net, gproj_sums, *scratch[3:6])
    for off in reversed(range(1, Z)):
        fc_along.copy(off).start()
        proj_along.copy(off).start()
    attn_along, feat_along = Along(net, *scratch[6:10]), Along(net, *scratch[10:14])
    attn = Scatter(net, attn_along, gw_ref, *scratch[14:17])
    feat = Scatter(net, feat_along, featpart_ref, *scratch[17:20])
    odd = lax.rem(h, 2)

    down = lax.broadcasted_iota(jnp.int32, (256, 256), 0) // HD
    across = lax.broadcasted_iota(jnp.int32, (256, 256), 1) // HD
    other_half = ((down // 2 == across // 2) & (down != across)).astype(BF16)
    first = seq.first()
    pull_datt(0).wait()

    def ahead(g, _):
        for j in range(heads):
            total_ref[j] = jnp.zeros_like(total_ref[j])
        for pull in ahead_pulls:
            pull(g).wait()

        def piece(i, _):
            c = chunks - 1 - i
            at = pl.ds(pl.multiple_of(c * CHUNK, CHUNK), CHUNK)
            second = seq.second_column(c)
            dm = dot(datt_ref[at], wo_ref[g]).astype(BF16).astype(F32)
            rden = rden_ref[g, at].astype(F32)
            sums = dot((dm * mixed_ref[g, at].astype(F32)).astype(BF16), other_half)
            dnum = dm * rden
            dden = sums * swap_halves(rden) * (-1.0 / HD)
            for j in range(heads):
                lanes = slice(128 * (j // 2), 128 * (j // 2) + 128)
                mine, other = dnum[:, lanes], dden[:, lanes]
                dne = (jnp.where(low, mine, other) if j % 2 == 0 else jnp.where(low, other, mine)).astype(BF16)
                dne_ref[g, j, at] = dne
                back_ref[g, j, c] = total_ref[j].astype(BF16)
                total_ref[j] += dot_tn(fq_ref[g, at, 128 * j : 128 * j + 128], by_sequence(dne, second))
            return 0

        lax.fori_loop(0, chunks, piece, 0)
        for j in range(heads):
            picked_ref[g, j] = total_ref[j, :, :128] * (1.0 - first) + total_ref[j, :, 128:] * first
        return 0

    lax.fori_loop(0, groups, ahead, 0)
    after = seq.after()
    chain = Chain(-1, groups, h, equal(after, first), picked_ref, cin, cout, chain_send, chain_recv)
    lowd = low_half((width, 128))
    shape = (X, Z, part, 128)

    def out_grads(g, _):
        chain.step(g)
        beside = dot(dattt_ref[...], mixed_ref[g])
        for third, value in enumerate((swap_halves(beside[:, :128]), beside[:, :128], swap_halves(beside[:, 128:]))):
            gw_ref[:, :, g, :, 256 * third + 128 : 256 * third + 256] = value.astype(BF16).reshape(shape)
        return 0

    pull_dattt(0).wait()
    lax.fori_loop(0, groups, out_grads, 0)

    dnormed_ref[...] = jnp.zeros_like(dnormed_ref)
    pull_maps(0).wait()
    pull_normed(0).wait()

    def group(i, _):
        g = backwards(i)
        for pull in group_pulls:
            pull(g).wait()

        gsum_ref[...] = jnp.zeros_like(gsum_ref)

        def piece(c, _):
            at = pl.ds(pl.multiple_of(c * CHUNK, CHUNK), CHUNK)
            second = seq.second_column(c)
            lower, upper = seq.masks(c)
            dus_q, dus_k, dvs = [], [], []
            for j in range(heads):
                lanes = slice(128 * j, 128 * j + 128)
                fq, fk, dne = fq_ref[g, at, lanes], fk_ref[g, at, lanes], dne_ref[g, j, at]
                carry = cin[g, j].astype(F32)
                later = jnp.concatenate([carry * (1.0 - after), carry * after], axis=1)
                back = (back_ref[g, j, c].astype(F32) + later).astype(BF16)
                state = state_ref[g, j, c]
                block = qkv_ref[g, at, 512 + 128 * (j // 2) : 640 + 128 * (j // 2)]
                values = with_ones(block, j, low)
                scores_t = jnp.where(upper, dot_nt(fk, fq), 0.0).astype(BF16)
                weigh = jnp.where(lower, dot_nt(dne, values), 0.0).astype(BF16)
                weigh_t = jnp.where(upper, dot_nt(values, dne), 0.0).astype(BF16)
                dfq = dot(weigh, fk) + dot_nt(by_sequence(dne, second), state)
                dfk = dot(weigh_t, fq) + dot_nt(by_sequence(values, second), back)
                inter = dot(fk, back)
                dvs.append(dot(scores_t, dne) + jnp.where(second, inter[:, 128:], inter[:, :128]))
                dus_q.append(feature_back(fq.astype(F32), dfq.astype(BF16).astype(F32)).astype(BF16))
                dus_k.append(feature_back(fk.astype(F32), dfk.astype(BF16).astype(F32)).astype(BF16))
            du_q, du_k = jnp.concatenate(dus_q, axis=1), jnp.concatenate(dus_k, axis=1)
            dq = dot_nt(du_q, maps_ref[0, g]).astype(BF16)
            dk = dot_nt(du_k, maps_ref[1, g]).astype(BF16)
            dv = jnp.concatenate([jnp.where(low, dvs[0], dvs[1]), jnp.where(low, dvs[2], 0.0)], axis=1).astype(BF16)
            gsum_ref[0] += dot_tn(qkv_ref[g, at, 0:256], du_q)
            gsum_ref[1] += dot_tn(qkv_ref[g, at, 256:512], du_k)
            dqkv = jnp.concatenate([dq, dk, dv], axis=1)
            qkv_ref[g, at] = dqkv
            return 0

        lax.fori_loop(0, chunks, piece, 0)
        if (X, H) == (2, 4):

            @pl.when((i == groups - 1) & (odd == 1))
            def _():
                for off in reversed(range(Z)):
                    attn.step(attn.early_sets()[1], off)

        low64 = low_half((HD, 128))
        for j in range(heads):
            sums = [gsum_ref[side, HD * j : HD * j + HD, 128 * j : 128 * j + 128] for side in range(2)]
            sums = [value - pltpu.roll(value, HD, 1) for value in sums]
            pair = jnp.where(low64, sums[0], -sums[1])
            for k in range(X * Z):
                featsum_ref[k // Z, k % Z, g, depth * j : depth * j + depth] = pair[depth * k : depth * k + depth]
        for third in range(3):
            grad = dot(normed_ref[...], qkv_ref[g, :, 256 * third : 256 * third + 256])
            at = 256 * third
            gw_ref[:, :, g, :, at : at + 128] = grad[:, 0:128].astype(BF16).reshape(shape)
            beside = gw_ref[:, :, g, :, at + 128 : at + 256].reshape(width, 128)
            gw_ref[:, :, g, :, at + 128 : at + 256] = (
                jnp.where(lowd, grad[:, 128:256], beside.astype(F32)).astype(BF16).reshape(shape)
            )
        attn.begin(lambda dp_at, h_at: h_at == g)

        if (X, H) == (2, 4):

            @pl.when(i == groups - 2)
            def _():
                for off in reversed(range(Z)):
                    attn.step(attn.early_sets()[3], off)

                @pl.when(odd == 0)
                def _():
                    for off in reversed(range(Z)):
                        attn.step(attn.early_sets()[2], off)

        return 0

    featsum_ref[...] = jnp.zeros_like(featsum_ref)
    lax.fori_loop(0, groups, group, 0)
    for k in range(X * Z):
        for g in range(groups):
            featpart_ref[k // Z, k % Z, g] = featsum_ref[k // Z, k % Z, g].astype(BF16)
    feat.begin()

    gnorm_ref[...] = gnorm_in[...]
    turns = groups * chunks
    slots = {}
    for scatter in (attn, feat):
        own, *others = scatter.early_sets()
        for off in reversed(range(Z)):
            late = (Z - 1 - off) * turns // Z
            turn = {chosen: functools.partial(scatter.step, chosen, off) for chosen in (own, *others)}
            if scatter is attn and (X, H) == (2, 4):

                def cross(turn=turn):
                    pl.when(odd == 0)(turn[others[0]])
                    pl.when(odd == 1)(turn[others[1]])

                slots.setdefault(1 + late // 4, []).append(cross)
                slots.setdefault(4 + late * 3 // 4, []).append(turn[own])
            else:
                for k, chosen in enumerate(reversed(others)):
                    slots.setdefault(1 + 4 * k if len(others) == 3 else 1, []).append(turn[chosen])
                slots.setdefault(turns - 2, []).append(turn[own])

    def through(i, _):
        slot = lax.rem(i, 2)
        pull_weight(i).wait()

        def piece(c, _):
            run_at(slots, i * chunks + c, turns)
            at = pl.ds(pl.multiple_of(c * CHUNK, CHUNK), CHUNK)
            dnormed_ref[at] += dot_nt(qkv_ref[backwards(i), at], w_ref[slot].reshape(width, width))
            return 0

        lax.fori_loop(0, chunks, piece, 0)

        @pl.when(i < groups - 2)
        def _():
            pull_weight(i + 2).start()

        return 0

    lax.fori_loop(0, groups, through, 0)
    pull_x(0).wait()
    pull_dmid(0).wait()

    def close(c, _):
        at = pl.ds(pl.multiple_of(c * CHUNK, CHUNK), CHUNK)
        gain_row = norm_ref[0:1].astype(BF16).astype(F32)
        back, gain, shift = norm_backward(x_ref[at].astype(F32), gain_row, dnormed_ref[at])
        dmid_ref[at] = dmid_ref[at] + back
        gnorm_ref[0:1] += gain
        gnorm_ref[1:2] += shift
        return 0

    lax.fori_loop(0, chunks, close, 0)
    push_dx(0).start()
    square = jnp.zeros((1, 128), F32)
    gfc_ref[...] = fc_along.result()
    gproj_ref[...] = proj_along.result()
    gattn_out[...] = attn_along.result()
    gfeat_out[...] = feat_along.result()
    for ref in (gattn_out, gfeat_out, gfc_ref, gproj_ref):
        column = jnp.sum(ref[...] * ref[...], axis=0, keepdims=True)
        for at in range(0, column.shape[1], 128):
            square = square + column[:, at : at + 128]
    gnorm_ref[4:5, 0:128] = square
    sums_out[...] = total_over_all(net, gnorm_ref[...], *scratch[20:])
    push_dx(0).wait()
    chain.finish(groups)
    for moving in (attn, feat, fc_along, proj_along, attn_along, feat_along):
        moving.finish()


def adamw_update(master, first_mom, second_mom, grad_in, factor, step_rate, decay_rate):
    clipped = grad_in * factor
    first_new = beta_one * first_mom + (1.0 - beta_one) * clipped
    second_new = beta_two * second_mom + (1.0 - beta_two) * clipped * clipped
    direction = (
        first_new
        / (1.0 - beta_one**STEP)
        / (jnp.sqrt(second_new / (1.0 - beta_two**STEP)) + adam_eps)
    )
    master_new = master - step_rate * (direction + decay_rate * master)
    return (master_new, first_new, second_new)


def update_kernel(heads, depth, sums_ref, gattn_ref, gfeat_ref, gfc_ref, gproj_ref, *refs):
    masters, firsts, seconds = refs[0:6], refs[6:12], refs[12:18]
    block_in, dx_in, norm_out = refs[18:21]
    outs, (block_out, dx_out), (feat_grads, block_ref, dx_ref, sems) = refs[21:46], refs[46:48], refs[48:]
    mover = Mover(sems)
    pulls = [mover.plan(block_in, block_ref)(0), mover.plan(dx_in, dx_ref)(0)]
    pushes = [mover.plan(block_ref, block_out)(0), mover.plan(dx_ref, dx_out)(0)]
    for pull in pulls:
        pull.start()
    norm_grads = sums_ref[0:4]
    squares = jnp.sum(sums_ref[4:5, 0:128], keepdims=True) + jnp.sum(norm_grads * norm_grads, keepdims=True)
    grad_norm = jnp.sqrt(squares)
    norm_out[...] = jnp.broadcast_to(grad_norm, norm_out.shape)
    factor = clip_limit / jnp.maximum(grad_norm, clip_limit)
    rates, decays = (0.02, 0.4, 0.15, 0.02, 0.01, 0.3), (0.1, 0.1, 0.1, 0.1, 0.1, 0.0)

    def update(which, at, grads):
        results = adamw_update(
            masters[which][at], firsts[which][at], seconds[which][at], grads, factor, rates[which], decays[which]
        )
        results += (results[0].astype(BF16),)
        if which < 5:
            for kind, value in enumerate(results):
                outs[6 * kind + which][at] = value
        else:
            outs[5][...], outs[11][...] = results[0], results[1]
            outs[17][...], outs[23][...] = results[2][0:2], results[2][2:4]
            outs[24][...] = results[3]

    low = low_half((1, 128))
    for j in range(heads):
        for d in range(0, depth, 2):
            row, other = (gfeat_ref[depth * j + d + k : depth * j + d + k + 1] for k in range(2))
            at = slice(64 * d, 64 * d + 128)
            feat_grads[j, 0:1, at] = jnp.where(low, row, pltpu.roll(other, HD, 1))
            feat_grads[j, 1:2, at] = jnp.where(low, pltpu.roll(row, HD, 1), other)
    for j in range(3):
        update(0, (j,), gattn_ref[:, 256 * j : 256 * j + heads * HD])
        update(1, (slice(HD * j, HD * j + HD),), gattn_ref[:, 256 * j + heads * HD : 256 * j + 256].T)
    update(2, (slice(None),), feat_grads[...])
    update(3, (slice(None),), gfc_ref[...])
    for pull, push in zip(pulls, pushes):
        pull.wait()
        push.start()
    update(4, (slice(None),), gproj_ref[...])
    update(5, (slice(None),), norm_grads)
    for push in pushes:
        push.wait()


def in_vmem(count):
    return [pl.BlockSpec(memory_space=VMEM)] * count


def struct(shape, dtype):
    return jax.ShapeDtypeStruct(shape, dtype)


def call(kernel, outs, smem, operands, scratch, collective_id, name, flops, hbm_in=0, hbm_out=(), limit=63):
    specs = [pl.BlockSpec(memory_space=pltpu.SMEM)] * smem + in_vmem(len(operands) - smem - hbm_in)
    specs += [pl.BlockSpec(memory_space=pl.ANY)] * hbm_in
    out_specs = [pl.BlockSpec(memory_space=pl.ANY if i in hbm_out else VMEM) for i in range(len(outs))]
    traffic = sum(o.size * o.dtype.itemsize for o in outs) + sum(o.size * o.dtype.itemsize for o in operands)
    extra = {} if collective_id is None else {"collective_id": collective_id, "has_side_effects": True}
    return pl.pallas_call(
        kernel,
        out_shape=tuple(outs),
        in_specs=specs,
        out_specs=tuple(out_specs),
        scratch_shapes=scratch,
        compiler_params=pltpu.CompilerParams(vmem_limit_bytes=limit * 2**20, **extra),
        cost_estimate=pl.CostEstimate(flops=flops, bytes_accessed=traffic, transcendentals=0),
        name=name,
    )(*operands)


def on_device(
    sizes,
    block_in,
    cotangent,
    seq_len,
    w_qkv,
    w_out,
    w_feat,
    w_fc,
    w_proj,
    norm_params,
    first_qkv,
    second_qkv,
    first_out,
    second_out,
    first_feat,
    second_feat,
    first_fc,
    second_fc,
    first_proj,
    second_proj,
    first_norms,
    second_norms,
):
    X, Z, H = sizes
    rows, width = block_in.shape
    part, _, head_width = w_qkv.shape
    heads = w_feat.shape[1]
    depth = w_feat.shape[2] // HD
    chunks = rows // CHUNK

    big = (X, Z, H, part, width)
    small = (X, Z, H, FEAT_ROWS, 2 * HD)
    dma = pltpu.SemaphoreType.DMA
    chain_scratch = [
        VMEM((H, heads, 128, 128), F32),
        VMEM((H, heads, 128, 128), BF16),
        VMEM((H, heads, 128, 128), BF16),
        dma((H,)),
        dma((H,)),
    ]
    turned = struct((width, rows), BF16)
    held = [
        struct((rows, width), BF16),
        struct((H, rows, width), BF16),
        struct((H, rows, 128 * heads), BF16),
        struct((H, rows, 128 * heads), BF16),
        struct((H, heads, chunks, 128, 256), BF16),
        struct((H, rows, 256), BF16),
        struct((H, rows, 256), BF16),
        struct((H, width, 256), BF16),
        struct((2, H, 256, 128 * heads), BF16),
        struct((rows, width), F32),
        struct((rows, width), BF16),
    ]
    normed, qkv, fq, fk, states, mixed, rden, wo, maps, middle, hidden, attn_w, fc_w, proj_w = call(
        functools.partial(attention_forward, sizes, heads, depth),
        [turned] + held[1:] + [struct(big, BF16)] * 3,
        1,
        [seq_len, block_in, w_qkv.transpose(1, 0, 2), w_out, w_feat.transpose(1, 0, 2), w_fc.T, w_proj, norm_params],
        [VMEM(item.shape, item.dtype) for item in held]
        + [
            VMEM(turned.shape, BF16),
            VMEM((part, width), BF16),
            VMEM((FEAT_ROWS, 128), BF16),
            VMEM((part, width), BF16),
            VMEM((part, width), BF16),
            VMEM((FEAT_ROWS, 128), F32),
            VMEM((4, width), F32),
        ]
        + [VMEM(big, BF16), VMEM(big, BF16), VMEM(big, BF16), VMEM(small, BF16), VMEM((H * heads, HD, 128), F32), VMEM((heads, 128, 256), F32)]
        + chain_scratch
        + [dma((8 + 6 * H,))]
        + [sem for _ in range(5) for sem in gather_sems(sizes)],
        0,
        "attention_forward",
        10**10,
        hbm_out=range(14),
    )

    turns = 4 if (X, H) == (2, 4) else X
    size = X * Z * H * part // turns
    block_out, d_middle, d_att, d_att_t, fc_sums, proj_sums, g_norm = call(
        functools.partial(feed_forward, sizes),
        [
            struct((rows, width), BF16),
            struct((rows, width), F32),
            struct((rows, width), BF16),
            turned,
            struct((Z, part, width), BF16),
            struct((Z, part, width), BF16),
            struct((8, width), F32),
        ],
        0,
        [hidden, cotangent, norm_params, fc_w, proj_w, middle],
        [
            VMEM((turns, size, width), BF16),
            VMEM((turns, size, width), BF16),
            VMEM((rows, width), F32),
            VMEM((rows, width), BF16),
            VMEM((rows, width), BF16),
            VMEM(turned.shape, BF16),
            VMEM(big, BF16),
            VMEM(big, BF16),
            VMEM((rows, width), F32),
            VMEM((rows, width), F32),
            VMEM((rows, size), BF16),
            VMEM((rows, size), BF16),
            dma((5,)),
            dma((turns, size // part)),
            dma((turns, size // part)),
        ]
        + scatter_scratch(sizes, (part, width)) * 2,
        1,
        "feed_forward",
        3 * 10**10,
        hbm_in=3,
        hbm_out=range(4),
    )

    pulled = [struct((rows, width), BF16), turned] + held[1:9] + [struct((rows, width), BF16), turned, struct((rows, width), F32)]
    block_in_grad, g_attn, g_feat, g_fc, g_proj, sums = call(
        functools.partial(attention_backward, sizes, heads, depth),
        [
            struct((rows, width), F32),
            struct((part, width), F32),
            struct((FEAT_ROWS, 128), F32),
            struct((part, width), F32),
            struct((part, width), F32),
            struct((8, width), F32),
        ],
        1,
        [
            seq_len, norm_params, g_norm, fc_sums, proj_sums, block_in, normed, qkv, fq, fk, states, mixed, rden, wo, maps,
            attn_w, d_att, d_att_t, d_middle,
        ],
        [VMEM(item.shape, item.dtype) for item in pulled]
        + [
            VMEM((2, X, Z, part, width), BF16),
            VMEM(big, BF16),
            VMEM((8, width), F32),
            VMEM(small, F32),
            VMEM(small, BF16),
            VMEM((H, heads, rows, 128), BF16),
            VMEM((H, heads, chunks, 128, 256), BF16),
            VMEM((heads, 128, 256), F32),
            chain_scratch[0],
            VMEM((rows, width), F32),
            VMEM((2, 256, 128 * heads), F32),
        ]
        + chain_scratch[1:]
        + [dma((2,)), dma((7 + 7 * H,))]
        + along_scratch(sizes, (part, width)) * 2
        + [VMEM((Z, part, width), BF16)]
        + along_scratch(sizes, (part, width))
        + [VMEM((Z, FEAT_ROWS, 128), BF16)]
        + along_scratch(sizes, (FEAT_ROWS, 128))
        + scatter_scratch(sizes, (part, width))
        + scatter_scratch(sizes, (FEAT_ROWS, 128))
        + total_scratch(sizes, (8, width)),
        2,
        "attention_backward",
        2 * 10**10,
        hbm_in=14,
        hbm_out=(0,),
    )

    def turned(qkv, out, feat, fc, proj, *norms):
        return [qkv.transpose(1, 0, 2), out, feat.transpose(1, 0, 2), fc.T, proj, *norms]

    masters = turned(w_qkv, w_out, w_feat, w_fc, w_proj, norm_params)
    firsts = turned(first_qkv, first_out, first_feat, first_fc, first_proj, first_norms)
    seconds = turned(second_qkv, second_out, second_feat, second_fc, second_proj, second_norms)
    shapes = [item.shape for item in masters]
    halves = (2, width)
    norm_filled, *updated, block_out, block_in_grad = call(
        functools.partial(update_kernel, heads, depth),
        [struct((8, 128), F32)]
        + [struct(shape, F32) for shape in shapes * 2 + shapes[:5] + [halves]]
        + [struct(shape, BF16) for shape in shapes[:5]]
        + [struct(halves, F32), struct(shapes[5], BF16)]
        + [struct((rows, width), BF16), struct((rows, width), F32)],
        0,
        [sums, g_attn, g_feat, g_fc, g_proj] + masters + firsts + seconds + [block_out, block_in_grad],
        [VMEM(shapes[2], F32), VMEM((rows, width), BF16), VMEM((rows, width), F32), dma((4,))],
        None,
        "update",
        10**7,
        hbm_in=2,
        hbm_out=(26, 27),
    )
    new, new_first, new_second = (turned(*updated[6 * kind : 6 * kind + 6]) for kind in range(3))
    copies = turned(*updated[18:23], updated[24])
    return (
        norm_filled[0, 0],
        block_out,
        block_in_grad,
        *new,
        *new_first,
        *new_second[:5],
        new_second[5],
        updated[23],
        *copies,
    )


def solution(mesh):
    everything = ("dp", "batch", "head")
    rows = P(everything, None)
    qkv, out, feat = P(("dp", "batch"), None, "head"), P("head", ("dp", "batch")), P(None, "head", ("dp", "batch"))
    fc, proj, whole = P(None, everything), P(everything, None), P()
    weights = (qkv, out, feat, fc, proj, whole)
    in_specs = (rows, rows, P(("dp", "batch"), None)) + weights
    for spec in weights:
        in_specs += (spec, spec)
    out_specs = (whole, rows, rows) + weights + weights + weights[:5] + (whole, whole) + weights
    sizes = (mesh.shape["dp"], mesh.shape["batch"], mesh.shape["head"])
    return jax.shard_map(
        functools.partial(on_device, sizes), mesh=mesh, in_specs=in_specs, out_specs=out_specs, check_vma=False
    )
```
